32 devices in a mesh: req: 8 (over z, x), tp: 4 (over y, core).
Axes of the slice: x: 2, y: 2, z: 4, core: 2. Of those that a mesh axis runs over, the one named last changes fastest.
Arguments:
- hidden_in: bfloat16 [4096, 1024], P('req', 'tp'), may hold values from -6 to 6
- w_qkv: bfloat16 [1024, 3, 1024], P(None, None, 'tp'), may hold values from -0.1875 to 0.1875
- w_out: bfloat16 [1024, 1024], P('tp'), may hold values from -0.75 to 0.75
- first_gain: float32 [1024], replicated, may hold values from 0.1 to 1.9
- w_up: bfloat16 [1024, 4096], P(None, 'tp'), may hold values from -0.1875 to 0.1875
- w_down: bfloat16 [4096, 1024], P('tp'), may hold values from -0.09375 to 0.09375
- second_gain: float32 [1024], replicated, may hold values from 0.1 to 1.9
- cache_pool: bfloat16 [512, 128, 2, 1024], P('req', None, None, 'tp'), may hold values from -600 to 600
- page_table: int32 [64, 8], P('req'), may hold values from 0 to 63, as said below
- cache_len: int32 [64], P('req'), may hold values from 1 to 1024, as said below
- tree_parent: int32 [64, 64], P('req'), may hold values from -1 to 62, as said below
- accept_node: int32 [64], P('req'), may hold values from 0 to 63
Outputs:
- layer_out: bfloat16 [4096, 1024], P('req', 'tp')
- accepted_kv: bfloat16 [64, 64, 2, 1024], P('req', None, None, 'tp')
The draws below stay inside these ranges and needn't reach their ends.
Inputs may be any that keep to these rules, and one draw needn't show every extreme that they name: `page_table`: on each index e of req, the 8 x 8 entries of its rows are a permutation of the slots 0 to 63; row j, column m holds the slot in e's pool of page j of member m of the index e - j of req (modulo the axis size). `cache_len`: on each index of req exactly 2 requests have lengths over 256, and the others at most 256; the length 1024 occurs in every draw, and so does the length 256. `tree_parent`: node 0 is the root with parent -1; every other node's parent is an earlier node.
All inputs are finite; a program needn't handle non-finite values.
Results may differ from the reference program's by a relative error of at most 0.012.
Values may be sent and summed in bfloat16 or wider, within the bound.
No kernel may reach another device: no remote copies, remote signals or barrier semaphores. Data moves between devices by JAX's collectives and lax.ppermute only.
A program may use at most 128 MiB of HBM per device.

```python
import jax
import jax.numpy as jnp
from jax import lax

D = 1024
H = 16
HD = 64
FF = 4096
DRAFT = 64
PAGE = 128
MAXPG = 8
REQ_DEV = 8
LONG_DEV = 2
REQS = 64
TOKENS = 4096
POOL_DEV = 64
POOL = 512
PAGE_ROWS = 64
N_REQ = 8


def draw_cache_pool(key, part):
    shape = (POOL, PAGE, 2, H * HD)
    keys = jax.random.split(key, 1)
    base = jnp.clip(jax.random.normal(keys[0], shape, jnp.float32), -6.0, 6.0)
    return base.astype(jnp.bfloat16)


def draw_page_table(key, part):
    groups = PAGE_ROWS // MAXPG
    keys = jax.random.split(key, groups)
    perms = jax.vmap(lambda one_key: jax.random.permutation(one_key, POOL_DEV))(keys)
    return perms.reshape(PAGE_ROWS, REQ_DEV).astype(jnp.int32)


def draw_cache_len(key, part):
    keys = jax.random.split(key, 5)
    groups = REQS // REQ_DEV
    longest = MAXPG * PAGE
    group_keys = jax.random.split(keys[0], groups)
    ranks = jax.vmap(lambda one_key: jax.random.permutation(one_key, REQ_DEV))(group_keys)
    group_ids = jnp.broadcast_to(jnp.arange(groups, dtype=jnp.int32)[:, None], (groups, REQ_DEV))
    is_long = ranks < LONG_DEV
    short_len = jax.random.randint(keys[1], (groups, REQ_DEV), 1, 2 * PAGE + 1)
    long_len = jax.random.randint(keys[2], (groups, REQ_DEV), longest // 2 + 1, longest + 1)
    lengths = jnp.where(is_long, long_len, short_len)
    forced_long = jax.random.randint(keys[3], (), 0, groups)
    forced_short = jax.random.randint(keys[4], (), 0, groups)
    lengths = jnp.where((group_ids == forced_long) & (ranks == 0), longest, lengths)
    lengths = jnp.where((group_ids == forced_short) & (ranks == REQ_DEV - 1) & (ranks >= LONG_DEV), 2 * PAGE, lengths)
    return lengths.reshape(REQS).astype(jnp.int32)


def draw_tree_parent(key, part):
    index = jnp.arange(DRAFT, dtype=jnp.int32)[None, :]
    back = jax.random.randint(key, (REQS, DRAFT), 0, 3)
    parent = jnp.maximum(index - 1 - back, 0)
    parent = jnp.where(index == 0, -1, parent)
    return parent.astype(jnp.int32)


def plant(array, key, smallest, high):
    shape = array.shape
    index_at = [jax.random.randint(jax.random.fold_in(key, axis), (), 0, shape[axis]) for axis in range(len(shape))]
    array = array.at[tuple(index_at)].set(smallest)
    longest = shape.index(max(shape))
    index_at[longest] = (index_at[longest] + 1) % shape[longest]
    return array.at[tuple(index_at)].set(high)


def block_scale(own_key, dims, cuts, low, largest):
    def one(axis_at, blocks):
        heights = jax.random.uniform(jax.random.fold_in(jax.random.fold_in(own_key, 6), axis_at), (blocks,), jnp.float32, low / len(cuts), largest / len(cuts))
        return jnp.repeat(jnp.exp(heights), dims[axis_at] // blocks).reshape((-1,) + (1,) * (len(dims) - axis_at - 1))

    level = one(*cuts[0])
    for cut in cuts[1:]:
        level = level * one(*cut)
    return level


def normal_values(key, extent, deviation, most, cuts=(), kind=jnp.bfloat16):
    array = jax.random.normal(key, extent, jnp.float32) * deviation
    if len(cuts) > 0:
        array = block_scale(key, extent, cuts, -0.22, 0.18) * array
    return jnp.clip(array, min=-most, max=most).astype(kind)


def setup_inputs(seed: int = 0) -> dict:
    splits = jax.random.split(jax.random.key(seed), 13)
    return {
        "hidden_in": normal_values(splits[0], (TOKENS, D), 1.0, 6.0, ((0, 8), (1, 4))),
        "w_qkv": normal_values(splits[1], (D, 3, H * HD), D ** -0.5, 0.1875, ((2, 4),)),
        "w_out": normal_values(splits[2], (H * HD, D), (H * HD // 16) ** -0.5, 0.75, ((0, 4),)),
        "first_gain": jnp.clip(1.0 + 0.18 * jax.random.normal(splits[3], (D,), jnp.float32), 0.1, 1.9),
        "w_up": normal_values(splits[4], (D, FF), D ** -0.5, 0.1875, ((1, 4),)),
        "w_down": normal_values(splits[5], (FF, D), FF ** -0.5, 0.09375, ((0, 4),)),
        "second_gain": jnp.clip(1.0 + 0.18 * jax.random.normal(splits[6], (D,), jnp.float32), 0.1, 1.9),
        "cache_pool": draw_cache_pool(jax.random.fold_in(splits[12], 71), 0),
        "page_table": draw_page_table(jax.random.fold_in(splits[12], 71), 0),
        "cache_len": draw_cache_len(jax.random.fold_in(splits[12], 71), 0),
        "tree_parent": draw_tree_parent(jax.random.fold_in(splits[12], 71), 0),
        "accept_node": plant(jax.random.randint(splits[11], (REQS,), 0, DRAFT), jax.random.fold_in(splits[11], 1), 0, DRAFT - 1).astype(jnp.int32),
    }


NEG = -1e+30
EPS = 1e-05

def block_partial(queries, key_rows, value_rows, valid):
    scores = jnp.einsum('bqhd,bkhd->bhqk', queries.astype(jnp.float32), key_rows.astype(jnp.float32), precision=lax.Precision.HIGHEST)
    allowed = valid[:, None, :, :]
    maxima = lax.optimization_barrier(jnp.max(jnp.where(allowed, scores, NEG), axis=-1))
    weights = jnp.where(allowed, jnp.exp(scores - maxima[..., None]), 0.0).astype(jnp.bfloat16)
    totals = lax.optimization_barrier(jnp.sum(weights.astype(jnp.float32), axis=-1))
    mixture = jnp.einsum('bhqk,bkhd->bqhd', weights.astype(jnp.float32), value_rows.astype(jnp.float32), precision=lax.Precision.HIGHEST)
    return (mixture, maxima, totals)

def combine_blocks(mixture, maxima, totals):
    best = lax.optimization_barrier(jnp.max(maxima, axis=0))
    scale = jnp.swapaxes(jnp.exp(maxima - best[None]), -1, -2)
    numer = lax.optimization_barrier(jnp.sum(mixture * scale[..., None], axis=0))
    denom = lax.optimization_barrier(jnp.sum(jnp.swapaxes(totals, -1, -2) * scale, axis=0))
    return numer / denom[..., None]

def ancestors(parents):
    count = parents.shape[-1]
    reach = jax.nn.one_hot(parents, count, dtype=jnp.float32) + jnp.eye(count, dtype=jnp.float32)
    for sweep in range(max(1, (count - 1).bit_length())):
        reach = jnp.minimum(jnp.einsum('rij,rjk->rik', reach, reach, precision=lax.Precision.HIGHEST), 1.0)
    return reach

def layer_norm(values, gain):
    width_all = values.shape[-1]
    center = lax.optimization_barrier(jnp.sum(values, axis=-1, keepdims=True)) / width_all
    spread = lax.optimization_barrier(jnp.sum(values * values, axis=-1, keepdims=True)) / width_all - center * center
    return (values - center) * lax.rsqrt(spread + EPS) * gain

def reference(hidden_in, w_qkv, w_out, first_gain, w_up, w_down, second_gain, cache_pool, page_table, cache_len, tree_parent, accept_node):
    width_all = H * HD
    projected = jnp.dot(hidden_in, w_qkv.reshape(D, 3 * width_all), preferred_element_type=jnp.float32)
    queries = (projected[:, :width_all] * 0.125).astype(jnp.bfloat16).reshape(REQS, DRAFT, H, HD)
    key_new = projected[:, width_all:2 * width_all].astype(jnp.bfloat16).reshape(REQS, DRAFT, H, HD)
    value_new = projected[:, 2 * width_all:].astype(jnp.bfloat16).reshape(REQS, DRAFT, H, HD)
    reach = ancestors(tree_parent)
    offsets = jnp.arange(MAXPG, dtype=jnp.int32)
    positions = offsets[:, None] * PAGE + jnp.arange(PAGE, dtype=jnp.int32)[None, :]

    def one_request(request):
        owner = request // REQ_DEV
        member = request % REQ_DEV
        device_ids = (owner + offsets) % N_REQ
        slot_ids = page_table[device_ids * MAXPG + offsets, member]
        page_rows = cache_pool[device_ids * POOL_DEV + slot_ids]
        key_rows = page_rows[:, :, 0].reshape(MAXPG, PAGE, H, HD)
        value_rows = page_rows[:, :, 1].reshape(MAXPG, PAGE, H, HD)
        own_queries = queries[request]
        valid = jnp.broadcast_to((positions < cache_len[request])[:, None, :], (MAXPG, DRAFT, PAGE))
        page_parts = block_partial(jnp.broadcast_to(own_queries[None], (MAXPG, DRAFT, H, HD)), key_rows, value_rows, valid)
        tree_parts = block_partial(own_queries[None], key_new[request][None], value_new[request][None], (reach[request] > 0.5)[None])
        mixture = jnp.concatenate([tree_parts[0], page_parts[0]], axis=0)
        maxima = jnp.concatenate([tree_parts[1], page_parts[1]], axis=0)
        totals = jnp.concatenate([tree_parts[2], page_parts[2]], axis=0)
        return combine_blocks(mixture, maxima, totals)
    attended = lax.map(one_request, jnp.arange(REQS, dtype=jnp.int32))
    attended = attended.reshape(TOKENS, width_all).astype(jnp.bfloat16)
    branch = jnp.dot(attended, w_out, preferred_element_type=jnp.float32)
    normed = layer_norm(hidden_in.astype(jnp.float32) + branch, first_gain).astype(jnp.bfloat16)
    inner = jax.nn.gelu(jnp.dot(normed, w_up, preferred_element_type=jnp.float32), approximate=False).astype(jnp.bfloat16)
    outer = jnp.dot(inner, w_down, preferred_element_type=jnp.float32)
    layer_out = layer_norm(normed.astype(jnp.float32) + outer, second_gain).astype(jnp.bfloat16)
    pairs = jnp.stack([key_new.reshape(REQS, DRAFT, width_all), value_new.reshape(REQS, DRAFT, width_all)], axis=2)
    depth = lax.optimization_barrier(jnp.sum(reach, axis=-1)) - 1.0
    chosen = jnp.einsum('rq,rqk->rk', jax.nn.one_hot(accept_node, DRAFT, dtype=jnp.float32), reach, precision=lax.Precision.HIGHEST)
    levels = jnp.arange(DRAFT, dtype=jnp.float32)
    select = chosen[:, None, :] * (depth[:, None, :] == levels[None, :, None]).astype(jnp.float32)
    accepted_kv = jnp.einsum('rsk,rkcf->rscf', select, pairs.astype(jnp.float32), precision=lax.Precision.HIGHEST).astype(jnp.bfloat16)
    return (layer_out, accepted_kv)
```

```python
import functools

import jax
import jax.numpy as jnp
from jax import lax
from jax.experimental import pallas as pl
from jax.experimental.pallas import tpu as pltpu
from jax.sharding import PartitionSpec as P

HD = 64
NEG = -1e30
EPS = 1e-05
META = 16
F32 = jnp.float32
BF16 = jnp.bfloat16

VMEM = pl.BlockSpec(memory_space=pltpu.VMEM)
SMEM = pl.BlockSpec(memory_space=pltpu.SMEM)
ANY = pl.BlockSpec(memory_space=pl.ANY)


def shape_of(dims, dtype):
    return jax.ShapeDtypeStruct(dims, dtype)


def call(kernel, outs, ins, out_specs, scratch, operands, name, flops=0, nbytes=0, vmem=40):
    return pl.pallas_call(
        kernel,
        out_shape=outs,
        in_specs=ins,
        out_specs=out_specs,
        scratch_shapes=scratch,
        compiler_params=pltpu.CompilerParams(vmem_limit_bytes=vmem << 20),
        cost_estimate=pl.CostEstimate(flops=flops, bytes_accessed=nbytes, transcendentals=0),
        name=name,
    )(*operands)


def send_req(value, by):
    size = lax.axis_size("req")
    return lax.ppermute(value, "req", [(i, (i + by) % size) for i in range(size)])


def send_tp(value, flip):
    size = lax.axis_size("tp")
    return lax.ppermute(value, "tp", [(i, i ^ flip) for i in range(size)])


def write_order(len_ref, order_ref, requests, page_len):
    flags = [(len_ref[r] > 2 * page_len).astype(jnp.int32) for r in range(requests)]
    total = sum(flags)
    before = jnp.int32(0)
    for r in range(requests):
        place = jnp.where(flags[r] > 0, before, total + r - before)
        order_ref[place] = jnp.int32(r)
        before = before + flags[r]


def split3(value):
    high = value.astype(BF16)
    rest = value - high.astype(F32)
    middle = rest.astype(BF16)
    low = (rest - middle.astype(F32)).astype(BF16)
    return high, middle, low


def dot_t(a, b):
    return lax.dot_general(a, b, (((1,), (1,)), ((), ())), preferred_element_type=F32)


def head_rows(value, heads):
    lane = lax.broadcasted_iota(jnp.int32, value.shape, 1) // HD
    zero = jnp.zeros_like(value)
    return jnp.concatenate([jnp.where(lane == h, value, zero) for h in range(heads)], axis=0)


def head_lanes(stacked, heads, rows, width):
    lane = lax.broadcasted_iota(jnp.int32, (rows, width), 1) // HD
    out = jnp.zeros((rows, width), stacked.dtype)
    for h in range(heads):
        piece = stacked[h * rows : (h + 1) * rows]
        if piece.shape[1] != width:
            piece = jnp.broadcast_to(piece[:, :1], (rows, width))
        out = jnp.where(lane == h, piece, out)
    return out


def unpick(page_len):
    row = lax.broadcasted_iota(jnp.int32, (2 * page_len, 2 * page_len), 0)
    col = lax.broadcasted_iota(jnp.int32, (2 * page_len, 2 * page_len), 1)
    source = jnp.where(row < page_len, 2 * row, 2 * (row - page_len) + 1)
    return jnp.where(source == col, 1.0, 0.0).astype(BF16)


def split_page(page, picker, page_len):
    flat = page.reshape(2 * page_len, page.shape[2])
    both = jnp.dot(picker, flat, preferred_element_type=F32).astype(BF16)
    return both[:page_len], both[page_len:]


def to_row(column):
    return jnp.transpose(jnp.broadcast_to(column, (column.shape[0], 128)))[:1]


def attend(scores, masks, values):
    kept = [jnp.where(mask, score, NEG) for score, mask in zip(scores, masks)]
    top = functools.reduce(jnp.maximum, [jnp.max(s, axis=-1, keepdims=True) for s in kept])
    weights = [jnp.where(mask, jnp.exp(s - top), 0.0).astype(BF16) for s, mask in zip(kept, masks)]
    total = sum(jnp.sum(w.astype(F32), axis=-1, keepdims=True) for w in weights)
    mixed = sum(jnp.dot(w, v, preferred_element_type=F32) for w, v in zip(weights, values))
    return mixed, top, total


def pick_long_kernel(dims, len_ref, hidden_ref, out_ref, order_ref, sems):
    requests, draft, page_len, long_count = dims
    write_order(len_ref, order_ref, requests, page_len)
    copies = []
    for i in range(long_count):
        row = pl.multiple_of(order_ref[i] * draft, draft)
        copies.append(
            pltpu.make_async_copy(
                hidden_ref.at[pl.ds(row, draft)], out_ref.at[pl.ds(i * draft, draft)], sems.at[i]
            )
        )
    for copy in copies:
        copy.start()
    for copy in copies:
        copy.wait()


def pick_pages_kernel(dims, table_ref, pool_ref, out_ref, sems):
    requests, row = dims
    copies = [
        pltpu.make_async_copy(pool_ref.at[table_ref[row, m]], out_ref.at[m], sems.at[m])
        for m in range(requests)
    ]
    for copy in copies:
        copy.start()
    for copy in copies:
        copy.wait()


def long_query_kernel(dims, len_ref, own_ref, core_ref, y_ref, diag_ref, w_ref, out_ref, order_ref, wq_ref, sem):
    requests, page_len, long_count = dims
    copy = pltpu.make_async_copy(w_ref.at[0], wq_ref, sem)
    copy.start()
    me = lax.axis_index("tp")
    share = own_ref.shape[1]
    rows = own_ref.shape[0]
    width = wq_ref.shape[1]
    write_order(len_ref, order_ref, requests, page_len)
    row = lax.broadcasted_iota(jnp.int32, (META, width), 0)
    facts = jnp.zeros((META, width), jnp.int32)
    for i in range(long_count):
        member = order_ref[i]
        length = len_ref[member]
        facts = jnp.where(row == 3 * i, member, facts)
        facts = jnp.where(row == 3 * i + 1, length // page_len, facts)
        facts = jnp.where(row == 3 * i + 2, length % page_len, facts)
    out_ref[pl.ds(rows, META)] = facts.astype(F32).astype(BF16)
    copy.wait()
    total = jnp.zeros((rows, width), F32)
    for flip, ref in enumerate((own_ref, core_ref, y_ref, diag_ref)):
        at = pl.multiple_of((me ^ flip) * share, share)
        total += jnp.dot(ref[...], wq_ref[pl.ds(at, share), :], preferred_element_type=F32)
    out_ref[pl.ds(0, rows)] = (total * 0.125).astype(BF16)


def remote_kernel(dims, msg_ref, table_ref, pool_ref, out_ref, page_ref, sems):
    page_index, page_len, draft, heads, long_count = dims
    width = heads * HD
    tokens = long_count * draft
    facts = msg_ref[pl.ds(tokens, META), :].astype(F32)
    facts_row = lax.broadcasted_iota(jnp.int32, facts.shape, 0)

    def fact(k):
        return jnp.max(jnp.where(facts_row == k, facts, 0.0)).astype(jnp.int32)

    copies, limits = [], []
    for i in range(long_count):
        slot = table_ref[page_index, fact(3 * i)]
        copy = pltpu.make_async_copy(pool_ref.at[slot], page_ref.at[i], sems.at[i])
        copy.start()
        copies.append(copy)
        length = fact(3 * i + 1) * page_len + fact(3 * i + 2)
        limits.append(length - page_index * page_len)
    picker = unpick(page_len)
    lane = lax.broadcasted_iota(jnp.int32, (heads * draft, page_len), 1)
    stats = []
    for i in range(long_count):
        stacked = head_rows(msg_ref[pl.ds(i * draft, draft), :], heads)
        copies[i].wait()
        keys, values = split_page(page_ref[i], picker, page_len)
        mixed, top, total = attend([dot_t(stacked, keys)], [lane < limits[i]], [values])
        out_ref[pl.ds(i * draft, draft)] = head_lanes(mixed, heads, draft, width).astype(BF16)
        stats += list(split3(to_row(top))) + list(split3(to_row(total)))
    stats.append(jnp.zeros((META - len(stats), width), BF16))
    out_ref[pl.ds(tokens, META)] = jnp.concatenate([s.astype(F32) for s in stats], axis=0).astype(BF16)


def project_kernel(dims, accept_ref, own_ref, core_ref, y_ref, diag_ref, w_ref, parent_ref,
                   q_ref, k_ref, v_ref, reach_ref, acc_k_ref, acc_v_ref, wide_ref):
    requests, draft = dims
    me = lax.axis_index("tp")
    share = own_ref.shape[1]
    group = parent_ref.shape[1] // draft
    side = group * draft
    row = lax.broadcasted_iota(jnp.int32, (side, side), 0)
    col = lax.broadcasted_iota(jnp.int32, (side, side), 1)
    eye = jnp.where(row == col, 1.0, 0.0)
    up = []
    for g in range(requests // group):
        parent = parent_ref[pl.ds(g, 1), :]
        lane = lax.broadcasted_iota(jnp.int32, parent.shape, 1)
        target = jnp.where(parent < 0, -1, parent + (lane // draft) * draft)
        up.append((eye + jnp.where(row == target, 1.0, 0.0)).astype(BF16))
    for sweep in range(max(1, (draft - 1).bit_length())):
        up = [jnp.minimum(jnp.dot(u, u, preferred_element_type=F32), 1.0).astype(BF16) for u in up]
    for part, out in ((0, q_ref), (1, k_ref), (2, v_ref)):
        total = jnp.zeros(q_ref.shape, F32)
        for flip, ref in enumerate((own_ref, core_ref, y_ref, diag_ref)):
            at = pl.multiple_of((me ^ flip) * share, share)
            total += jnp.dot(ref[...], w_ref[part, pl.ds(at, share), :], preferred_element_type=F32)
        if part == 0:
            total = total * 0.125
        out[...] = total.astype(BF16)
    for g in range(requests // group):
        reach = jnp.transpose(up[g].astype(F32))
        wide_ref[...] = reach
        depth = jnp.sum(up[g].astype(F32), axis=0, keepdims=True) - 1.0
        chosen = jnp.zeros((1, side), F32)
        for i in range(group):
            r = g * group + i
            reach_ref[pl.ds(r * draft, draft), :] = reach[i * draft : (i + 1) * draft, i * draft : (i + 1) * draft]
            chosen += wide_ref[pl.ds(i * draft + accept_ref[r], 1), :]
        level = (row % draft).astype(F32)
        select = jnp.where((row // draft == col // draft) & (depth == level), chosen, 0.0).astype(BF16)
        rows = pl.ds(g * side, side)
        acc_k_ref[rows] = jnp.dot(select, k_ref[rows], preferred_element_type=F32).astype(BF16)
        acc_v_ref[rows] = jnp.dot(select, v_ref[rows], preferred_element_type=F32).astype(BF16)


def local_kernel(dims, len_ref, table_ref, q_ref, k_ref, v_ref, reach_ref, near_ref, pool_ref,
                 rest_ref, long_ref, stats_ref, order_ref, first_ref, second_ref, sems):
    requests, draft, heads, page_len, long_count = dims
    width = heads * HD
    write_order(len_ref, order_ref, requests, page_len)
    copies = []
    for p in range(requests):
        r = order_ref[p]
        one = pltpu.make_async_copy(pool_ref.at[table_ref[0, r]], first_ref.at[p], sems.at[p, 0])
        two = pltpu.make_async_copy(near_ref.at[r], second_ref.at[p], sems.at[p, 1])
        one.start()
        two.start()
        copies.append((one, two))
    picker = unpick(page_len)
    lane = lax.broadcasted_iota(jnp.int32, (heads * draft, page_len), 1)
    stats = []
    for p in range(requests):
        r = order_ref[p]
        rows = pl.ds(pl.multiple_of(r * draft, draft), draft)
        length = len_ref[r]
        stacked = head_rows(q_ref[rows, :], heads)
        tree_ok = jnp.concatenate([reach_ref[rows, :]] * heads, axis=0) > 0.5
        for copy in copies[p]:
            copy.wait()
        key_0, value_0 = split_page(first_ref[p], picker, page_len)
        key_1, value_1 = split_page(second_ref[p], picker, page_len)
        mixed, top, total = attend(
            [dot_t(stacked, k_ref[rows, :]), dot_t(stacked, key_0), dot_t(stacked, key_1)],
            [tree_ok, lane < length, lane < length - page_len],
            [v_ref[rows, :], value_0, value_1],
        )
        if p < long_count:
            long_ref[pl.ds(p * draft, draft)] = head_lanes(mixed, heads, draft, width)
            stats += [to_row(top), to_row(total)]
        else:
            whole = head_lanes(mixed, heads, draft, width) / head_lanes(total, heads, draft, width)
            rest_ref[pl.ds((p - long_count) * draft, draft)] = whole.astype(BF16)
    stats.append(jnp.zeros((META - len(stats), width), F32))
    stats_ref[...] = jnp.concatenate(stats, axis=0)


def merge_kernel(dims, count, own_ref, stats_ref, *refs):
    draft, heads, long_count = dims
    width = heads * HD
    msgs, out_ref = refs[:count], refs[count]
    tokens = long_count * draft
    own = stats_ref[...]
    facts = [ref[pl.ds(tokens, META), :].astype(F32) for ref in msgs]
    for i in range(long_count):
        tops = [own[2 * i : 2 * i + 1]]
        totals = [own[2 * i + 1 : 2 * i + 2]]
        for f in facts:
            b = 6 * i
            tops.append(f[b : b + 1] + f[b + 1 : b + 2] + f[b + 2 : b + 3])
            totals.append(f[b + 3 : b + 4] + f[b + 4 : b + 5] + f[b + 5 : b + 6])
        best = functools.reduce(jnp.maximum, tops)
        scales = [jnp.exp(t - best) for t in tops]
        denom = sum(s * t for s, t in zip(scales, totals))
        factors = jnp.concatenate([s / denom for s in scales] + [jnp.zeros((128 - len(scales), width), F32)], axis=0)
        factors = jnp.transpose(factors)
        rows = pl.ds(i * draft, draft)
        out = own_ref[rows, :] * head_lanes(factors[:, :1], heads, draft, width)
        for j, ref in enumerate(msgs):
            out += ref[rows, :].astype(F32) * head_lanes(factors[:, j + 1 : j + 2], heads, draft, width)
        out_ref[rows] = out.astype(BF16)


def norm(values, sums, squares, gain, width_all):
    center = sums / width_all
    spread = squares / width_all - center * center
    return (values - center) * lax.rsqrt(spread + EPS) * gain


def forward_kernel(dims, len_ref, *refs):
    requests, draft, page_len, first, count = dims
    att, hid, wout = refs[0:4], refs[4:8], refs[8:12]
    gain_ref, up_ref, down_ref = refs[12:15]
    parts, normed_ref = refs[15:19], refs[19]
    order_ref, z_ref, up_v, down_v, sems = refs[20:]
    copies = [
        pltpu.make_async_copy(up_ref, up_v, sems.at[0]),
        pltpu.make_async_copy(down_ref, down_v, sems.at[1]),
    ]
    for copy in copies:
        copy.start()
    me = lax.axis_index("tp")
    share = hid[0].shape[1]
    width_all = z_ref.shape[1]
    write_order(len_ref, order_ref, requests, page_len)
    for p in range(count):
        rows = pl.ds(pl.multiple_of(order_ref[first + p] * draft, draft), draft)
        for flip in range(4):
            at = pl.ds(pl.multiple_of((me ^ flip) * share, share), share)
            z_ref[pl.ds(p * draft, draft), at] = hid[flip][rows, :].astype(F32)
    branch = sum(jnp.dot(a[...], w[...], preferred_element_type=F32) for a, w in zip(att, wout))
    z = z_ref[...] + branch
    sums = jnp.sum(z, axis=-1, keepdims=True)
    squares = jnp.sum(z * z, axis=-1, keepdims=True)
    normed_wide = norm(z, sums, squares, gain_ref[...], width_all)
    normed = normed_wide.astype(BF16)
    z_ref[...] = normed_wide
    normed_ref[...] = z_ref[:, pl.ds(pl.multiple_of(me * share, share), share)].astype(BF16)
    copies[0].wait()
    inner = jnp.dot(normed, up_v[...], preferred_element_type=F32)
    inner = (0.5 * inner * (1.0 + lax.erf(inner * (0.5 ** 0.5)))).astype(BF16)
    copies[1].wait()
    for flip in range(4):
        at = pl.ds(pl.multiple_of((me ^ flip) * share, share), share)
        parts[flip][...] = jnp.dot(inner, down_v[:, at], preferred_element_type=F32).astype(BF16)


def gather_sum_kernel(a_ref, b_ref, c_ref, d_ref, normed_ref, x_ref, stats_ref):
    x = normed_ref[...].astype(F32) + (
        (a_ref[...].astype(F32) + b_ref[...].astype(F32)) + (c_ref[...].astype(F32) + d_ref[...].astype(F32))
    )
    x_ref[...] = x
    row = lax.broadcasted_iota(jnp.int32, stats_ref.shape, 0)
    sums = to_row(jnp.sum(x, axis=-1, keepdims=True))
    squares = to_row(jnp.sum(x * x, axis=-1, keepdims=True))
    stats_ref[...] = jnp.where(row == 0, sums, jnp.where(row == 1, squares, 0.0))


def finish_kernel(dims, len_ref, gain_ref, *refs):
    requests, draft, page_len, counts = dims
    order_ref = refs[-1]
    out_ref = refs[-2]
    me = lax.axis_index("tp")
    write_order(len_ref, order_ref, requests, page_len)
    share = out_ref.shape[1]
    gain = gain_ref[:, pl.ds(pl.multiple_of(me * share, share), share)]
    width_all = gain_ref.shape[1]
    place = 0
    for g, count in enumerate(counts):
        x_ref = refs[5 * g]
        stats = sum(ref[...] for ref in refs[5 * g + 1 : 5 * g + 5])
        stats = jnp.transpose(jnp.concatenate([stats] * (128 // stats.shape[0]), axis=0))
        y = norm(x_ref[...], stats[:, 0:1], stats[:, 1:2], gain, width_all).astype(BF16)
        for p in range(count):
            rows = pl.ds(pl.multiple_of(order_ref[place] * draft, draft), draft)
            out_ref[rows, :] = y[p * draft : (p + 1) * draft]
            place += 1


def shards(hidden_in, w_qkv, w_out, first_gain, w_up, w_down, second_gain, cache_pool,
           page_table, cache_len, tree_parent, accept_node):
    tokens, share = hidden_in.shape
    requests, draft = tree_parent.shape
    width = w_qkv.shape[2]
    heads = width // HD
    pages = page_table.shape[0]
    page_len = cache_pool.shape[1]
    width_all = w_qkv.shape[0]
    long_count = (requests + 3) // 4
    long_rows = long_count * draft
    msg_rows = long_rows + META
    side = 4 * draft
    dma = pltpu.SemaphoreType.DMA
    order = pltpu.SMEM((requests,), jnp.int32)

    w_planes = jnp.transpose(w_qkv, (1, 0, 2))
    gain_1 = first_gain.reshape(1, -1)
    gain_2 = second_gain.reshape(1, -1)
    parents = tree_parent.reshape(requests * draft // side, side)

    hidden_long = call(
        functools.partial(pick_long_kernel, (requests, draft, page_len, long_count)),
        shape_of((long_rows, share), BF16), [SMEM, ANY], VMEM, [order, dma((long_count,))],
        (cache_len, hidden_in), "pick_long",
    )
    long_core = send_tp(hidden_long, 1)
    long_y = send_tp(hidden_long, 2)
    long_diag = send_tp(long_y, 1)

    near = call(
        functools.partial(pick_pages_kernel, (requests, 1)),
        shape_of((requests,) + cache_pool.shape[1:], BF16), [SMEM, ANY], ANY, [dma((requests,))],
        (page_table, cache_pool), "pick_pages",
    )
    near = send_req(near, -1)

    message = call(
        functools.partial(long_query_kernel, (requests, page_len, long_count)),
        shape_of((msg_rows, width), BF16), [SMEM, VMEM, VMEM, VMEM, VMEM, ANY], VMEM,
        [order, pltpu.VMEM((width_all, width), BF16), dma(())],
        (cache_len, hidden_long, long_core, long_y, long_diag, w_planes), "long_queries",
        flops=2 * long_rows * width_all * width, nbytes=2 * width_all * width,
    )
    queue = sorted(range(2, pages), key=lambda j: (abs(2 * j - pages), j))
    asked = {j: send_req(message, j) for j in queue}

    hid_core = send_tp(hidden_in, 1)
    hid_y = send_tp(hidden_in, 2)
    hid_diag = send_tp(hid_y, 1)
    hid = (hidden_in, hid_core, hid_y, hid_diag)
    wout_core = send_tp(w_out, 1)
    wout_y = send_tp(w_out, 2)
    wout_diag = send_tp(wout_y, 1)
    wout = (w_out, wout_core, wout_y, wout_diag)

    block = shape_of((tokens, width), BF16)
    queries, key_new, value_new, reach, acc_k, acc_v = call(
        functools.partial(project_kernel, (requests, draft)),
        [block, block, block, shape_of((tokens, draft), F32), block, block],
        [SMEM] + [VMEM] * 6, [VMEM] * 6, [pltpu.VMEM((side, side), F32)],
        (accept_node, *hid, w_planes, parents), "project",
        flops=2 * tokens * width_all * width * 3, nbytes=2 * width_all * width * 3,
    )

    answers = []
    for j in queue:
        answer = call(
            functools.partial(remote_kernel, (j, page_len, draft, heads, long_count)),
            shape_of((msg_rows, width), BF16), [VMEM, SMEM, ANY], VMEM,
            [pltpu.VMEM((long_count,) + cache_pool.shape[1:], BF16), dma((long_count,))],
            (asked[j], page_table, cache_pool), "remote_%d" % j,
            flops=long_count * 6 * 256 ** 3, nbytes=long_count * 131072,
        )
        answers.append(send_req(answer, -j))

    rest, long_own, long_stats = call(
        functools.partial(local_kernel, (requests, draft, heads, page_len, long_count)),
        [shape_of((tokens - long_rows, width), BF16), shape_of((long_rows, width), F32), shape_of((META, width), F32)],
        [SMEM, SMEM, VMEM, VMEM, VMEM, VMEM, ANY, ANY], [VMEM] * 3,
        [order, pltpu.VMEM((requests,) + cache_pool.shape[1:], BF16),
         pltpu.VMEM((requests,) + cache_pool.shape[1:], BF16), dma((requests, 2))],
        (cache_len, page_table, queries, key_new, value_new, reach, near, cache_pool), "local_attention",
        flops=requests * 14 * 256 ** 3, nbytes=requests * 2 * 131072,
    )

    def forward(attended, first, count, name):
        rows = count * draft
        att_core = send_tp(attended, 1)
        att_y = send_tp(attended, 2)
        att_diag = send_tp(att_y, 1)
        part = shape_of((rows, share), BF16)
        outs = call(
            functools.partial(forward_kernel, (requests, draft, page_len, first, count)),
            [part] * 5, [SMEM] + [VMEM] * 13 + [ANY, ANY], [VMEM] * 5,
            [order, pltpu.VMEM((rows, width_all), F32), pltpu.VMEM(w_up.shape, BF16),
             pltpu.VMEM(w_down.shape, BF16), dma((2,))],
            (cache_len, attended, att_core, att_y, att_diag, *hid, *wout, gain_1, w_up, w_down), name,
            flops=2 * rows * width_all * (width_all + 2 * w_up.shape[1]), nbytes=3 * 2 * 1024 * 1024,
        )
        got = [send_tp(outs[flip], flip) for flip in (2, 3, 1)]
        x, stats = call(
            gather_sum_kernel,
            [shape_of((rows, share), F32), shape_of((8, rows), F32)], [VMEM] * 5, [VMEM] * 2, [],
            (outs[0], *got, outs[4]), name + "_sum",
        )
        return (x, stats) + tuple(send_tp(stats, flip) for flip in (2, 3, 1))

    tail_rest = forward(rest, long_count, requests - long_count, "forward_short")

    merged = call(
        functools.partial(merge_kernel, (draft, heads, long_count), len(answers)),
        shape_of((long_rows, width), BF16), [VMEM] * (2 + len(answers)), VMEM, [],
        (long_own, long_stats, *answers), "merge",
    )
    tail_long = forward(merged, 0, long_count, "forward_long")

    layer_out = call(
        functools.partial(finish_kernel, (requests, draft, page_len, (long_count, requests - long_count))),
        shape_of((tokens, share), BF16), [SMEM] + [VMEM] * 11, VMEM, [order],
        (cache_len, gain_2, *tail_long, *tail_rest), "finish",
    )
    accepted_kv = jnp.stack(
        [acc_k.reshape(requests, draft, width), acc_v.reshape(requests, draft, width)], axis=2
    )
    return (layer_out, accepted_kv)


def solution(mesh):
    placed = (
        P("req", "tp"),
        P(None, None, "tp"),
        P("tp", None),
        P(),
        P(None, "tp"),
        P("tp", None),
        P(),
        P("req", None, None, "tp"),
        P("req", None),
        P("req"),
        P("req", None),
        P("req"),
    )
    return jax.shard_map(
        shards,
        mesh=mesh,
        in_specs=placed,
        out_specs=(P("req", "tp"), P("req", None, None, "tp")),
        check_vma=False,
    )
```

```python
import functools

import jax
import jax.numpy as jnp
from jax import lax
from jax.experimental import pallas as pl
from jax.experimental.pallas import tpu as pltpu
from jax.sharding import PartitionSpec as P

HD = 64
NEG = -1e30
EPS = 1e-05
META = 16
F32 = jnp.float32
BF16 = jnp.bfloat16

VMEM = pl.BlockSpec(memory_space=pltpu.VMEM)
SMEM = pl.BlockSpec(memory_space=pltpu.SMEM)
ANY = pl.BlockSpec(memory_space=pl.ANY)
HBM = pl.BlockSpec(memory_space=pltpu.HBM)


def shape_of(dims, dtype):
    return jax.ShapeDtypeStruct(dims, dtype)


def call(kernel, outs, ins, out_specs, scratch, operands, name, flops=0, nbytes=0, after=()):
    split = len(operands)

    def body(*refs):
        kernel(*refs[:split], *refs[split + len(after) :])

    return pl.pallas_call(
        body,
        out_shape=outs,
        in_specs=list(ins) + [ANY] * len(after),
        out_specs=out_specs,
        scratch_shapes=scratch,
        compiler_params=pltpu.CompilerParams(vmem_limit_bytes=24 << 20),
        cost_estimate=pl.CostEstimate(flops=flops, bytes_accessed=nbytes, transcendentals=0),
        name=name,
    )(*operands, *after)


def send_req(value, by):
    size = lax.axis_size("req")
    return lax.ppermute(value, "req", [(i, (i + by) % size) for i in range(size)])


def send_tp(value, flip):
    size = lax.axis_size("tp")
    return lax.ppermute(value, "tp", [(i, i ^ flip) for i in range(size)])


def write_order(len_ref, order_ref, requests, page_len):
    flags = [(len_ref[r] > 2 * page_len).astype(jnp.int32) for r in range(requests)]
    total = sum(flags)
    before = jnp.int32(0)
    for r in range(requests):
        place = jnp.where(flags[r] > 0, before, total + r - before)
        order_ref[place] = jnp.int32(r)
        before = before + flags[r]


def split3(value):
    high = value.astype(BF16)
    rest = value - high.astype(F32)
    middle = rest.astype(BF16)
    low = (rest - middle.astype(F32)).astype(BF16)
    return high, middle, low


def dot_t(a, b):
    return lax.dot_general(a, b, (((1,), (1,)), ((), ())), preferred_element_type=F32)


def head_rows(value, heads):
    lane = lax.broadcasted_iota(jnp.int32, value.shape, 1) // HD
    zero = jnp.zeros_like(value)
    return jnp.concatenate([jnp.where(lane == h, value, zero) for h in range(heads)], axis=0)


def head_lanes(stacked, heads, rows, width):
    lane = lax.broadcasted_iota(jnp.int32, (rows, width), 1) // HD
    out = jnp.zeros((rows, width), stacked.dtype)
    for h in range(heads):
        piece = stacked[h * rows : (h + 1) * rows]
        if piece.shape[1] != width:
            piece = jnp.broadcast_to(piece[:, :1], (rows, width))
        out = jnp.where(lane == h, piece, out)
    return out


def unpick(page_len):
    row = lax.broadcasted_iota(jnp.int32, (2 * page_len, 2 * page_len), 0)
    col = lax.broadcasted_iota(jnp.int32, (2 * page_len, 2 * page_len), 1)
    source = jnp.where(row < page_len, 2 * row, 2 * (row - page_len) + 1)
    return jnp.where(source == col, 1.0, 0.0).astype(BF16)


def split_page(page, picker, page_len):
    flat = page.reshape(2 * page_len, page.shape[2])
    both = jnp.dot(picker, flat, preferred_element_type=F32).astype(BF16)
    return both[:page_len], both[page_len:]


def to_row(column):
    return jnp.transpose(jnp.broadcast_to(column, (column.shape[0], 128)))[:1]


def attend(scores, values):
    top = functools.reduce(jnp.maximum, [jnp.max(s, axis=-1, keepdims=True) for s in scores])
    weights = [jnp.exp(s - top).astype(BF16) for s in scores]
    total = sum(jnp.sum(w.astype(F32), axis=-1, keepdims=True) for w in weights)
    mixed = sum(jnp.dot(w, v, preferred_element_type=F32) for w, v in zip(weights, values))
    return mixed, top, total


def pick_pages_kernel(dims, table_ref, pool_ref, out_ref, sems):
    requests, row = dims
    copies = [
        pltpu.make_async_copy(pool_ref.at[table_ref[row, m]], out_ref.at[m], sems.at[m])
        for m in range(requests)
    ]
    for copy in copies:
        copy.start()
    for copy in copies:
        copy.wait()


def full_product(hid, w_ref, part):
    me = lax.axis_index("tp")
    share = hid[0].shape[1]
    total = None
    for flip, ref in enumerate(hid):
        at = pl.multiple_of((me ^ flip) * share, share)
        term = jnp.dot(ref[...], w_ref[part, pl.ds(at, share), :], preferred_element_type=F32)
        total = term if total is None else total + term
    return total


def tree_kernel(dims, accept_ref, parent_ref, bias_ref, select_ref, wide_ref):
    requests, draft = dims
    group = parent_ref.shape[1] // draft
    side = group * draft
    row = lax.broadcasted_iota(jnp.int32, (side, side), 0)
    col = lax.broadcasted_iota(jnp.int32, (side, side), 1)
    eye = jnp.where(row == col, 1.0, 0.0)
    up = []
    for g in range(requests // group):
        parent = parent_ref[pl.ds(g, 1), :]
        lane = lax.broadcasted_iota(jnp.int32, parent.shape, 1)
        target = jnp.where(parent < 0, -1, parent + (lane // draft) * draft)
        up.append((eye + jnp.where(row == target, 1.0, 0.0)).astype(BF16))
    for sweep in range(max(1, (draft - 1).bit_length())):
        up = [jnp.minimum(jnp.dot(u, u, preferred_element_type=F32), 1.0).astype(BF16) for u in up]
    row = lax.broadcasted_iota(jnp.int32, (2 * side, 2 * side), 0)
    col = lax.broadcasted_iota(jnp.int32, (2 * side, 2 * side), 1)
    fits = (row % 2 == col // side) & (row // (2 * draft) == (col % side) // draft)
    level = ((row // 2) % draft).astype(F32)
    for g in range(requests // group):
        wide = up[g].astype(F32)
        reach = jnp.transpose(wide)
        wide_ref[...] = reach
        depth = jnp.sum(wide, axis=0, keepdims=True) - 1.0
        chosen = jnp.zeros((1, side), F32)
        for i in range(group):
            r = g * group + i
            own = reach[i * draft : (i + 1) * draft, i * draft : (i + 1) * draft]
            bias_ref[pl.ds(r * draft, draft), :] = jnp.where(own > 0.5, 0.0, NEG)
            chosen += wide_ref[pl.ds(i * draft + accept_ref[r], 1), :]
        depth = jnp.concatenate([depth, depth], axis=1)
        chosen = jnp.concatenate([chosen, chosen], axis=1)
        select_ref[g] = jnp.where(fits & (depth == level), chosen, 0.0).astype(BF16)


def query_kernel(dims, len_ref, own_ref, core_ref, y_ref, diag_ref, w_ref, q_ref, out_ref, order_ref):
    requests, draft, page_len, long_count = dims
    rows = long_count * draft
    width = q_ref.shape[1]
    write_order(len_ref, order_ref, requests, page_len)
    row = lax.broadcasted_iota(jnp.int32, (META, width), 0)
    facts = jnp.zeros((META, width), jnp.int32)
    for i in range(long_count):
        member = order_ref[i]
        length = len_ref[member]
        facts = jnp.where(row == 3 * i, member, facts)
        facts = jnp.where(row == 3 * i + 1, length // page_len, facts)
        facts = jnp.where(row == 3 * i + 2, length % page_len, facts)
    out_ref[pl.ds(rows, META)] = facts.astype(F32).astype(BF16)
    q_ref[...] = (full_product((own_ref, core_ref, y_ref, diag_ref), w_ref, 0) * 0.125).astype(BF16)
    for i in range(long_count):
        at = pl.multiple_of(order_ref[i] * draft, draft)
        out_ref[pl.ds(i * draft, draft)] = q_ref[pl.ds(at, draft), :]


def key_value_kernel(own_ref, core_ref, y_ref, diag_ref, w_ref, select_ref, k_ref, v_ref, acc_ref):
    hid = (own_ref, core_ref, y_ref, diag_ref)
    k_ref[...] = full_product(hid, w_ref, 1).astype(BF16)
    v_ref[...] = full_product(hid, w_ref, 2).astype(BF16)
    groups, side = select_ref.shape[0], select_ref.shape[1] // 2
    for g in range(groups):
        rows = pl.ds(g * side, side)
        pairs = jnp.concatenate([k_ref[rows], v_ref[rows]], axis=0)
        path = jnp.dot(select_ref[g], pairs, preferred_element_type=F32).astype(BF16)
        acc_ref[rows] = path.reshape(side, 2, path.shape[1])


def remote_kernel(dims, page_indices, *refs):
    page_len, draft, heads, long_count = dims
    count = len(page_indices)
    msgs, table_ref, pool_ref = refs[:count], refs[count], refs[count + 1]
    outs = refs[count + 2 : 2 * count + 2]
    page_ref, sems = refs[2 * count + 2 :]
    width = heads * HD
    tokens = long_count * draft
    copies, limits = [], []
    for n, page_index in enumerate(page_indices):
        facts = msgs[n][pl.ds(tokens, META), :].astype(F32)[:, :page_len]
        for i in range(long_count):
            member = jnp.max(facts[3 * i : 3 * i + 1]).astype(jnp.int32)
            copy = pltpu.make_async_copy(
                pool_ref.at[table_ref[page_index, member]], page_ref.at[n, i], sems.at[n, i]
            )
            copy.start()
            copies.append(copy)
            length = facts[3 * i + 1 : 3 * i + 2] * page_len + facts[3 * i + 2 : 3 * i + 3]
            limits.append(length - page_index * page_len)
    picker = unpick(page_len)
    lane = lax.broadcasted_iota(jnp.int32, (heads * draft, page_len), 1).astype(F32)
    for copy in copies:
        copy.wait()
    for n in range(count):
        stats = []
        for i in range(long_count):
            stacked = head_rows(msgs[n][pl.ds(i * draft, draft), :], heads)
            keys, values = split_page(page_ref[n, i], picker, page_len)
            scores = jnp.where(lane < limits[n * long_count + i], dot_t(stacked, keys), NEG)
            mixed, top, total = attend([scores], [values])
            outs[n][pl.ds(i * draft, draft)] = head_lanes(mixed, heads, draft, width).astype(BF16)
            stats += list(split3(to_row(top))) + list(split3(to_row(total)))
        stats.append(jnp.zeros((META - len(stats), width), BF16))
        outs[n][pl.ds(tokens, META)] = jnp.concatenate([s.astype(F32) for s in stats], axis=0).astype(BF16)


def local_kernel(dims, len_ref, table_ref, q_ref, k_ref, v_ref, bias_ref, near_ref, pool_ref,
                 rest_ref, long_ref, stats_ref, order_ref, first_ref, second_ref, sems):
    requests, draft, heads, page_len, long_count = dims
    width = heads * HD
    write_order(len_ref, order_ref, requests, page_len)
    copies = []
    for p in range(requests):
        r = order_ref[p]
        copies.append(pltpu.make_async_copy(pool_ref.at[table_ref[0, r]], first_ref.at[p], sems.at[p, 0]))
        copies.append(pltpu.make_async_copy(near_ref.at[r], second_ref.at[p], sems.at[p, 1]))
    for copy in copies:
        copy.start()
    picker = unpick(page_len)
    lane = lax.broadcasted_iota(jnp.int32, (heads * draft, 2 * page_len), 1)
    for copy in copies:
        copy.wait()
    stats = []
    for p in range(requests):
        r = order_ref[p]
        rows = pl.ds(pl.multiple_of(r * draft, draft), draft)
        stacked = head_rows(q_ref[rows, :], heads)
        bias = jnp.concatenate([bias_ref[rows, :]] * heads, axis=0)
        key_0, value_0 = split_page(first_ref[p], picker, page_len)
        key_1, value_1 = split_page(second_ref[p], picker, page_len)
        paged = dot_t(stacked, jnp.concatenate([key_0, key_1], axis=0))
        mixed, top, total = attend(
            [jnp.where(lane < len_ref[r], paged, NEG), dot_t(stacked, k_ref[rows, :]) + bias],
            [jnp.concatenate([value_0, value_1], axis=0), v_ref[rows, :]],
        )
        if p < long_count:
            long_ref[pl.ds(p * draft, draft)] = head_lanes(mixed, heads, draft, width)
            stats += [to_row(top), to_row(total)]
        else:
            whole = head_lanes(mixed, heads, draft, width) / head_lanes(total, heads, draft, width)
            rest_ref[pl.ds((p - long_count) * draft, draft)] = whole.astype(BF16)
    stats.append(jnp.zeros((META - len(stats), width), F32))
    stats_ref[...] = jnp.concatenate(stats, axis=0)


def merge_kernel(dims, count, own_ref, stats_ref, *refs):
    draft, heads, long_count = dims
    width = heads * HD
    msgs, out_ref = refs[:count], refs[count]
    tokens = long_count * draft
    own = stats_ref[...]
    facts = [ref[pl.ds(tokens, META), :].astype(F32) for ref in msgs]
    for i in range(long_count):
        tops = [own[2 * i : 2 * i + 1]]
        totals = [own[2 * i + 1 : 2 * i + 2]]
        for f in facts:
            b = 6 * i
            tops.append(f[b : b + 1] + f[b + 1 : b + 2] + f[b + 2 : b + 3])
            totals.append(f[b + 3 : b + 4] + f[b + 4 : b + 5] + f[b + 5 : b + 6])
        best = functools.reduce(jnp.maximum, tops)
        scales = [jnp.exp(t - best) for t in tops]
        denom = sum(s * t for s, t in zip(scales, totals))
        factors = jnp.concatenate([s / denom for s in scales] + [jnp.zeros((128 - len(scales), width), F32)], axis=0)
        factors = jnp.transpose(factors)
        rows = pl.ds(i * draft, draft)
        out = own_ref[rows, :] * head_lanes(factors[:, :1], heads, draft, width)
        for j, ref in enumerate(msgs):
            out += ref[rows, :].astype(F32) * head_lanes(factors[:, j + 1 : j + 2], heads, draft, width)
        out_ref[rows] = out.astype(BF16)


def norm(values, sums, squares, gain, width_all):
    center = sums / width_all
    spread = squares / width_all - center * center
    return (values - center) * lax.rsqrt(spread + EPS) * gain


def forward_kernel(dims, len_ref, *refs):
    requests, draft, page_len, first, count = dims
    att, hid, wout = refs[0:4], refs[4:8], refs[8:12]
    gain_ref, up_ref, down_ref = refs[12:15]
    parts, normed_ref = refs[15:19], refs[19]
    order_ref, z_ref = refs[20:]
    me = lax.axis_index("tp")
    share = hid[0].shape[1]
    width_all = z_ref.shape[1]
    write_order(len_ref, order_ref, requests, page_len)
    for p in range(count):
        rows = pl.ds(pl.multiple_of(order_ref[first + p] * draft, draft), draft)
        for flip in range(4):
            at = pl.ds(pl.multiple_of((me ^ flip) * share, share), share)
            z_ref[pl.ds(p * draft, draft), at] = hid[flip][rows, :].astype(F32)
    branch = sum(jnp.dot(a[...], w[...], preferred_element_type=F32) for a, w in zip(att, wout))
    z = z_ref[...] + branch
    sums = jnp.sum(z, axis=-1, keepdims=True)
    squares = jnp.sum(z * z, axis=-1, keepdims=True)
    normed_wide = norm(z, sums, squares, gain_ref[...], width_all)
    normed = normed_wide.astype(BF16)
    z_ref[...] = normed_wide
    normed_ref[...] = z_ref[:, pl.ds(pl.multiple_of(me * share, share), share)].astype(BF16)
    inner = jnp.dot(normed, up_ref[...], preferred_element_type=F32)
    inner = (0.5 * inner * (1.0 + lax.erf(inner * (0.5 ** 0.5)))).astype(BF16)
    for flip in range(4):
        at = pl.ds(pl.multiple_of((me ^ flip) * share, share), share)
        parts[flip][...] = jnp.dot(inner, down_ref[:, at], preferred_element_type=F32).astype(BF16)


def gather_sum_kernel(a_ref, b_ref, c_ref, d_ref, normed_ref, x_ref, stats_ref):
    x = normed_ref[...].astype(F32) + (
        (a_ref[...].astype(F32) + b_ref[...].astype(F32)) + (c_ref[...].astype(F32) + d_ref[...].astype(F32))
    )
    x_ref[...] = x
    row = lax.broadcasted_iota(jnp.int32, stats_ref.shape, 0)
    sums = to_row(jnp.sum(x, axis=-1, keepdims=True))
    squares = to_row(jnp.sum(x * x, axis=-1, keepdims=True))
    stats_ref[...] = jnp.where(row == 0, sums, jnp.where(row == 1, squares, 0.0))


def finish_kernel(dims, len_ref, gain_ref, *refs):
    requests, draft, page_len, counts = dims
    order_ref = refs[-1]
    out_ref = refs[-2]
    me = lax.axis_index("tp")
    write_order(len_ref, order_ref, requests, page_len)
    share = out_ref.shape[1]
    gain = gain_ref[:, pl.ds(pl.multiple_of(me * share, share), share)]
    width_all = gain_ref.shape[1]
    place = 0
    for g, count in enumerate(counts):
        x_ref = refs[5 * g]
        stats = sum(ref[...] for ref in refs[5 * g + 1 : 5 * g + 5])
        stats = jnp.transpose(jnp.concatenate([stats] * (128 // stats.shape[0]), axis=0))
        y = norm(x_ref[...], stats[:, 0:1], stats[:, 1:2], gain, width_all).astype(BF16)
        for p in range(count):
            rows = pl.ds(pl.multiple_of(order_ref[place] * draft, draft), draft)
            out_ref[rows, :] = y[p * draft : (p + 1) * draft]
            place += 1


def shards(hidden_in, w_qkv, w_out, first_gain, w_up, w_down, second_gain, cache_pool,
           page_table, cache_len, tree_parent, accept_node):
    tokens, share = hidden_in.shape
    requests, draft = tree_parent.shape
    width = w_qkv.shape[2]
    heads = width // HD
    pages = page_table.shape[0]
    page_len = cache_pool.shape[1]
    width_all = w_qkv.shape[0]
    long_count = (requests + 3) // 4
    long_rows = long_count * draft
    msg_rows = long_rows + META
    side = 4 * draft
    dma = pltpu.SemaphoreType.DMA
    order = pltpu.SMEM((requests,), jnp.int32)

    w_planes = jnp.transpose(w_qkv, (1, 0, 2))
    gain_1 = first_gain.reshape(1, -1)
    gain_2 = second_gain.reshape(1, -1)
    parents = tree_parent.reshape(requests * draft // side, side)

    hid_y = send_tp(hidden_in, 2)
    hid_core = send_tp(hidden_in, 1)
    hid_diag = send_tp(hid_y, 1)
    hid = (hidden_in, hid_core, hid_y, hid_diag)
    near = call(
        functools.partial(pick_pages_kernel, (requests, 1)),
        shape_of((requests,) + cache_pool.shape[1:], BF16), [SMEM, HBM], HBM, [dma((requests,))],
        (page_table, cache_pool), "pick_pages", after=(hid_core,),
    )
    near = send_req(near, -1)

    bias, select = call(
        functools.partial(tree_kernel, (requests, draft)),
        [shape_of((tokens, draft), F32), shape_of((requests * draft // side, 2 * side, 2 * side), BF16)],
        [SMEM, VMEM], [VMEM] * 2, [pltpu.VMEM((side, side), F32)],
        (accept_node, parents), "tree", flops=14 * 256 ** 3 * 2,
    )

    block = shape_of((tokens, width), BF16)
    queries, message = call(
        functools.partial(query_kernel, (requests, draft, page_len, long_count)),
        [block, shape_of((msg_rows, width), BF16)],
        [SMEM] + [VMEM] * 5, [VMEM] * 2, [order],
        (cache_len, *hid, w_planes), "queries",
        flops=2 * tokens * width_all * width, nbytes=2 * width_all * width, after=(bias,),
    )
    queue = sorted(range(2, pages), key=lambda j: (abs(2 * j - pages), j))
    asked = {j: send_req(message, j) for j in queue}

    w_later, _ = lax.optimization_barrier((w_out, queries))
    wout_core = send_tp(w_later, 1)
    wout_y = send_tp(w_later, 2)
    wout_diag = send_tp(wout_y, 1)
    wout = (w_out, wout_core, wout_y, wout_diag)

    key_new, value_new, accepted = call(
        key_value_kernel,
        [block, block, shape_of((tokens, 2, width), BF16)],
        [VMEM] * 6, [VMEM] * 3, [],
        (*hid, w_planes, select), "keys_values",
        flops=2 * tokens * width_all * width * 2, nbytes=2 * width_all * width * 2, after=(message,),
    )

    answers, last = [], (key_new,)
    half = (len(queue) + 1) // 2
    for group in (queue[:half], queue[half:]):
        outs = call(
            functools.partial(remote_kernel, (page_len, draft, heads, long_count), tuple(group)),
            [shape_of((msg_rows, width), BF16)] * len(group),
            [VMEM] * len(group) + [SMEM, HBM], [VMEM] * len(group),
            [pltpu.VMEM((len(group), long_count) + cache_pool.shape[1:], BF16), dma((len(group), long_count))],
            (*[asked[j] for j in group], page_table, cache_pool), "remote_%d" % group[0],
            flops=len(group) * long_count * 6 * 256 ** 3, nbytes=len(group) * long_count * 131072, after=last,
        )
        answers += [send_req(answer, -j) for j, answer in zip(group, outs)]
        last = (outs[0],)

    rest, long_own, long_stats = call(
        functools.partial(local_kernel, (requests, draft, heads, page_len, long_count)),
        [shape_of((tokens - long_rows, width), BF16), shape_of((long_rows, width), F32), shape_of((META, width), F32)],
        [SMEM, SMEM, VMEM, VMEM, VMEM, VMEM, HBM, HBM], [VMEM] * 3,
        [order, pltpu.VMEM((requests,) + cache_pool.shape[1:], BF16),
         pltpu.VMEM((requests,) + cache_pool.shape[1:], BF16), dma((requests, 2))],
        (cache_len, page_table, queries, key_new, value_new, bias, near, cache_pool), "local_attention",
        flops=requests * 14 * 256 ** 3, nbytes=requests * 2 * 131072, after=last,
    )

    def forward(attended, first, count, name):
        rows = count * draft
        att_core = send_tp(attended, 1)
        att_y = send_tp(attended, 2)
        att_diag = send_tp(att_y, 1)
        part = shape_of((rows, share), BF16)
        outs = call(
            functools.partial(forward_kernel, (requests, draft, page_len, first, count)),
            [part] * 5, [SMEM] + [VMEM] * 15, [VMEM] * 5,
            [order, pltpu.VMEM((rows, width_all), F32)],
            (cache_len, attended, att_core, att_y, att_diag, *hid, *wout, gain_1, w_up, w_down), name,
            flops=2 * rows * width_all * (width_all + 2 * w_up.shape[1]), nbytes=3 * 2 * 1024 * 1024,
        )
        got = [send_tp(outs[flip], flip) for flip in (2, 3, 1)]
        x, stats = call(
            gather_sum_kernel,
            [shape_of((rows, share), F32), shape_of((8, rows), F32)], [VMEM] * 5, [VMEM] * 2, [],
            (outs[0], *got, outs[4]), name + "_sum",
        )
        return (x, stats) + tuple(send_tp(stats, flip) for flip in (2, 3, 1))

    tail_rest = forward(rest, long_count, requests - long_count, "forward_short")

    merged = call(
        functools.partial(merge_kernel, (draft, heads, long_count), len(answers)),
        shape_of((long_rows, width), BF16), [VMEM] * (2 + len(answers)), VMEM, [],
        (long_own, long_stats, *answers), "merge",
    )
    tail_long = forward(merged, 0, long_count, "forward_long")

    layer_out = call(
        functools.partial(finish_kernel, (requests, draft, page_len, (long_count, requests - long_count))),
        shape_of((tokens, share), BF16), [SMEM] + [VMEM] * 11, VMEM, [order],
        (cache_len, gain_2, *tail_long, *tail_rest), "finish",
    )
    accepted_kv = accepted.reshape(requests, draft, 2, width)
    return (layer_out, accepted_kv)


def solution(mesh):
    placed = (
        P("req", "tp"),
        P(None, None, "tp"),
        P("tp", None),
        P(),
        P(None, "tp"),
        P("tp", None),
        P(),
        P("req", None, None, "tp"),
        P("req", None),
        P("req"),
        P("req", None),
        P("req"),
    )
    return jax.shard_map(
        shards,
        mesh=mesh,
        in_specs=placed,
        out_specs=(P("req", "tp"), P("req", None, None, "tp")),
        check_vma=False,
    )
```

```python
import functools

import jax
import jax.numpy as jnp
from jax import lax
from jax.experimental import pallas as pl
from jax.experimental.pallas import tpu as pltpu
from jax.sharding import PartitionSpec as P

HD = 64
NEG = -1e30
EPS = 1e-05
META = 16
F32 = jnp.float32
BF16 = jnp.bfloat16

VMEM = pl.BlockSpec(memory_space=pltpu.VMEM)
SMEM = pl.BlockSpec(memory_space=pltpu.SMEM)
ANY = pl.BlockSpec(memory_space=pl.ANY)


def shape_of(dims, dtype):
    return jax.ShapeDtypeStruct(dims, dtype)


def call(kernel, outs, ins, out_specs, scratch, operands, name, flops=0, nbytes=0, after=(), vmem=24):
    split = len(operands)

    def body(*refs):
        kernel(*refs[:split], *refs[split + len(after) :])

    return pl.pallas_call(
        body,
        out_shape=outs,
        in_specs=list(ins) + [ANY] * len(after),
        out_specs=out_specs,
        scratch_shapes=scratch,
        compiler_params=pltpu.CompilerParams(vmem_limit_bytes=vmem << 20),
        cost_estimate=pl.CostEstimate(flops=flops, bytes_accessed=nbytes, transcendentals=0),
        name=name,
    )(*operands, *after)


def send_req(value, by):
    size = lax.axis_size("req")
    return lax.ppermute(value, "req", [(i, (i + by) % size) for i in range(size)])


def send_tp(value, flip):
    size = lax.axis_size("tp")
    return lax.ppermute(value, "tp", [(i, i ^ flip) for i in range(size)])


def write_order(len_ref, order_ref, requests, page_len):
    flags = [(len_ref[r] > 2 * page_len).astype(jnp.int32) for r in range(requests)]
    total = sum(flags)
    before = jnp.int32(0)
    for r in range(requests):
        place = jnp.where(flags[r] > 0, before, total + r - before)
        order_ref[place] = jnp.int32(r)
        before = before + flags[r]


def split3(value):
    high = value.astype(BF16)
    rest = value - high.astype(F32)
    middle = rest.astype(BF16)
    low = (rest - middle.astype(F32)).astype(BF16)
    return high, middle, low


def dot_t(a, b):
    return lax.dot_general(a, b, (((1,), (1,)), ((), ())), preferred_element_type=F32)


def head_rows(value, heads):
    lane = lax.broadcasted_iota(jnp.int32, value.shape, 1) // HD
    zero = jnp.zeros_like(value)
    return jnp.concatenate([jnp.where(lane == h, value, zero) for h in range(heads)], axis=0)


def head_lanes(stacked, heads, rows, width):
    lane = lax.broadcasted_iota(jnp.int32, (rows, width), 1) // HD
    out = jnp.zeros((rows, width), stacked.dtype)
    for h in range(heads):
        piece = stacked[h * rows : (h + 1) * rows]
        if piece.shape[1] != width:
            piece = jnp.broadcast_to(piece[:, :1], (rows, width))
        out = jnp.where(lane == h, piece, out)
    return out


def unpick(page_len):
    row = lax.broadcasted_iota(jnp.int32, (2 * page_len, 2 * page_len), 0)
    col = lax.broadcasted_iota(jnp.int32, (2 * page_len, 2 * page_len), 1)
    source = jnp.where(row < page_len, 2 * row, 2 * (row - page_len) + 1)
    return jnp.where(source == col, 1.0, 0.0).astype(BF16)


def split_page(page, picker, page_len):
    flat = page.reshape(2 * page_len, page.shape[2])
    both = jnp.dot(picker, flat, preferred_element_type=F32).astype(BF16)
    return both[:page_len], both[page_len:]


def to_row(column):
    return jnp.transpose(jnp.broadcast_to(column, (column.shape[0], 128)))[:1]


def attend(scores, values):
    top = functools.reduce(jnp.maximum, [jnp.max(s, axis=-1, keepdims=True) for s in scores])
    weights = [jnp.exp(s - top).astype(BF16) for s in scores]
    total = sum(jnp.sum(w.astype(F32), axis=-1, keepdims=True) for w in weights)
    mixed = sum(jnp.dot(w, v, preferred_element_type=F32) for w, v in zip(weights, values))
    return mixed, top, total


def pages_kernel(table_ref, pool_ref, key_ref, value_ref, page_ref, sems):
    rows, requests, page_len = key_ref.shape[:3]
    copies = [
        pltpu.make_async_copy(pool_ref.at[table_ref[j, m]], page_ref.at[j, m], sems.at[j, m])
        for j in range(rows)
        for m in range(requests)
    ]
    for copy in copies:
        copy.start()
    picker = unpick(page_len)
    for copy in copies:
        copy.wait()
    for j in range(rows):
        for m in range(requests):
            key_ref[j, m], value_ref[j, m] = split_page(page_ref[j, m], picker, page_len)


def full_product(hid, w_ref, part):
    me = lax.axis_index("tp")
    share = hid[0].shape[1]
    total = None
    for flip, ref in enumerate(hid):
        at = pl.multiple_of((me ^ flip) * share, share)
        term = jnp.dot(ref[...], w_ref[part, pl.ds(at, share), :], preferred_element_type=F32)
        total = term if total is None else total + term
    return total


def tree_kernel(dims, accept_ref, parent_ref, bias_ref, select_ref, wide_ref):
    requests, draft = dims
    group = parent_ref.shape[1] // draft
    side = group * draft
    row = lax.broadcasted_iota(jnp.int32, (side, side), 0)
    col = lax.broadcasted_iota(jnp.int32, (side, side), 1)
    eye = jnp.where(row == col, 1.0, 0.0)
    up = []
    for g in range(requests // group):
        parent = parent_ref[pl.ds(g, 1), :]
        lane = lax.broadcasted_iota(jnp.int32, parent.shape, 1)
        target = jnp.where(parent < 0, -1, parent + (lane // draft) * draft)
        up.append((eye + jnp.where(row == target, 1.0, 0.0)).astype(BF16))
    for sweep in range(max(1, (draft - 1).bit_length())):
        up = [jnp.minimum(jnp.dot(u, u, preferred_element_type=F32), 1.0).astype(BF16) for u in up]
    row = lax.broadcasted_iota(jnp.int32, (2 * side, 2 * side), 0)
    col = lax.broadcasted_iota(jnp.int32, (2 * side, 2 * side), 1)
    fits = (row % 2 == col // side) & (row // (2 * draft) == (col % side) // draft)
    level = ((row // 2) % draft).astype(F32)
    for g in range(requests // group):
        wide = up[g].astype(F32)
        reach = jnp.transpose(wide)
        wide_ref[...] = reach
        depth = jnp.sum(wide, axis=0, keepdims=True) - 1.0
        chosen = jnp.zeros((1, side), F32)
        for i in range(group):
            r = g * group + i
            own = reach[i * draft : (i + 1) * draft, i * draft : (i + 1) * draft]
            bias_ref[pl.ds(r * draft, draft), :] = jnp.where(own > 0.5, 0.0, NEG)
            chosen += wide_ref[pl.ds(i * draft + accept_ref[r], 1), :]
        depth = jnp.concatenate([depth, depth], axis=1)
        chosen = jnp.concatenate([chosen, chosen], axis=1)
        select_ref[g] = jnp.where(fits & (depth == level), chosen, 0.0).astype(BF16)


def query_kernel(dims, len_ref, own_ref, core_ref, y_ref, diag_ref, w_ref, q_ref, out_ref, near_ref, order_ref):
    requests, draft, page_len, long_count = dims
    rows = long_count * draft
    width = q_ref.shape[1]
    write_order(len_ref, order_ref, requests, page_len)
    row = lax.broadcasted_iota(jnp.int32, (META, width), 0)
    facts = jnp.zeros((META, width), jnp.int32)
    for i in range(long_count):
        member = order_ref[i]
        length = len_ref[member]
        facts = jnp.where(row == 3 * i, member, facts)
        facts = jnp.where(row == 3 * i + 1, length // page_len, facts)
        facts = jnp.where(row == 3 * i + 2, length % page_len, facts)
    out_ref[pl.ds(rows, META)] = facts.astype(F32).astype(BF16)
    limits = jnp.zeros((META, width), jnp.int32)
    for r in range(requests):
        limits = jnp.where(row == r, jnp.clip(len_ref[r] - page_len, 0, page_len), limits)
    near_ref[pl.ds(requests * draft, META)] = limits.astype(F32).astype(BF16)
    queries = (full_product((own_ref, core_ref, y_ref, diag_ref), w_ref, 0) * 0.125).astype(BF16)
    q_ref[...] = queries
    near_ref[pl.ds(0, requests * draft)] = queries
    for i in range(long_count):
        at = pl.multiple_of(order_ref[i] * draft, draft)
        out_ref[pl.ds(i * draft, draft)] = q_ref[pl.ds(at, draft), :]


def key_value_kernel(own_ref, core_ref, y_ref, diag_ref, w_ref, select_ref, k_ref, v_ref, acc_ref):
    hid = (own_ref, core_ref, y_ref, diag_ref)
    k_ref[...] = full_product(hid, w_ref, 1).astype(BF16)
    v_ref[...] = full_product(hid, w_ref, 2).astype(BF16)
    groups, side = select_ref.shape[0], select_ref.shape[1] // 2
    for g in range(groups):
        rows = pl.ds(g * side, side)
        pairs = jnp.concatenate([k_ref[rows], v_ref[rows]], axis=0)
        path = jnp.dot(select_ref[g], pairs, preferred_element_type=F32).astype(BF16)
        acc_ref[rows] = path.reshape(side, 2, path.shape[1])


def remote_kernel(dims, page_indices, *refs, between=None):
    page_len, draft, heads, long_count = dims
    count = len(page_indices)
    msgs, table_ref, pool_ref = refs[:count], refs[count], refs[count + 1]
    outs = refs[count + 2 : 2 * count + 2]
    page_ref, sems = refs[2 * count + 2 :]
    width = heads * HD
    tokens = long_count * draft
    copies, limits = [], []
    for n, page_index in enumerate(page_indices):
        facts = msgs[n][pl.ds(tokens, META), :].astype(F32)[:, :page_len]
        for i in range(long_count):
            member = jnp.max(facts[3 * i : 3 * i + 1]).astype(jnp.int32)
            copy = pltpu.make_async_copy(
                pool_ref.at[table_ref[page_index, member]], page_ref.at[n, i], sems.at[n, i]
            )
            copy.start()
            copies.append(copy)
            length = facts[3 * i + 1 : 3 * i + 2] * page_len + facts[3 * i + 2 : 3 * i + 3]
            limits.append(length - page_index * page_len)
    picker = unpick(page_len)
    lane = lax.broadcasted_iota(jnp.int32, (heads * draft, page_len), 1).astype(F32)
    if between is not None:
        between()
    for copy in copies:
        copy.wait()
    for n in range(count):
        stats = []
        for i in range(long_count):
            stacked = head_rows(msgs[n][pl.ds(i * draft, draft), :], heads)
            keys, values = split_page(page_ref[n, i], picker, page_len)
            scores = jnp.where(lane < limits[n * long_count + i], dot_t(stacked, keys), NEG)
            mixed, top, total = attend([scores], [values])
            outs[n][pl.ds(i * draft, draft)] = head_lanes(mixed, heads, draft, width).astype(BF16)
            stats += list(split3(to_row(top))) + list(split3(to_row(total)))
        stats.append(jnp.zeros((META - len(stats), width), BF16))
        outs[n][pl.ds(tokens, META)] = jnp.concatenate([s.astype(F32) for s in stats], axis=0).astype(BF16)


def near_pages(dims, msg_ref, key_ref, value_ref, out_ref):
    draft, heads = dims
    requests, page_len, width = key_ref.shape[1:]
    tokens = requests * draft
    limits = msg_ref[pl.ds(tokens, META), :].astype(F32)[:, :page_len]
    lane = lax.broadcasted_iota(jnp.int32, (heads * draft, page_len), 1).astype(F32)
    stats = []
    for r in range(requests):
        stacked = head_rows(msg_ref[pl.ds(r * draft, draft), :], heads)
        scores = jnp.where(lane < limits[r : r + 1], dot_t(stacked, key_ref[1, r]), NEG)
        mixed, top, total = attend([scores], [value_ref[1, r]])
        out_ref[pl.ds(r * draft, draft)] = head_lanes(mixed, heads, draft, width).astype(BF16)
        stats += list(split3(to_row(top))) + list(split3(to_row(total)))
    out_ref[pl.ds(tokens, len(stats))] = jnp.concatenate([s.astype(F32) for s in stats], axis=0).astype(BF16)


def visiting_kernel(dims, page_indices, msg_ref, key_ref, value_ref, *refs):
    page_len, draft, heads, long_count = dims
    count = len(page_indices)
    near = functools.partial(near_pages, (draft, heads), msg_ref, key_ref, value_ref, refs[count + 2])
    remote_kernel(dims, page_indices, *refs[: count + 2], *refs[count + 3 :], between=near)


def local_kernel(dims, len_ref, q_ref, k_ref, v_ref, bias_ref, key_ref, value_ref, keep_ref, out_ref, stats_ref, kept_ref):
    kept_ref[...] = keep_ref[...]
    requests, draft, heads = dims
    page_len, width = key_ref.shape[2:]
    lane = lax.broadcasted_iota(jnp.int32, (heads * draft, page_len), 1)
    stats = []
    for r in range(requests):
        rows = pl.ds(r * draft, draft)
        stacked = head_rows(q_ref[rows, :], heads)
        bias = jnp.concatenate([bias_ref[rows, :]] * heads, axis=0)
        mixed, top, total = attend(
            [jnp.where(lane < len_ref[r], dot_t(stacked, key_ref[0, r]), NEG), dot_t(stacked, k_ref[rows, :]) + bias],
            [value_ref[0, r], v_ref[rows, :]],
        )
        out_ref[rows] = head_lanes(mixed, heads, draft, width)
        stats += [to_row(top), to_row(total)]
    stats_ref[...] = jnp.concatenate(stats, axis=0)


def merge_kernel(dims, span, len_ref, own_ref, stats_ref, near_ref, *refs):
    requests, draft, heads, page_len = dims
    width = heads * HD
    msgs, out_ref, order_ref, facts_ref = refs[:-3], refs[-3], refs[-2], refs[-1]
    write_order(len_ref, order_ref, requests, page_len)
    tokens = requests * draft
    facts_ref[...] = near_ref[pl.ds(tokens, 6 * requests), :].astype(F32)
    far = [ref[pl.ds(ref.shape[0] - META, META), :].astype(F32) for ref in msgs]
    factors = []
    for i, p in enumerate(range(*span)):
        r = order_ref[p]
        near = [facts_ref[pl.ds(6 * r + k, 1), :] for k in range(6)]
        tops = [stats_ref[pl.ds(2 * r, 1), :], near[0] + near[1] + near[2]]
        totals = [stats_ref[pl.ds(2 * r + 1, 1), :], near[3] + near[4] + near[5]]
        for f in far:
            part = [f[6 * i + k : 6 * i + k + 1] for k in range(6)]
            tops.append(part[0] + part[1] + part[2])
            totals.append(part[3] + part[4] + part[5])
        best = functools.reduce(jnp.maximum, tops)
        scales = [jnp.exp(t - best) for t in tops]
        denom = sum(s * t for s, t in zip(scales, totals))
        factors += [s / denom for s in scales]
    each = 2 + len(far)
    factors.append(jnp.zeros((128 - len(factors), width), F32))
    columns = jnp.transpose(jnp.concatenate(factors, axis=0))
    for i, p in enumerate(range(*span)):
        rows = pl.ds(pl.multiple_of(order_ref[p] * draft, draft), draft)
        parts = [own_ref[rows, :], near_ref[rows, :].astype(F32)]
        parts += [ref[pl.ds(i * draft, draft), :].astype(F32) for ref in msgs]
        out = None
        for j, part in enumerate(parts):
            c = each * i + j
            term = part * head_lanes(columns[:, c : c + 1], heads, draft, width)
            out = term if out is None else out + term
        out_ref[pl.ds(i * draft, draft)] = out.astype(BF16)


def norm(values, sums, squares, gain, width_all):
    center = sums / width_all
    spread = squares / width_all - center * center
    return (values - center) * lax.rsqrt(spread + EPS) * gain


def forward_kernel(dims, len_ref, *refs):
    requests, draft, page_len, first, count = dims
    att, hid = refs[0:4], refs[4:8]
    wout_ref, gain_ref, up_ref, down_ref = refs[8:12]
    parts, normed_ref = refs[12:16], refs[16]
    order_ref, z_ref, hid_v, wout_v, up_v, down_v, sems = refs[17:]
    pairs = [(hid[k], hid_v.at[k]) for k in range(4)] + [(wout_ref, wout_v), (up_ref, up_v), (down_ref, down_v)]
    copies = [pltpu.make_async_copy(src, dst, sems.at[n]) for n, (src, dst) in enumerate(pairs)]
    for copy in copies:
        copy.start()
    me = lax.axis_index("tp")
    share = hid[0].shape[1]
    width_all = z_ref.shape[1]
    write_order(len_ref, order_ref, requests, page_len)
    for copy in copies[:4]:
        copy.wait()
    for p in range(count):
        rows = pl.ds(pl.multiple_of(order_ref[first + p] * draft, draft), draft)
        for flip in range(4):
            at = pl.ds(pl.multiple_of((me ^ flip) * share, share), share)
            z_ref[pl.ds(p * draft, draft), at] = hid_v[flip, rows, :].astype(F32)
    copies[4].wait()
    branch = None
    for flip in range(4):
        at = pl.ds(pl.multiple_of((me ^ flip) * share, share), share)
        term = jnp.dot(att[flip][...], wout_v[at, :], preferred_element_type=F32)
        branch = term if branch is None else branch + term
    z = z_ref[...] + branch
    sums = jnp.sum(z, axis=-1, keepdims=True)
    squares = jnp.sum(z * z, axis=-1, keepdims=True)
    normed_wide = norm(z, sums, squares, gain_ref[...], width_all)
    normed = normed_wide.astype(BF16)
    z_ref[...] = normed_wide
    normed_ref[...] = z_ref[:, pl.ds(pl.multiple_of(me * share, share), share)].astype(BF16)
    copies[5].wait()
    inner = jnp.dot(normed, up_v[...], preferred_element_type=F32)
    inner = (0.5 * inner * (1.0 + lax.erf(inner * (0.5 ** 0.5)))).astype(BF16)
    copies[6].wait()
    for flip in range(4):
        at = pl.ds(pl.multiple_of((me ^ flip) * share, share), share)
        parts[flip][...] = jnp.dot(inner, down_v[:, at], preferred_element_type=F32).astype(BF16)


def gather_sum_kernel(*refs):
    groups = (len(refs) - 1) // 6
    stats_ref = refs[-1]
    place = 0
    for g in range(groups):
        a_ref, b_ref, c_ref, d_ref, normed_ref = refs[5 * g : 5 * g + 5]
        x = normed_ref[...].astype(F32) + (
            (a_ref[...].astype(F32) + b_ref[...].astype(F32)) + (c_ref[...].astype(F32) + d_ref[...].astype(F32))
        )
        refs[5 * groups + g][...] = x
        rows = x.shape[0]
        row = lax.broadcasted_iota(jnp.int32, (stats_ref.shape[0], rows), 0)
        sums = to_row(jnp.sum(x, axis=-1, keepdims=True))
        squares = to_row(jnp.sum(x * x, axis=-1, keepdims=True))
        stats_ref[:, pl.ds(place, rows)] = jnp.where(row == 0, sums, jnp.where(row == 1, squares, 0.0))
        place += rows


def finish_kernel(dims, len_ref, gain_ref, *refs):
    requests, draft, page_len = dims
    order_ref = refs[-1]
    out_ref = refs[-2]
    stats_refs = refs[-6:-2]
    me = lax.axis_index("tp")
    write_order(len_ref, order_ref, requests, page_len)
    share = out_ref.shape[1]
    gain = gain_ref[:, pl.ds(pl.multiple_of(me * share, share), share)]
    width_all = gain_ref.shape[1]
    stats = sum(ref[...] for ref in stats_refs)
    stats = jnp.transpose(jnp.concatenate([stats] * (128 // stats.shape[0]), axis=0))
    place = 0
    for x_ref in refs[:-6]:
        count = x_ref.shape[0] // draft
        own = stats[place * draft : (place + count) * draft]
        y = norm(x_ref[...], own[:, 0:1], own[:, 1:2], gain, width_all).astype(BF16)
        for p in range(count):
            rows = pl.ds(pl.multiple_of(order_ref[place] * draft, draft), draft)
            out_ref[rows, :] = y[p * draft : (p + 1) * draft]
            place += 1


def shards(hidden_in, w_qkv, w_out, first_gain, w_up, w_down, second_gain, cache_pool,
           page_table, cache_len, tree_parent, accept_node):
    tokens, share = hidden_in.shape
    cache_pool, w_up, w_down = [pltpu.with_memory_space_constraint(a, pltpu.HBM) for a in (cache_pool, w_up, w_down)]
    requests, draft = tree_parent.shape
    width = w_qkv.shape[2]
    heads = width // HD
    pages = page_table.shape[0]
    page_len = cache_pool.shape[1]
    width_all = w_qkv.shape[0]
    long_count = (requests + 3) // 4
    long_rows = long_count * draft
    msg_rows = long_rows + META
    side = 4 * draft
    dma = pltpu.SemaphoreType.DMA
    order = pltpu.SMEM((requests,), jnp.int32)

    w_planes = jnp.transpose(w_qkv, (1, 0, 2))
    gain_1 = first_gain.reshape(1, -1)
    gain_2 = second_gain.reshape(1, -1)
    parents = tree_parent.reshape(requests * draft // side, side)

    hid_y = send_tp(hidden_in, 2)
    hid_core = send_tp(hidden_in, 1)
    wout = lax.all_gather(w_out, "tp", axis=0, tiled=True)

    bias, select = call(
        functools.partial(tree_kernel, (requests, draft)),
        [shape_of((tokens, draft), F32), shape_of((requests * draft // side, 2 * side, 2 * side), BF16)],
        [SMEM, VMEM], [VMEM] * 2, [pltpu.VMEM((side, side), F32)],
        (accept_node, parents), "tree", flops=14 * 256 ** 3 * 2,
    )
    split = shape_of((2, requests, page_len, width), BF16)
    page_keys, page_values = call(
        pages_kernel, [split, split], [SMEM, ANY], [VMEM] * 2,
        [pltpu.VMEM((2, requests) + cache_pool.shape[1:], BF16), dma((2, requests))],
        (page_table, cache_pool), "pages", flops=2 * requests * 2 * 256 ** 3,
    )

    hid_y, _, _ = lax.optimization_barrier((hid_y, bias, page_keys))
    hid_diag = send_tp(hid_y, 1)
    hid = (hidden_in, hid_core, hid_y, hid_diag)
    block = shape_of((tokens, width), BF16)
    queries, message, near_message = call(
        functools.partial(query_kernel, (requests, draft, page_len, long_count)),
        [block, shape_of((msg_rows, width), BF16), shape_of((tokens + META, width), BF16)],
        [SMEM] + [VMEM] * 5, [VMEM] * 3, [order],
        (cache_len, *hid, w_planes), "queries",
        flops=2 * tokens * width_all * width, nbytes=2 * width_all * width, after=(bias, page_keys),
    )
    near_asked = send_req(near_message, 1)
    queue = sorted(range(2, pages), key=lambda j: (abs(2 * j - pages), j))
    early, late = queue[:4], queue[4:]
    asked = {j: send_req(message, j) for j in early}

    key_new, value_new, accepted = call(
        key_value_kernel,
        [block, block, shape_of((tokens, 2, width), BF16)],
        [VMEM] * 6, [VMEM] * 3, [],
        (*hid, w_planes, select), "keys_values",
        flops=2 * tokens * width_all * width * 2, nbytes=2 * width_all * width * 2, after=(message,),
    )
    own, own_stats, message = call(
        functools.partial(local_kernel, (requests, draft, heads)),
        [shape_of((tokens, width), F32), shape_of((2 * requests, width), F32), shape_of((msg_rows, width), BF16)],
        [SMEM] + [VMEM] * 7, [VMEM] * 3, [],
        (cache_len, queries, key_new, value_new, bias, page_keys, page_values, message), "local_attention",
    )
    asked |= {j: send_req(message, j) for j in late}

    answer = shape_of((msg_rows, width), BF16)
    buffers = lambda n: [pltpu.VMEM((n, long_count) + cache_pool.shape[1:], BF16), dma((n, long_count))]
    near_answer, *outs = call(
        functools.partial(visiting_kernel, (page_len, draft, heads, long_count), tuple(early)),
        [shape_of((tokens + 6 * requests, width), BF16)] + [answer] * len(early),
        [VMEM] * (3 + len(early)) + [SMEM, ANY], [VMEM] * (1 + len(early)), buffers(len(early)),
        (near_asked, page_keys, page_values, *[asked[j] for j in early], page_table, cache_pool), "visitors_early",
        after=(own,),
    )
    near_got = send_req(near_answer, -1)
    answers = [send_req(out, -j) for j, out in zip(early, outs)]
    outs = call(
        functools.partial(remote_kernel, (page_len, draft, heads, long_count), tuple(late)),
        [answer] * len(late), [VMEM] * len(late) + [SMEM, ANY], [VMEM] * len(late), buffers(len(late)),
        (*[asked[j] for j in late], page_table, cache_pool), "visitors_late", after=(near_answer,),
    )
    answers += [send_req(out, -j) for j, out in zip(late, outs)]
    last = (outs[0],)

    def merge(span, msgs, name, after):
        return call(
            functools.partial(merge_kernel, (requests, draft, heads, page_len), span),
            shape_of(((span[1] - span[0]) * draft, width), BF16), [SMEM] + [VMEM] * (3 + len(msgs)), VMEM,
            [order, pltpu.VMEM((6 * requests, width), F32)],
            (cache_len, own, own_stats, near_got, *msgs), name, after=after,
        )

    def forward(attended, first, count, name, after):
        rows = count * draft
        att_y = send_tp(attended, 2)
        att_core = send_tp(attended, 1)
        att_diag = send_tp(att_y, 1)
        part = shape_of((rows, share), BF16)
        outs = call(
            functools.partial(forward_kernel, (requests, draft, page_len, first, count)),
            [part] * 5, [SMEM] + [VMEM] * 4 + [ANY] * 5 + [VMEM] + [ANY] * 2, [VMEM] * 5,
            [order, pltpu.VMEM((rows, width_all), F32), pltpu.VMEM((4, tokens, share), BF16)]
            + [pltpu.VMEM(w.shape, BF16) for w in (wout, w_up, w_down)] + [dma((7,))],
            (cache_len, attended, att_core, att_y, att_diag, *stay, gain_1, w_up, w_down), name,
            flops=2 * rows * width_all * (width_all + 2 * w_up.shape[1]), nbytes=3 * 2 * 1024 * 1024, after=after,
        )
        got = [send_tp(outs[flip], flip) for flip in (2, 3, 1)]
        return outs, [outs[0], *got, outs[4]]

    stay = tuple(pltpu.with_memory_space_constraint(a, pltpu.HBM) for a in (*hid, wout))
    merged_short = merge((long_count, requests), (), "merge_short", last)
    outs_short, parts_short = forward(merged_short, long_count, requests - long_count, "forward_short", ())
    merged_long = merge((0, long_count), answers, "merge_long", (merged_short,))
    outs_long, parts_long = forward(merged_long, 0, long_count, "forward_long", (outs_short[4],))

    x_long, x_short, stats = call(
        gather_sum_kernel,
        [shape_of((long_rows, share), F32), shape_of((tokens - long_rows, share), F32), shape_of((8, tokens), F32)],
        [VMEM] * 10, [VMEM] * 3, [], (*parts_long, *parts_short), "gather_sum",
    )
    all_stats = (stats,) + tuple(send_tp(stats, flip) for flip in (2, 3, 1))
    layer_out = call(
        functools.partial(finish_kernel, (requests, draft, page_len)),
        shape_of((tokens, share), BF16), [SMEM] + [VMEM] * 7, VMEM, [order],
        (cache_len, gain_2, x_long, x_short, *all_stats), "finish",
    )
    accepted_kv = accepted.reshape(requests, draft, 2, width)
    return (layer_out, accepted_kv)


def solution(mesh):
    placed = (
        P("req", "tp"),
        P(None, None, "tp"),
        P("tp", None),
        P(),
        P(None, "tp"),
        P("tp", None),
        P(),
        P("req", None, None, "tp"),
        P("req", None),
        P("req"),
        P("req", None),
        P("req"),
    )
    return jax.shard_map(
        shards,
        mesh=mesh,
        in_specs=placed,
        out_specs=(P("req", "tp"), P("req", None, None, "tp")),
        check_vma=False,
    )
```

```python
import functools

import jax
import jax.numpy as jnp
from jax import lax
from jax.experimental import pallas as pl
from jax.experimental.pallas import tpu as pltpu
from jax.sharding import PartitionSpec as P

HD = 64
NEG = -1e30
EPS = 1e-05
META = 16
F32 = jnp.float32
BF16 = jnp.bfloat16

VMEM = pl.BlockSpec(memory_space=pltpu.VMEM)
SMEM = pl.BlockSpec(memory_space=pltpu.SMEM)
ANY = pl.BlockSpec(memory_space=pl.ANY)


def shape_of(dims, dtype):
    return jax.ShapeDtypeStruct(dims, dtype)


def call(kernel, outs, ins, out_specs, scratch, operands, name, flops=0, nbytes=0, after=(), vmem=24):
    split = len(operands)

    def body(*refs):
        kernel(*refs[:split], *refs[split + len(after) :])

    return pl.pallas_call(
        body,
        out_shape=outs,
        in_specs=list(ins) + [ANY] * len(after),
        out_specs=out_specs,
        scratch_shapes=scratch,
        compiler_params=pltpu.CompilerParams(vmem_limit_bytes=vmem << 20),
        cost_estimate=pl.CostEstimate(flops=flops, bytes_accessed=nbytes, transcendentals=0),
        name=name,
    )(*operands, *after)


def send_req(value, by):
    size = lax.axis_size("req")
    return lax.ppermute(value, "req", [(i, (i + by) % size) for i in range(size)])


def send_tp(value, flip):
    size = lax.axis_size("tp")
    return lax.ppermute(value, "tp", [(i, i ^ flip) for i in range(size)])


def write_order(len_ref, order_ref, requests, page_len):
    flags = [(len_ref[r] > 2 * page_len).astype(jnp.int32) for r in range(requests)]
    total = sum(flags)
    before = jnp.int32(0)
    for r in range(requests):
        place = jnp.where(flags[r] > 0, before, total + r - before)
        order_ref[place] = jnp.int32(r)
        before = before + flags[r]


def split3(value):
    high = value.astype(BF16)
    rest = value - high.astype(F32)
    middle = rest.astype(BF16)
    low = (rest - middle.astype(F32)).astype(BF16)
    return high, middle, low


def dot_t(a, b):
    return lax.dot_general(a, b, (((1,), (1,)), ((), ())), preferred_element_type=F32)


def head_rows(value, heads):
    lane = lax.broadcasted_iota(jnp.int32, value.shape, 1) // HD
    zero = jnp.zeros_like(value)
    return jnp.concatenate([jnp.where(lane == h, value, zero) for h in range(heads)], axis=0)


def head_lanes(stacked, heads, rows, width):
    lane = lax.broadcasted_iota(jnp.int32, (rows, width), 1) // HD
    out = jnp.zeros((rows, width), stacked.dtype)
    for h in range(heads):
        piece = stacked[h * rows : (h + 1) * rows]
        if piece.shape[1] != width:
            piece = jnp.broadcast_to(piece[:, :1], (rows, width))
        out = jnp.where(lane == h, piece, out)
    return out


def unpick(page_len):
    row = lax.broadcasted_iota(jnp.int32, (2 * page_len, 2 * page_len), 0)
    col = lax.broadcasted_iota(jnp.int32, (2 * page_len, 2 * page_len), 1)
    source = jnp.where(row < page_len, 2 * row, 2 * (row - page_len) + 1)
    return jnp.where(source == col, 1.0, 0.0).astype(BF16)


def split_page(page, picker, page_len):
    flat = page.reshape(2 * page_len, page.shape[2])
    both = jnp.dot(picker, flat, preferred_element_type=F32).astype(BF16)
    return both[:page_len], both[page_len:]


def to_row(column):
    return jnp.transpose(jnp.broadcast_to(column, (column.shape[0], 128)))[:1]


def attend(scores, values):
    top = functools.reduce(jnp.maximum, [jnp.max(s, axis=-1, keepdims=True) for s in scores])
    weights = [jnp.exp(s - top).astype(BF16) for s in scores]
    total = sum(jnp.sum(w.astype(F32), axis=-1, keepdims=True) for w in weights)
    mixed = sum(jnp.dot(w, v, preferred_element_type=F32) for w, v in zip(weights, values))
    return mixed, top, total


def pages_kernel(table_ref, pool_ref, key_ref, value_ref, page_ref, sems):
    rows, requests, page_len = key_ref.shape[:3]
    copies = [
        pltpu.make_async_copy(pool_ref.at[table_ref[j, m]], page_ref.at[j, m], sems.at[j, m])
        for j in range(rows)
        for m in range(requests)
    ]
    for copy in copies:
        copy.start()
    picker = unpick(page_len)
    for copy in copies:
        copy.wait()
    for j in range(rows):
        for m in range(requests):
            key_ref[j, m], value_ref[j, m] = split_page(page_ref[j, m], picker, page_len)


def full_product(hid, w_ref, part):
    me = lax.axis_index("tp")
    share = hid[0].shape[1]
    total = None
    for flip, ref in enumerate(hid):
        at = pl.multiple_of((me ^ flip) * share, share)
        term = jnp.dot(ref[...], w_ref[part, pl.ds(at, share), :], preferred_element_type=F32)
        total = term if total is None else total + term
    return total


def tree_kernel(dims, accept_ref, parent_ref, bias_ref, select_ref, wide_ref):
    requests, draft = dims
    group = parent_ref.shape[1] // draft
    side = group * draft
    row = lax.broadcasted_iota(jnp.int32, (side, side), 0)
    col = lax.broadcasted_iota(jnp.int32, (side, side), 1)
    eye = jnp.where(row == col, 1.0, 0.0)
    up = []
    for g in range(requests // group):
        parent = parent_ref[pl.ds(g, 1), :]
        lane = lax.broadcasted_iota(jnp.int32, parent.shape, 1)
        target = jnp.where(parent < 0, -1, parent + (lane // draft) * draft)
        up.append((eye + jnp.where(row == target, 1.0, 0.0)).astype(BF16))
    for sweep in range(max(1, (draft - 1).bit_length())):
        up = [jnp.minimum(jnp.dot(u, u, preferred_element_type=F32), 1.0).astype(BF16) for u in up]
    row = lax.broadcasted_iota(jnp.int32, (2 * side, 2 * side), 0)
    col = lax.broadcasted_iota(jnp.int32, (2 * side, 2 * side), 1)
    fits = (row % 2 == col // side) & (row // (2 * draft) == (col % side) // draft)
    level = ((row // 2) % draft).astype(F32)
    for g in range(requests // group):
        wide = up[g].astype(F32)
        reach = jnp.transpose(wide)
        wide_ref[...] = reach
        depth = jnp.sum(wide, axis=0, keepdims=True) - 1.0
        chosen = jnp.zeros((1, side), F32)
        for i in range(group):
            r = g * group + i
            own = reach[i * draft : (i + 1) * draft, i * draft : (i + 1) * draft]
            bias_ref[pl.ds(r * draft, draft), :] = jnp.where(own > 0.5, 0.0, NEG)
            chosen += wide_ref[pl.ds(i * draft + accept_ref[r], 1), :]
        depth = jnp.concatenate([depth, depth], axis=1)
        chosen = jnp.concatenate([chosen, chosen], axis=1)
        select_ref[g] = jnp.where(fits & (depth == level), chosen, 0.0).astype(BF16)


def query_kernel(dims, len_ref, own_ref, core_ref, y_ref, diag_ref, w_ref, q_ref, out_ref, near_ref, order_ref):
    requests, draft, page_len, long_count = dims
    rows = long_count * draft
    width = q_ref.shape[1]
    write_order(len_ref, order_ref, requests, page_len)
    row = lax.broadcasted_iota(jnp.int32, (META, width), 0)
    facts = jnp.zeros((META, width), jnp.int32)
    for i in range(long_count):
        member = order_ref[i]
        length = len_ref[member]
        facts = jnp.where(row == 3 * i, member, facts)
        facts = jnp.where(row == 3 * i + 1, length // page_len, facts)
        facts = jnp.where(row == 3 * i + 2, length % page_len, facts)
    out_ref[pl.ds(rows, META)] = facts.astype(F32).astype(BF16)
    limits = jnp.zeros((META, width), jnp.int32)
    for r in range(requests):
        limits = jnp.where(row == r, jnp.clip(len_ref[r] - page_len, 0, page_len), limits)
    near_ref[pl.ds(requests * draft, META)] = limits.astype(F32).astype(BF16)
    queries = (full_product((own_ref, core_ref, y_ref, diag_ref), w_ref, 0) * 0.125).astype(BF16)
    q_ref[...] = queries
    near_ref[pl.ds(0, requests * draft)] = queries
    for i in range(long_count):
        at = pl.multiple_of(order_ref[i] * draft, draft)
        out_ref[pl.ds(i * draft, draft)] = q_ref[pl.ds(at, draft), :]


def key_value_kernel(own_ref, core_ref, y_ref, diag_ref, w_ref, select_ref, k_ref, v_ref, acc_ref):
    hid = (own_ref, core_ref, y_ref, diag_ref)
    k_ref[...] = full_product(hid, w_ref, 1).astype(BF16)
    v_ref[...] = full_product(hid, w_ref, 2).astype(BF16)
    groups, side = select_ref.shape[0], select_ref.shape[1] // 2
    for g in range(groups):
        rows = pl.ds(g * side, side)
        pairs = jnp.concatenate([k_ref[rows], v_ref[rows]], axis=0)
        path = jnp.dot(select_ref[g], pairs, preferred_element_type=F32).astype(BF16)
        acc_ref[rows] = path.reshape(side, 2, path.shape[1])


def remote_kernel(dims, page_indices, *refs, between=None):
    page_len, draft, heads, long_count = dims
    count = len(page_indices)
    msgs, table_ref, pool_ref = refs[:count], refs[count], refs[count + 1]
    outs = refs[count + 2 : 2 * count + 2]
    page_ref, sems = refs[2 * count + 2 :]
    width = heads * HD
    tokens = long_count * draft
    copies, limits = [], []
    for n, page_index in enumerate(page_indices):
        facts = msgs[n][pl.ds(tokens, META), :].astype(F32)[:, :page_len]
        for i in range(long_count):
            member = jnp.max(facts[3 * i : 3 * i + 1]).astype(jnp.int32)
            copy = pltpu.make_async_copy(
                pool_ref.at[table_ref[page_index, member]], page_ref.at[n, i], sems.at[n, i]
            )
            copy.start()
            copies.append(copy)
            length = facts[3 * i + 1 : 3 * i + 2] * page_len + facts[3 * i + 2 : 3 * i + 3]
            limits.append(length - page_index * page_len)
    picker = unpick(page_len)
    lane = lax.broadcasted_iota(jnp.int32, (heads * draft, page_len), 1).astype(F32)
    if between is not None:
        between()
    for copy in copies:
        copy.wait()
    for n in range(count):
        stats = []
        for i in range(long_count):
            stacked = head_rows(msgs[n][pl.ds(i * draft, draft), :], heads)
            keys, values = split_page(page_ref[n, i], picker, page_len)
            scores = jnp.where(lane < limits[n * long_count + i], dot_t(stacked, keys), NEG)
            mixed, top, total = attend([scores], [values])
            outs[n][pl.ds(i * draft, draft)] = head_lanes(mixed, heads, draft, width).astype(BF16)
            stats += list(split3(to_row(top))) + list(split3(to_row(total)))
        stats.append(jnp.zeros((META - len(stats), width), BF16))
        outs[n][pl.ds(tokens, META)] = jnp.concatenate([s.astype(F32) for s in stats], axis=0).astype(BF16)


def near_pages(dims, msg_ref, key_ref, value_ref, out_ref):
    draft, heads = dims
    requests, page_len, width = key_ref.shape[1:]
    tokens = requests * draft
    limits = msg_ref[pl.ds(tokens, META), :].astype(F32)[:, :page_len]
    lane = lax.broadcasted_iota(jnp.int32, (heads * draft, page_len), 1).astype(F32)
    stats = []
    for r in range(requests):
        stacked = head_rows(msg_ref[pl.ds(r * draft, draft), :], heads)
        scores = jnp.where(lane < limits[r : r + 1], dot_t(stacked, key_ref[1, r]), NEG)
        mixed, top, total = attend([scores], [value_ref[1, r]])
        out_ref[pl.ds(r * draft, draft)] = head_lanes(mixed, heads, draft, width).astype(BF16)
        stats += list(split3(to_row(top))) + list(split3(to_row(total)))
    out_ref[pl.ds(tokens, len(stats))] = jnp.concatenate([s.astype(F32) for s in stats], axis=0).astype(BF16)


def visiting_kernel(dims, page_indices, msg_ref, key_ref, value_ref, *refs):
    page_len, draft, heads, long_count = dims
    count = len(page_indices)
    near = functools.partial(near_pages, (draft, heads), msg_ref, key_ref, value_ref, refs[count + 2])
    remote_kernel(dims, page_indices, *refs[: count + 2], *refs[count + 3 :], between=near)


def local_kernel(dims, len_ref, q_ref, k_ref, v_ref, bias_ref, key_ref, value_ref, keep_ref, out_ref, stats_ref, kept_ref):
    kept_ref[...] = keep_ref[...]
    requests, draft, heads = dims
    page_len, width = key_ref.shape[2:]
    lane = lax.broadcasted_iota(jnp.int32, (heads * draft, page_len), 1)
    stats = []
    for r in range(requests):
        rows = pl.ds(r * draft, draft)
        stacked = head_rows(q_ref[rows, :], heads)
        bias = jnp.concatenate([bias_ref[rows, :]] * heads, axis=0)
        mixed, top, total = attend(
            [jnp.where(lane < len_ref[r], dot_t(stacked, key_ref[0, r]), NEG), dot_t(stacked, k_ref[rows, :]) + bias],
            [value_ref[0, r], v_ref[rows, :]],
        )
        out_ref[rows] = head_lanes(mixed, heads, draft, width)
        stats += [to_row(top), to_row(total)]
    stats_ref[...] = jnp.concatenate(stats, axis=0)


def merge_kernel(dims, span, len_ref, own_ref, stats_ref, near_ref, *refs):
    requests, draft, heads, page_len = dims
    width = heads * HD
    msgs, out_ref, order_ref, facts_ref = refs[:-3], refs[-3], refs[-2], refs[-1]
    write_order(len_ref, order_ref, requests, page_len)
    tokens = requests * draft
    facts_ref[...] = near_ref[pl.ds(tokens, 6 * requests), :].astype(F32)
    far = [ref[pl.ds(ref.shape[0] - META, META), :].astype(F32) for ref in msgs]
    factors = []
    for i, p in enumerate(range(*span)):
        r = order_ref[p]
        near = [facts_ref[pl.ds(6 * r + k, 1), :] for k in range(6)]
        tops = [stats_ref[pl.ds(2 * r, 1), :], near[0] + near[1] + near[2]]
        totals = [stats_ref[pl.ds(2 * r + 1, 1), :], near[3] + near[4] + near[5]]
        for f in far:
            part = [f[6 * i + k : 6 * i + k + 1] for k in range(6)]
            tops.append(part[0] + part[1] + part[2])
            totals.append(part[3] + part[4] + part[5])
        best = functools.reduce(jnp.maximum, tops)
        scales = [jnp.exp(t - best) for t in tops]
        denom = sum(s * t for s, t in zip(scales, totals))
        factors += [s / denom for s in scales]
    each = 2 + len(far)
    factors.append(jnp.zeros((128 - len(factors), width), F32))
    columns = jnp.transpose(jnp.concatenate(factors, axis=0))
    for i, p in enumerate(range(*span)):
        rows = pl.ds(pl.multiple_of(order_ref[p] * draft, draft), draft)
        parts = [own_ref[rows, :], near_ref[rows, :].astype(F32)]
        parts += [ref[pl.ds(i * draft, draft), :].astype(F32) for ref in msgs]
        out = None
        for j, part in enumerate(parts):
            c = each * i + j
            term = part * head_lanes(columns[:, c : c + 1], heads, draft, width)
            out = term if out is None else out + term
        out_ref[pl.ds(i * draft, draft)] = out.astype(BF16)


def norm(values, sums, squares, gain, width_all):
    center = sums / width_all
    spread = squares / width_all - center * center
    return (values - center) * lax.rsqrt(spread + EPS) * gain


def forward_kernel(dims, len_ref, *refs):
    requests, draft, page_len, first, count = dims
    att, hid = refs[0:4], refs[4:8]
    wout, (gain_ref, up_ref, down_ref) = refs[8:12], refs[12:15]
    parts, normed_ref = refs[15:19], refs[19]
    order_ref, z_ref, hid_v, wout_v, up_v, down_v, sems = refs[20:]
    pairs = [(hid[k], hid_v.at[k]) for k in range(4)] + [(wout[k], wout_v.at[k]) for k in range(4)]
    pairs += [(up_ref, up_v), (down_ref, down_v)]
    copies = [pltpu.make_async_copy(src, dst, sems.at[n]) for n, (src, dst) in enumerate(pairs)]
    for copy in copies:
        copy.start()
    me = lax.axis_index("tp")
    share = hid[0].shape[1]
    width_all = z_ref.shape[1]
    write_order(len_ref, order_ref, requests, page_len)
    for copy in copies[:4]:
        copy.wait()
    for p in range(count):
        rows = pl.ds(pl.multiple_of(order_ref[first + p] * draft, draft), draft)
        for flip in range(4):
            at = pl.ds(pl.multiple_of((me ^ flip) * share, share), share)
            z_ref[pl.ds(p * draft, draft), at] = hid_v[flip, rows, :].astype(F32)
    for copy in copies[4:8]:
        copy.wait()
    branch = None
    for flip in range(4):
        term = jnp.dot(att[flip][...], wout_v[flip], preferred_element_type=F32)
        branch = term if branch is None else branch + term
    z = z_ref[...] + branch
    sums = jnp.sum(z, axis=-1, keepdims=True)
    squares = jnp.sum(z * z, axis=-1, keepdims=True)
    normed_wide = norm(z, sums, squares, gain_ref[...], width_all)
    normed = normed_wide.astype(BF16)
    z_ref[...] = normed_wide
    normed_ref[...] = z_ref[:, pl.ds(pl.multiple_of(me * share, share), share)].astype(BF16)
    copies[8].wait()
    inner = jnp.dot(normed, up_v[...], preferred_element_type=F32)
    inner = (0.5 * inner * (1.0 + lax.erf(inner * (0.5 ** 0.5)))).astype(BF16)
    copies[9].wait()
    for flip in range(4):
        at = pl.ds(pl.multiple_of((me ^ flip) * share, share), share)
        parts[flip][...] = jnp.dot(inner, down_v[:, at], preferred_element_type=F32).astype(BF16)


def gather_sum_kernel(*refs):
    groups = (len(refs) - 1) // 6
    stats_ref = refs[-1]
    place = 0
    for g in range(groups):
        a_ref, b_ref, c_ref, d_ref, normed_ref = refs[5 * g : 5 * g + 5]
        x = normed_ref[...].astype(F32) + (
            (a_ref[...].astype(F32) + b_ref[...].astype(F32)) + (c_ref[...].astype(F32) + d_ref[...].astype(F32))
        )
        refs[5 * groups + g][...] = x
        rows = x.shape[0]
        row = lax.broadcasted_iota(jnp.int32, (stats_ref.shape[0], rows), 0)
        sums = to_row(jnp.sum(x, axis=-1, keepdims=True))
        squares = to_row(jnp.sum(x * x, axis=-1, keepdims=True))
        stats_ref[:, pl.ds(place, rows)] = jnp.where(row == 0, sums, jnp.where(row == 1, squares, 0.0))
        place += rows


def finish_kernel(dims, len_ref, gain_ref, *refs):
    requests, draft, page_len = dims
    order_ref = refs[-1]
    out_ref = refs[-2]
    stats_refs = refs[-6:-2]
    me = lax.axis_index("tp")
    write_order(len_ref, order_ref, requests, page_len)
    share = out_ref.shape[1]
    gain = gain_ref[:, pl.ds(pl.multiple_of(me * share, share), share)]
    width_all = gain_ref.shape[1]
    stats = sum(ref[...] for ref in stats_refs)
    stats = jnp.transpose(jnp.concatenate([stats] * (128 // stats.shape[0]), axis=0))
    place = 0
    for x_ref in refs[:-6]:
        count = x_ref.shape[0] // draft
        own = stats[place * draft : (place + count) * draft]
        y = norm(x_ref[...], own[:, 0:1], own[:, 1:2], gain, width_all).astype(BF16)
        for p in range(count):
            rows = pl.ds(pl.multiple_of(order_ref[place] * draft, draft), draft)
            out_ref[rows, :] = y[p * draft : (p + 1) * draft]
            place += 1


def shards(hidden_in, w_qkv, w_out, first_gain, w_up, w_down, second_gain, cache_pool,
           page_table, cache_len, tree_parent, accept_node):
    tokens, share = hidden_in.shape
    cache_pool, w_up, w_down = [pltpu.with_memory_space_constraint(a, pltpu.HBM) for a in (cache_pool, w_up, w_down)]
    requests, draft = tree_parent.shape
    width = w_qkv.shape[2]
    heads = width // HD
    pages = page_table.shape[0]
    page_len = cache_pool.shape[1]
    width_all = w_qkv.shape[0]
    long_count = (requests + 3) // 4
    long_rows = long_count * draft
    msg_rows = long_rows + META
    side = 4 * draft
    dma = pltpu.SemaphoreType.DMA
    order = pltpu.SMEM((requests,), jnp.int32)

    w_planes = jnp.transpose(w_qkv, (1, 0, 2))
    gain_1 = first_gain.reshape(1, -1)
    gain_2 = second_gain.reshape(1, -1)
    parents = tree_parent.reshape(requests * draft // side, side)

    hid_y = send_tp(hidden_in, 2)
    hid_core = send_tp(hidden_in, 1)
    bias, select = call(
        functools.partial(tree_kernel, (requests, draft)),
        [shape_of((tokens, draft), F32), shape_of((requests * draft // side, 2 * side, 2 * side), BF16)],
        [SMEM, VMEM], [VMEM] * 2, [pltpu.VMEM((side, side), F32)],
        (accept_node, parents), "tree", flops=14 * 256 ** 3 * 2,
    )
    split = shape_of((2, requests, page_len, width), BF16)
    page_keys, page_values = call(
        pages_kernel, [split, split], [SMEM, ANY], [VMEM] * 2,
        [pltpu.VMEM((2, requests) + cache_pool.shape[1:], BF16), dma((2, requests))],
        (page_table, cache_pool), "pages", flops=2 * requests * 2 * 256 ** 3,
    )

    hid_y, _, _ = lax.optimization_barrier((hid_y, bias, page_keys))
    hid_diag = send_tp(hid_y, 1)
    hid = (hidden_in, hid_core, hid_y, hid_diag)
    block = shape_of((tokens, width), BF16)
    queries, message, near_message = call(
        functools.partial(query_kernel, (requests, draft, page_len, long_count)),
        [block, shape_of((msg_rows, width), BF16), shape_of((tokens + META, width), BF16)],
        [SMEM] + [VMEM] * 5, [VMEM] * 3, [order],
        (cache_len, *hid, w_planes), "queries",
        flops=2 * tokens * width_all * width, nbytes=2 * width_all * width, after=(bias, page_keys),
    )
    near_asked = send_req(near_message, 1)
    queue = sorted(range(2, pages), key=lambda j: (abs(2 * j - pages), j))
    early, late = queue, []
    asked = {j: send_req(message, j) for j in early}

    key_new, value_new, accepted = call(
        key_value_kernel,
        [block, block, shape_of((tokens, 2, width), BF16)],
        [VMEM] * 6, [VMEM] * 3, [],
        (*hid, w_planes, select), "keys_values",
        flops=2 * tokens * width_all * width * 2, nbytes=2 * width_all * width * 2, after=(message,),
    )
    own, own_stats, message = call(
        functools.partial(local_kernel, (requests, draft, heads)),
        [shape_of((tokens, width), F32), shape_of((2 * requests, width), F32), shape_of((msg_rows, width), BF16)],
        [SMEM] + [VMEM] * 7, [VMEM] * 3, [],
        (cache_len, queries, key_new, value_new, bias, page_keys, page_values, message), "local_attention",
    )
    asked |= {j: send_req(message, j) for j in late}

    answer = shape_of((msg_rows, width), BF16)
    buffers = lambda n: [pltpu.VMEM((n, long_count) + cache_pool.shape[1:], BF16), dma((n, long_count))]
    near_answer, *outs = call(
        functools.partial(visiting_kernel, (page_len, draft, heads, long_count), tuple(early)),
        [shape_of((tokens + 6 * requests, width), BF16)] + [answer] * len(early),
        [VMEM] * (3 + len(early)) + [SMEM, ANY], [VMEM] * (1 + len(early)), buffers(len(early)),
        (near_asked, page_keys, page_values, *[asked[j] for j in early], page_table, cache_pool), "visitors_early",
        after=(own,),
    )
    near_got = send_req(near_answer, -1)
    answers = [send_req(out, -j) for j, out in zip(early, outs)]
    last = (near_answer,)

    w_later, _ = lax.optimization_barrier((w_out, near_answer))
    wout_core = send_tp(w_later, 1)
    wout_y = send_tp(w_later, 2)

    def merge(span, msgs, name, after):
        return call(
            functools.partial(merge_kernel, (requests, draft, heads, page_len), span),
            shape_of(((span[1] - span[0]) * draft, width), BF16), [SMEM] + [VMEM] * (3 + len(msgs)), VMEM,
            [order, pltpu.VMEM((6 * requests, width), F32)],
            (cache_len, own, own_stats, near_got, *msgs), name, after=after,
        )

    def forward(attended, first, count, name, after):
        rows = count * draft
        att_y = send_tp(attended, 2)
        att_core = send_tp(attended, 1)
        att_diag = send_tp(att_y, 1)
        part = shape_of((rows, share), BF16)
        outs = call(
            functools.partial(forward_kernel, (requests, draft, page_len, first, count)),
            [part] * 5, [SMEM] + [VMEM] * 4 + [ANY] * 8 + [VMEM] + [ANY] * 2, [VMEM] * 5,
            [order, pltpu.VMEM((rows, width_all), F32), pltpu.VMEM((4, tokens, share), BF16)]
            + [pltpu.VMEM((4,) + w_out.shape, BF16), pltpu.VMEM(w_up.shape, BF16), pltpu.VMEM(w_down.shape, BF16), dma((10,))],
            (cache_len, attended, att_core, att_y, att_diag, *stay, gain_1, w_up, w_down), name,
            flops=2 * rows * width_all * (width_all + 2 * w_up.shape[1]), nbytes=3 * 2 * 1024 * 1024, after=after,
        )
        got = [send_tp(outs[flip], flip) for flip in (2, 3, 1)]
        return outs, [outs[0], *got, outs[4]]

    wout_y_later, _ = lax.optimization_barrier((wout_y, near_got))
    wout = (w_out, wout_core, wout_y, send_tp(wout_y_later, 1))
    stay = tuple(pltpu.with_memory_space_constraint(a, pltpu.HBM) for a in (*hid, *wout))
    merged_short = merge((long_count, requests), (), "merge_short", last + tuple(answers) + (wout_y,))
    outs_short, parts_short = forward(merged_short, long_count, requests - long_count, "forward_short", ())
    merged_long = merge((0, long_count), answers, "merge_long", (merged_short,))
    outs_long, parts_long = forward(merged_long, 0, long_count, "forward_long", (outs_short[4],))

    x_long, x_short, stats = call(
        gather_sum_kernel,
        [shape_of((long_rows, share), F32), shape_of((tokens - long_rows, share), F32), shape_of((8, tokens), F32)],
        [VMEM] * 10, [VMEM] * 3, [], (*parts_long, *parts_short), "gather_sum",
    )
    all_stats = (stats,) + tuple(send_tp(stats, flip) for flip in (2, 3, 1))
    layer_out = call(
        functools.partial(finish_kernel, (requests, draft, page_len)),
        shape_of((tokens, share), BF16), [SMEM] + [VMEM] * 7, VMEM, [order],
        (cache_len, gain_2, x_long, x_short, *all_stats), "finish",
    )
    accepted_kv = accepted.reshape(requests, draft, 2, width)
    return (layer_out, accepted_kv)


def solution(mesh):
    placed = (
        P("req", "tp"),
        P(None, None, "tp"),
        P("tp", None),
        P(),
        P(None, "tp"),
        P("tp", None),
        P(),
        P("req", None, None, "tp"),
        P("req", None),
        P("req"),
        P("req", None),
        P("req"),
    )
    return jax.shard_map(
        shards,
        mesh=mesh,
        in_specs=placed,
        out_specs=(P("req", "tp"), P("req", None, None, "tp")),
        check_vma=False,
    )
```

```python
import functools

import jax
import jax.numpy as jnp
from jax import lax
from jax.experimental import pallas as pl
from jax.experimental.pallas import tpu as pltpu
from jax.sharding import PartitionSpec as P

HD = 64
NEG = -1e30
EPS = 1e-05
META = 16
F32 = jnp.float32
BF16 = jnp.bfloat16

VMEM = pl.BlockSpec(memory_space=pltpu.VMEM)
SMEM = pl.BlockSpec(memory_space=pltpu.SMEM)
ANY = pl.BlockSpec(memory_space=pl.ANY)


def shape_of(dims, dtype):
    return jax.ShapeDtypeStruct(dims, dtype)


def call(kernel, outs, ins, out_specs, scratch, operands, name, flops=0, nbytes=0, after=(), vmem=24):
    split = len(operands)

    def body(*refs):
        kernel(*refs[:split], *refs[split + len(after) :])

    return pl.pallas_call(
        body,
        out_shape=outs,
        in_specs=list(ins) + [ANY] * len(after),
        out_specs=out_specs,
        scratch_shapes=scratch,
        compiler_params=pltpu.CompilerParams(vmem_limit_bytes=vmem << 20),
        cost_estimate=pl.CostEstimate(flops=flops, bytes_accessed=nbytes, transcendentals=0),
        name=name,
    )(*operands, *after)


def send_req(value, by):
    size = lax.axis_size("req")
    return lax.ppermute(value, "req", [(i, (i + by) % size) for i in range(size)])


def send_tp(value, flip):
    size = lax.axis_size("tp")
    return lax.ppermute(value, "tp", [(i, i ^ flip) for i in range(size)])


def write_order(len_ref, order_ref, requests, page_len):
    flags = [(len_ref[r] > 2 * page_len).astype(jnp.int32) for r in range(requests)]
    total = sum(flags)
    before = jnp.int32(0)
    for r in range(requests):
        place = jnp.where(flags[r] > 0, before, total + r - before)
        order_ref[place] = jnp.int32(r)
        before = before + flags[r]


def split3(value):
    high = value.astype(BF16)
    rest = value - high.astype(F32)
    middle = rest.astype(BF16)
    low = (rest - middle.astype(F32)).astype(BF16)
    return high, middle, low


def dot_t(a, b):
    return lax.dot_general(a, b, (((1,), (1,)), ((), ())), preferred_element_type=F32)


def head_rows(value, heads):
    lane = lax.broadcasted_iota(jnp.int32, value.shape, 1) // HD
    zero = jnp.zeros_like(value)
    return jnp.concatenate([jnp.where(lane == h, value, zero) for h in range(heads)], axis=0)


def head_lanes(stacked, heads, rows, width):
    lane = lax.broadcasted_iota(jnp.int32, (rows, width), 1) // HD
    out = jnp.zeros((rows, width), stacked.dtype)
    for h in range(heads):
        piece = stacked[h * rows : (h + 1) * rows]
        if piece.shape[1] != width:
            piece = jnp.broadcast_to(piece[:, :1], (rows, width))
        out = jnp.where(lane == h, piece, out)
    return out


def unpick(page_len):
    row = lax.broadcasted_iota(jnp.int32, (2 * page_len, 2 * page_len), 0)
    col = lax.broadcasted_iota(jnp.int32, (2 * page_len, 2 * page_len), 1)
    source = jnp.where(row < page_len, 2 * row, 2 * (row - page_len) + 1)
    return jnp.where(source == col, 1.0, 0.0).astype(BF16)


def split_page(page, picker, page_len):
    flat = page.reshape(2 * page_len, page.shape[2])
    both = jnp.dot(picker, flat, preferred_element_type=F32).astype(BF16)
    return both[:page_len], both[page_len:]


def to_row(column):
    return jnp.transpose(jnp.broadcast_to(column, (column.shape[0], 128)))[:1]


def attend(scores, values):
    top = functools.reduce(jnp.maximum, [jnp.max(s, axis=-1, keepdims=True) for s in scores])
    weights = [jnp.exp(s - top).astype(BF16) for s in scores]
    total = sum(jnp.sum(w.astype(F32), axis=-1, keepdims=True) for w in weights)
    mixed = sum(jnp.dot(w, v, preferred_element_type=F32) for w, v in zip(weights, values))
    return mixed, top, total


def pages_kernel(table_ref, pool_ref, key_ref, value_ref, page_ref, sems):
    rows, requests, page_len = key_ref.shape[:3]
    copies = [
        pltpu.make_async_copy(pool_ref.at[table_ref[j, m]], page_ref.at[j, m], sems.at[j, m])
        for j in range(rows)
        for m in range(requests)
    ]
    for copy in copies:
        copy.start()
    picker = unpick(page_len)
    for copy in copies:
        copy.wait()
    for j in range(rows):
        for m in range(requests):
            key_ref[j, m], value_ref[j, m] = split_page(page_ref[j, m], picker, page_len)


def full_product(hid, w_ref, part):
    me = lax.axis_index("tp")
    share = hid[0].shape[1]
    total = None
    for flip, ref in enumerate(hid):
        at = pl.multiple_of((me ^ flip) * share, share)
        term = jnp.dot(ref[...], w_ref[part, pl.ds(at, share), :], preferred_element_type=F32)
        total = term if total is None else total + term
    return total


def tree_kernel(dims, accept_ref, parent_ref, bias_ref, select_ref, wide_ref):
    requests, draft = dims
    group = parent_ref.shape[1] // draft
    side = group * draft
    row = lax.broadcasted_iota(jnp.int32, (side, side), 0)
    col = lax.broadcasted_iota(jnp.int32, (side, side), 1)
    eye = jnp.where(row == col, 1.0, 0.0)
    up = []
    for g in range(requests // group):
        parent = parent_ref[pl.ds(g, 1), :]
        lane = lax.broadcasted_iota(jnp.int32, parent.shape, 1)
        target = jnp.where(parent < 0, -1, parent + (lane // draft) * draft)
        up.append((eye + jnp.where(row == target, 1.0, 0.0)).astype(BF16))
    for sweep in range(max(1, (draft - 1).bit_length())):
        up = [jnp.minimum(jnp.dot(u, u, preferred_element_type=F32), 1.0).astype(BF16) for u in up]
    row = lax.broadcasted_iota(jnp.int32, (2 * side, 2 * side), 0)
    col = lax.broadcasted_iota(jnp.int32, (2 * side, 2 * side), 1)
    fits = (row % 2 == col // side) & (row // (2 * draft) == (col % side) // draft)
    level = ((row // 2) % draft).astype(F32)
    for g in range(requests // group):
        wide = up[g].astype(F32)
        reach = jnp.transpose(wide)
        wide_ref[...] = reach
        depth = jnp.sum(wide, axis=0, keepdims=True) - 1.0
        chosen = jnp.zeros((1, side), F32)
        for i in range(group):
            r = g * group + i
            own = reach[i * draft : (i + 1) * draft, i * draft : (i + 1) * draft]
            bias_ref[pl.ds(r * draft, draft), :] = jnp.where(own > 0.5, 0.0, NEG)
            chosen += wide_ref[pl.ds(i * draft + accept_ref[r], 1), :]
        depth = jnp.concatenate([depth, depth], axis=1)
        chosen = jnp.concatenate([chosen, chosen], axis=1)
        select_ref[g] = jnp.where(fits & (depth == level), chosen, 0.0).astype(BF16)


def query_kernel(dims, len_ref, own_ref, core_ref, y_ref, diag_ref, w_ref, q_ref, out_ref, near_ref, order_ref):
    requests, draft, page_len, long_count = dims
    rows = long_count * draft
    width = q_ref.shape[1]
    write_order(len_ref, order_ref, requests, page_len)
    row = lax.broadcasted_iota(jnp.int32, (META, width), 0)
    facts = jnp.zeros((META, width), jnp.int32)
    for i in range(long_count):
        member = order_ref[i]
        length = len_ref[member]
        facts = jnp.where(row == 3 * i, member, facts)
        facts = jnp.where(row == 3 * i + 1, length // page_len, facts)
        facts = jnp.where(row == 3 * i + 2, length % page_len, facts)
    out_ref[pl.ds(rows, META)] = facts.astype(F32).astype(BF16)
    limits = jnp.zeros((META, width), jnp.int32)
    for r in range(requests):
        limits = jnp.where(row == r, jnp.clip(len_ref[r] - page_len, 0, page_len), limits)
    near_ref[pl.ds(requests * draft, META)] = limits.astype(F32).astype(BF16)
    queries = (full_product((own_ref, core_ref, y_ref, diag_ref), w_ref, 0) * 0.125).astype(BF16)
    q_ref[...] = queries
    near_ref[pl.ds(0, requests * draft)] = queries
    for i in range(long_count):
        at = pl.multiple_of(order_ref[i] * draft, draft)
        out_ref[pl.ds(i * draft, draft)] = q_ref[pl.ds(at, draft), :]


def key_value_kernel(own_ref, core_ref, y_ref, diag_ref, w_ref, select_ref, k_ref, v_ref, acc_ref):
    hid = (own_ref, core_ref, y_ref, diag_ref)
    k_ref[...] = full_product(hid, w_ref, 1).astype(BF16)
    v_ref[...] = full_product(hid, w_ref, 2).astype(BF16)
    groups, side = select_ref.shape[0], select_ref.shape[1] // 2
    for g in range(groups):
        rows = pl.ds(g * side, side)
        pairs = jnp.concatenate([k_ref[rows], v_ref[rows]], axis=0)
        path = jnp.dot(select_ref[g], pairs, preferred_element_type=F32).astype(BF16)
        acc_ref[rows] = path.reshape(side, 2, path.shape[1])


def remote_kernel(dims, page_indices, *refs, between=None):
    page_len, draft, heads, long_count = dims
    count = len(page_indices)
    msgs, table_ref, pool_ref = refs[:count], refs[count], refs[count + 1]
    outs = refs[count + 2 : 2 * count + 2]
    page_ref, sems = refs[2 * count + 2 :]
    width = heads * HD
    tokens = long_count * draft
    copies, limits = [], []
    for n, page_index in enumerate(page_indices):
        facts = msgs[n][pl.ds(tokens, META), :].astype(F32)[:, :page_len]
        for i in range(long_count):
            member = jnp.max(facts[3 * i : 3 * i + 1]).astype(jnp.int32)
            copy = pltpu.make_async_copy(
                pool_ref.at[table_ref[page_index, member]], page_ref.at[n, i], sems.at[n, i]
            )
            copy.start()
            copies.append(copy)
            length = facts[3 * i + 1 : 3 * i + 2] * page_len + facts[3 * i + 2 : 3 * i + 3]
            limits.append(length - page_index * page_len)
    picker = unpick(page_len)
    lane = lax.broadcasted_iota(jnp.int32, (heads * draft, page_len), 1).astype(F32)
    if between is not None:
        between()
    for copy in copies:
        copy.wait()
    for n in range(count):
        stats = []
        for i in range(long_count):
            stacked = head_rows(msgs[n][pl.ds(i * draft, draft), :], heads)
            keys, values = split_page(page_ref[n, i], picker, page_len)
            scores = jnp.where(lane < limits[n * long_count + i], dot_t(stacked, keys), NEG)
            mixed, top, total = attend([scores], [values])
            outs[n][pl.ds(i * draft, draft)] = head_lanes(mixed, heads, draft, width).astype(BF16)
            stats += list(split3(to_row(top))) + list(split3(to_row(total)))
        stats.append(jnp.zeros((META - len(stats), width), BF16))
        outs[n][pl.ds(tokens, META)] = jnp.concatenate([s.astype(F32) for s in stats], axis=0).astype(BF16)


def near_pages(dims, msg_ref, key_ref, value_ref, out_ref):
    draft, heads = dims
    requests, page_len, width = key_ref.shape[1:]
    tokens = requests * draft
    limits = msg_ref[pl.ds(tokens, META), :].astype(F32)[:, :page_len]
    lane = lax.broadcasted_iota(jnp.int32, (heads * draft, page_len), 1).astype(F32)
    stats = []
    for r in range(requests):
        stacked = head_rows(msg_ref[pl.ds(r * draft, draft), :], heads)
        scores = jnp.where(lane < limits[r : r + 1], dot_t(stacked, key_ref[1, r]), NEG)
        mixed, top, total = attend([scores], [value_ref[1, r]])
        out_ref[pl.ds(r * draft, draft)] = head_lanes(mixed, heads, draft, width).astype(BF16)
        stats += list(split3(to_row(top))) + list(split3(to_row(total)))
    out_ref[pl.ds(tokens, len(stats))] = jnp.concatenate([s.astype(F32) for s in stats], axis=0).astype(BF16)


def visiting_kernel(dims, page_indices, msg_ref, key_ref, value_ref, *refs):
    page_len, draft, heads, long_count = dims
    count = len(page_indices)
    near = functools.partial(near_pages, (draft, heads), msg_ref, key_ref, value_ref, refs[count + 2])
    remote_kernel(dims, page_indices, *refs[: count + 2], *refs[count + 3 :], between=near)


def local_kernel(dims, len_ref, q_ref, k_ref, v_ref, bias_ref, key_ref, value_ref, keep_ref, out_ref, stats_ref, kept_ref):
    kept_ref[...] = keep_ref[...]
    requests, draft, heads = dims
    page_len, width = key_ref.shape[2:]
    lane = lax.broadcasted_iota(jnp.int32, (heads * draft, page_len), 1)
    stats = []
    for r in range(requests):
        rows = pl.ds(r * draft, draft)
        stacked = head_rows(q_ref[rows, :], heads)
        bias = jnp.concatenate([bias_ref[rows, :]] * heads, axis=0)
        mixed, top, total = attend(
            [jnp.where(lane < len_ref[r], dot_t(stacked, key_ref[0, r]), NEG), dot_t(stacked, k_ref[rows, :]) + bias],
            [value_ref[0, r], v_ref[rows, :]],
        )
        out_ref[rows] = head_lanes(mixed, heads, draft, width)
        stats += [to_row(top), to_row(total)]
    stats_ref[...] = jnp.concatenate(stats, axis=0)


def merge_kernel(dims, len_ref, own_ref, stats_ref, near_ref, *refs):
    requests, draft, heads, page_len, long_count = dims
    width = heads * HD
    msgs, out_ref, order_ref, facts_ref = refs[:-3], refs[-3], refs[-2], refs[-1]
    write_order(len_ref, order_ref, requests, page_len)
    tokens = requests * draft
    facts_ref[...] = near_ref[pl.ds(tokens, 6 * requests), :].astype(F32)
    far = [ref[pl.ds(ref.shape[0] - META, META), :].astype(F32) for ref in msgs]
    factors, begins = [], []
    for p in range(requests):
        r = order_ref[p]
        near = [facts_ref[pl.ds(6 * r + k, 1), :] for k in range(6)]
        tops = [stats_ref[pl.ds(2 * r, 1), :], near[0] + near[1] + near[2]]
        totals = [stats_ref[pl.ds(2 * r + 1, 1), :], near[3] + near[4] + near[5]]
        for f in far if p < long_count else ():
            part = [f[6 * p + k : 6 * p + k + 1] for k in range(6)]
            tops.append(part[0] + part[1] + part[2])
            totals.append(part[3] + part[4] + part[5])
        best = functools.reduce(jnp.maximum, tops)
        scales = [jnp.exp(t - best) for t in tops]
        denom = sum(s * t for s, t in zip(scales, totals))
        begins.append(len(factors))
        factors += [s / denom for s in scales]
    factors.append(jnp.zeros((128 - len(factors), width), F32))
    columns = jnp.transpose(jnp.concatenate(factors, axis=0))
    for p in range(requests):
        rows = pl.ds(pl.multiple_of(order_ref[p] * draft, draft), draft)
        parts = [own_ref[rows, :], near_ref[rows, :].astype(F32)]
        parts += [ref[pl.ds(p * draft, draft), :].astype(F32) for ref in (msgs if p < long_count else ())]
        out = None
        for j, part in enumerate(parts):
            c = begins[p] + j
            term = part * head_lanes(columns[:, c : c + 1], heads, draft, width)
            out = term if out is None else out + term
        out_ref[pl.ds(p * draft, draft)] = out.astype(BF16)


def norm(values, sums, squares, gain, width_all):
    center = sums / width_all
    spread = squares / width_all - center * center
    return (values - center) * lax.rsqrt(spread + EPS) * gain


def forward_kernel(dims, len_ref, *refs):
    requests, draft, page_len, first, count = dims
    att, hid = refs[0:4], refs[4:8]
    wout, (gain_ref, up_ref, down_ref) = refs[8:12], refs[12:15]
    parts, normed_ref = refs[15:19], refs[19]
    order_ref, z_ref = refs[20:]
    me = lax.axis_index("tp")
    share = hid[0].shape[1]
    width_all = z_ref.shape[1]
    write_order(len_ref, order_ref, requests, page_len)
    for p in range(count):
        rows = pl.ds(pl.multiple_of(order_ref[first + p] * draft, draft), draft)
        for flip in range(4):
            at = pl.ds(pl.multiple_of((me ^ flip) * share, share), share)
            z_ref[pl.ds(p * draft, draft), at] = hid[flip][rows, :].astype(F32)
    branch = None
    for flip in range(4):
        term = jnp.dot(att[flip][pl.ds(first * draft, count * draft)], wout[flip][...], preferred_element_type=F32)
        branch = term if branch is None else branch + term
    z = z_ref[...] + branch
    sums = jnp.sum(z, axis=-1, keepdims=True)
    squares = jnp.sum(z * z, axis=-1, keepdims=True)
    normed_wide = norm(z, sums, squares, gain_ref[...], width_all)
    normed = normed_wide.astype(BF16)
    z_ref[...] = normed_wide
    normed_ref[...] = z_ref[:, pl.ds(pl.multiple_of(me * share, share), share)].astype(BF16)
    inner = jnp.dot(normed, up_ref[...], preferred_element_type=F32)
    inner = (0.5 * inner * (1.0 + lax.erf(inner * (0.5 ** 0.5)))).astype(BF16)
    for flip in range(4):
        at = pl.ds(pl.multiple_of((me ^ flip) * share, share), share)
        parts[flip][...] = jnp.dot(inner, down_ref[:, at], preferred_element_type=F32).astype(BF16)


def gather_sum_kernel(*refs):
    groups = (len(refs) - 1) // 6
    stats_ref = refs[-1]
    place = 0
    for g in range(groups):
        a_ref, b_ref, c_ref, d_ref, normed_ref = refs[5 * g : 5 * g + 5]
        x = normed_ref[...].astype(F32) + (
            (a_ref[...].astype(F32) + b_ref[...].astype(F32)) + (c_ref[...].astype(F32) + d_ref[...].astype(F32))
        )
        refs[5 * groups + g][...] = x
        rows = x.shape[0]
        row = lax.broadcasted_iota(jnp.int32, (stats_ref.shape[0], rows), 0)
        sums = to_row(jnp.sum(x, axis=-1, keepdims=True))
        squares = to_row(jnp.sum(x * x, axis=-1, keepdims=True))
        stats_ref[:, pl.ds(place, rows)] = jnp.where(row == 0, sums, jnp.where(row == 1, squares, 0.0))
        place += rows


def finish_kernel(dims, len_ref, gain_ref, *refs):
    requests, draft, page_len = dims
    order_ref = refs[-1]
    out_ref = refs[-2]
    stats_refs = refs[-6:-2]
    me = lax.axis_index("tp")
    write_order(len_ref, order_ref, requests, page_len)
    share = out_ref.shape[1]
    gain = gain_ref[:, pl.ds(pl.multiple_of(me * share, share), share)]
    width_all = gain_ref.shape[1]
    stats = sum(ref[...] for ref in stats_refs)
    stats = jnp.transpose(jnp.concatenate([stats] * (128 // stats.shape[0]), axis=0))
    place = 0
    for x_ref in refs[:-6]:
        count = x_ref.shape[0] // draft
        own = stats[place * draft : (place + count) * draft]
        y = norm(x_ref[...], own[:, 0:1], own[:, 1:2], gain, width_all).astype(BF16)
        for p in range(count):
            rows = pl.ds(pl.multiple_of(order_ref[place] * draft, draft), draft)
            out_ref[rows, :] = y[p * draft : (p + 1) * draft]
            place += 1


def shards(hidden_in, w_qkv, w_out, first_gain, w_up, w_down, second_gain, cache_pool,
           page_table, cache_len, tree_parent, accept_node):
    tokens, share = hidden_in.shape
    cache_pool = pltpu.with_memory_space_constraint(cache_pool, pltpu.HBM)
    requests, draft = tree_parent.shape
    width = w_qkv.shape[2]
    heads = width // HD
    pages = page_table.shape[0]
    page_len = cache_pool.shape[1]
    width_all = w_qkv.shape[0]
    long_count = (requests + 3) // 4
    long_rows = long_count * draft
    msg_rows = long_rows + META
    side = 4 * draft
    dma = pltpu.SemaphoreType.DMA
    order = pltpu.SMEM((requests,), jnp.int32)

    w_planes = jnp.transpose(w_qkv, (1, 0, 2))
    gain_1 = first_gain.reshape(1, -1)
    gain_2 = second_gain.reshape(1, -1)
    parents = tree_parent.reshape(requests * draft // side, side)

    hid_y = send_tp(hidden_in, 2)
    hid_core = send_tp(hidden_in, 1)
    bias, select = call(
        functools.partial(tree_kernel, (requests, draft)),
        [shape_of((tokens, draft), F32), shape_of((requests * draft // side, 2 * side, 2 * side), BF16)],
        [SMEM, VMEM], [VMEM] * 2, [pltpu.VMEM((side, side), F32)],
        (accept_node, parents), "tree", flops=14 * 256 ** 3 * 2,
    )
    split = shape_of((2, requests, page_len, width), BF16)
    page_keys, page_values = call(
        pages_kernel, [split, split], [SMEM, ANY], [VMEM] * 2,
        [pltpu.VMEM((2, requests) + cache_pool.shape[1:], BF16), dma((2, requests))],
        (page_table, cache_pool), "pages", flops=2 * requests * 2 * 256 ** 3,
    )

    hid_y, _, _ = lax.optimization_barrier((hid_y, bias, page_keys))
    hid_diag = send_tp(hid_y, 1)
    hid = (hidden_in, hid_core, hid_y, hid_diag)
    wout_core = send_tp(w_out, 1)
    block = shape_of((tokens, width), BF16)
    queries, message, near_message = call(
        functools.partial(query_kernel, (requests, draft, page_len, long_count)),
        [block, shape_of((msg_rows, width), BF16), shape_of((tokens + META, width), BF16)],
        [SMEM] + [VMEM] * 5, [VMEM] * 3, [order],
        (cache_len, *hid, w_planes), "queries",
        flops=2 * tokens * width_all * width, nbytes=2 * width_all * width, after=(bias, page_keys, wout_core),
    )
    near_asked = send_req(near_message, 1)
    queue = sorted(range(2, pages), key=lambda j: (abs(2 * j - pages), j))
    early, late = queue, []
    asked = {j: send_req(message, j) for j in early}

    key_new, value_new, accepted = call(
        key_value_kernel,
        [block, block, shape_of((tokens, 2, width), BF16)],
        [VMEM] * 6, [VMEM] * 3, [],
        (*hid, w_planes, select), "keys_values",
        flops=2 * tokens * width_all * width * 2, nbytes=2 * width_all * width * 2, after=(message,),
    )
    own, own_stats, message = call(
        functools.partial(local_kernel, (requests, draft, heads)),
        [shape_of((tokens, width), F32), shape_of((2 * requests, width), F32), shape_of((msg_rows, width), BF16)],
        [SMEM] + [VMEM] * 7, [VMEM] * 3, [],
        (cache_len, queries, key_new, value_new, bias, page_keys, page_values, message), "local_attention",
    )
    asked |= {j: send_req(message, j) for j in late}

    answer = shape_of((msg_rows, width), BF16)
    buffers = lambda n: [pltpu.VMEM((n, long_count) + cache_pool.shape[1:], BF16), dma((n, long_count))]
    near_answer, *outs = call(
        functools.partial(visiting_kernel, (page_len, draft, heads, long_count), tuple(early)),
        [shape_of((tokens + 6 * requests, width), BF16)] + [answer] * len(early),
        [VMEM] * (3 + len(early)) + [SMEM, ANY], [VMEM] * (1 + len(early)), buffers(len(early)),
        (near_asked, page_keys, page_values, *[asked[j] for j in early], page_table, cache_pool), "visitors_early",
        after=(own,),
    )
    near_got = send_req(near_answer, -1)
    answers = [send_req(out, -j) for j, out in zip(early, outs)]
    last = (near_answer,)

    w_later, _ = lax.optimization_barrier((w_out, near_answer))
    wout_y = send_tp(w_later, 2)

    merged = call(
        functools.partial(merge_kernel, (requests, draft, heads, page_len, long_count)),
        block, [SMEM] + [VMEM] * (3 + len(answers)), VMEM,
        [order, pltpu.VMEM((6 * requests, width), F32)],
        (cache_len, own, own_stats, near_got, *answers), "merge",
    )
    att_y = send_tp(merged, 2)
    att_core = send_tp(merged, 1)
    wout_y, _ = lax.optimization_barrier((wout_y, near_got))
    wout = (w_out, wout_core, wout_y, send_tp(wout_y, 1))
    att = (merged, att_core, att_y, send_tp(att_y, 1))

    def forward(first, count, name, after):
        rows = count * draft
        part = shape_of((rows, share), BF16)
        outs = call(
            functools.partial(forward_kernel, (requests, draft, page_len, first, count)),
            [part] * 5, [SMEM] + [VMEM] * 15, [VMEM] * 5,
            [order, pltpu.VMEM((rows, width_all), F32)],
            (cache_len, *att, *hid, *wout, gain_1, w_up, w_down), name,
            flops=2 * rows * width_all * (width_all + 2 * w_up.shape[1]), nbytes=3 * 2 * 1024 * 1024, after=after,
        )
        got = [send_tp(outs[flip], flip) for flip in (2, 3, 1)]
        return outs, [outs[0], *got, outs[4]]

    outs_short, parts_short = forward(long_count, requests - long_count, "forward_short", ())
    outs_long, parts_long = forward(0, long_count, "forward_long", (outs_short[4],))

    x_long, x_short, stats = call(
        gather_sum_kernel,
        [shape_of((long_rows, share), F32), shape_of((tokens - long_rows, share), F32), shape_of((8, tokens), F32)],
        [VMEM] * 10, [VMEM] * 3, [], (*parts_long, *parts_short), "gather_sum",
    )
    all_stats = (stats,) + tuple(send_tp(stats, flip) for flip in (2, 3, 1))
    layer_out = call(
        functools.partial(finish_kernel, (requests, draft, page_len)),
        shape_of((tokens, share), BF16), [SMEM] + [VMEM] * 7, VMEM, [order],
        (cache_len, gain_2, x_long, x_short, *all_stats), "finish",
    )
    accepted_kv = accepted.reshape(requests, draft, 2, width)
    return (layer_out, accepted_kv)


def solution(mesh):
    placed = (
        P("req", "tp"),
        P(None, None, "tp"),
        P("tp", None),
        P(),
        P(None, "tp"),
        P("tp", None),
        P(),
        P("req", None, None, "tp"),
        P("req", None),
        P("req"),
        P("req", None),
        P("req"),
    )
    return jax.shard_map(
        shards,
        mesh=mesh,
        in_specs=placed,
        out_specs=(P("req", "tp"), P("req", None, None, "tp")),
        check_vma=False,
    )
```

```python
import functools

import jax
import jax.numpy as jnp
from jax import lax
from jax.experimental import pallas as pl
from jax.experimental.pallas import tpu as pltpu
from jax.sharding import PartitionSpec as P

HD = 64
NEG = -1e30
EPS = 1e-05
META = 16
F32 = jnp.float32
BF16 = jnp.bfloat16

VMEM = pl.BlockSpec(memory_space=pltpu.VMEM)
SMEM = pl.BlockSpec(memory_space=pltpu.SMEM)
ANY = pl.BlockSpec(memory_space=pl.ANY)


def shape_of(dims, dtype):
    return jax.ShapeDtypeStruct(dims, dtype)


def call(kernel, outs, ins, out_specs, scratch, operands, name, flops=0, nbytes=0, after=(), vmem=24):
    split = len(operands)

    def body(*refs):
        kernel(*refs[:split], *refs[split + len(after) :])

    return pl.pallas_call(
        body,
        out_shape=outs,
        in_specs=list(ins) + [ANY] * len(after),
        out_specs=out_specs,
        scratch_shapes=scratch,
        compiler_params=pltpu.CompilerParams(vmem_limit_bytes=vmem << 20),
        cost_estimate=pl.CostEstimate(flops=flops, bytes_accessed=nbytes, transcendentals=0),
        name=name,
    )(*operands, *after)


def send_req(value, by):
    size = lax.axis_size("req")
    return lax.ppermute(value, "req", [(i, (i + by) % size) for i in range(size)])


def send_tp(value, flip):
    size = lax.axis_size("tp")
    return lax.ppermute(value, "tp", [(i, i ^ flip) for i in range(size)])


def write_order(len_ref, order_ref, requests, page_len):
    flags = [(len_ref[r] > 2 * page_len).astype(jnp.int32) for r in range(requests)]
    total = sum(flags)
    before = jnp.int32(0)
    for r in range(requests):
        place = jnp.where(flags[r] > 0, before, total + r - before)
        order_ref[place] = jnp.int32(r)
        before = before + flags[r]


def split3(value):
    high = value.astype(BF16)
    rest = value - high.astype(F32)
    middle = rest.astype(BF16)
    low = (rest - middle.astype(F32)).astype(BF16)
    return high, middle, low


def dot_t(a, b):
    return lax.dot_general(a, b, (((1,), (1,)), ((), ())), preferred_element_type=F32)


def head_rows(value, heads):
    lane = lax.broadcasted_iota(jnp.int32, value.shape, 1) // HD
    zero = jnp.zeros_like(value)
    return jnp.concatenate([jnp.where(lane == h, value, zero) for h in range(heads)], axis=0)


def head_lanes(stacked, heads, rows, width):
    lane = lax.broadcasted_iota(jnp.int32, (rows, width), 1) // HD
    out = jnp.zeros((rows, width), stacked.dtype)
    for h in range(heads):
        piece = stacked[h * rows : (h + 1) * rows]
        if piece.shape[1] != width:
            piece = jnp.broadcast_to(piece[:, :1], (rows, width))
        out = jnp.where(lane == h, piece, out)
    return out


def unpick(page_len):
    row = lax.broadcasted_iota(jnp.int32, (2 * page_len, 2 * page_len), 0)
    col = lax.broadcasted_iota(jnp.int32, (2 * page_len, 2 * page_len), 1)
    source = jnp.where(row < page_len, 2 * row, 2 * (row - page_len) + 1)
    return jnp.where(source == col, 1.0, 0.0).astype(BF16)


def split_page(page, picker, page_len):
    flat = page.reshape(2 * page_len, page.shape[2])
    both = jnp.dot(picker, flat, preferred_element_type=F32).astype(BF16)
    return both[:page_len], both[page_len:]


class Rows:
    def __init__(self, rows):
        self.lane = lax.broadcasted_iota(jnp.int32, (rows, 128), 1)
        self.table = jnp.zeros((rows, 128), F32)
        self.count = 0

    def add(self, column):
        self.table = jnp.where(self.lane == self.count, column, self.table)
        self.count += 1

    def rows(self):
        return jnp.transpose(self.table)


def to_row(column):
    return jnp.transpose(jnp.broadcast_to(column, (column.shape[0], 128)))[:1]


def attend(scores, values):
    top = functools.reduce(jnp.maximum, [jnp.max(s, axis=-1, keepdims=True) for s in scores])
    weights = [jnp.exp(s - top).astype(BF16) for s in scores]
    total = sum(jnp.sum(w.astype(F32), axis=-1, keepdims=True) for w in weights)
    mixed = sum(jnp.dot(w, v, preferred_element_type=F32) for w, v in zip(weights, values))
    return mixed, top, total


def pages_kernel(table_ref, pool_ref, key_ref, value_ref, page_ref, sems):
    rows, requests, page_len = key_ref.shape[:3]
    copies = [
        pltpu.make_async_copy(pool_ref.at[table_ref[j, m]], page_ref.at[j, m], sems.at[j, m])
        for j in range(rows)
        for m in range(requests)
    ]
    for copy in copies:
        copy.start()
    picker = unpick(page_len)
    for copy in copies:
        copy.wait()
    for j in range(rows):
        for m in range(requests):
            key_ref[j, m], value_ref[j, m] = split_page(page_ref[j, m], picker, page_len)


def full_product(hid, w_ref, part):
    me = lax.axis_index("tp")
    share = hid[0].shape[1]
    total = None
    for flip, ref in enumerate(hid):
        at = pl.multiple_of((me ^ flip) * share, share)
        term = jnp.dot(ref[...], w_ref[part, pl.ds(at, share), :], preferred_element_type=F32)
        total = term if total is None else total + term
    return total


def tree_kernel(dims, accept_ref, parent_ref, bias_ref, select_ref, wide_ref):
    requests, draft = dims
    group = parent_ref.shape[1] // draft
    side = group * draft
    row = lax.broadcasted_iota(jnp.int32, (side, side), 0)
    col = lax.broadcasted_iota(jnp.int32, (side, side), 1)
    eye = jnp.where(row == col, 1.0, 0.0)
    up = []
    for g in range(requests // group):
        parent = parent_ref[pl.ds(g, 1), :]
        lane = lax.broadcasted_iota(jnp.int32, parent.shape, 1)
        target = jnp.where(parent < 0, -1, parent + (lane // draft) * draft)
        up.append((eye + jnp.where(row == target, 1.0, 0.0)).astype(BF16))
    for sweep in range(max(1, (draft - 1).bit_length())):
        up = [jnp.minimum(jnp.dot(u, u, preferred_element_type=F32), 1.0).astype(BF16) for u in up]
    row = lax.broadcasted_iota(jnp.int32, (2 * side, 2 * side), 0)
    col = lax.broadcasted_iota(jnp.int32, (2 * side, 2 * side), 1)
    fits = (row % 2 == col // side) & (row // (2 * draft) == (col % side) // draft)
    level = ((row // 2) % draft).astype(F32)
    for g in range(requests // group):
        wide = up[g].astype(F32)
        reach = jnp.transpose(wide)
        wide_ref[...] = reach
        depth = jnp.sum(wide, axis=0, keepdims=True) - 1.0
        chosen = jnp.zeros((1, side), F32)
        for i in range(group):
            r = g * group + i
            own = reach[i * draft : (i + 1) * draft, i * draft : (i + 1) * draft]
            bias_ref[pl.ds(r * draft, draft), :] = jnp.where(own > 0.5, 0.0, NEG)
            chosen += wide_ref[pl.ds(i * draft + accept_ref[r], 1), :]
        depth = jnp.concatenate([depth, depth], axis=1)
        chosen = jnp.concatenate([chosen, chosen], axis=1)
        select_ref[g] = jnp.where(fits & (depth == level), chosen, 0.0).astype(BF16)


def query_kernel(dims, len_ref, own_ref, core_ref, y_ref, diag_ref, w_ref, q_ref, out_ref, near_ref, order_ref):
    requests, draft, page_len, long_count = dims
    rows = long_count * draft
    width = q_ref.shape[1]
    write_order(len_ref, order_ref, requests, page_len)
    row = lax.broadcasted_iota(jnp.int32, (META, width), 0)
    facts = jnp.zeros((META, width), jnp.int32)
    for i in range(long_count):
        member = order_ref[i]
        length = len_ref[member]
        facts = jnp.where(row == 3 * i, member, facts)
        facts = jnp.where(row == 3 * i + 1, length // page_len, facts)
        facts = jnp.where(row == 3 * i + 2, length % page_len, facts)
    out_ref[pl.ds(rows, META)] = facts.astype(F32).astype(BF16)
    limits = jnp.zeros((META, width), jnp.int32)
    for r in range(requests):
        limits = jnp.where(row == r, jnp.clip(len_ref[r] - page_len, 0, page_len), limits)
    near_ref[pl.ds(requests * draft, META)] = limits.astype(F32).astype(BF16)
    queries = (full_product((own_ref, core_ref, y_ref, diag_ref), w_ref, 0) * 0.125).astype(BF16)
    q_ref[...] = queries
    near_ref[pl.ds(0, requests * draft)] = queries
    for i in range(long_count):
        at = pl.multiple_of(order_ref[i] * draft, draft)
        out_ref[pl.ds(i * draft, draft)] = q_ref[pl.ds(at, draft), :]


def key_value_kernel(own_ref, core_ref, y_ref, diag_ref, w_ref, select_ref, k_ref, v_ref, acc_ref):
    hid = (own_ref, core_ref, y_ref, diag_ref)
    k_ref[...] = full_product(hid, w_ref, 1).astype(BF16)
    v_ref[...] = full_product(hid, w_ref, 2).astype(BF16)
    groups, side = select_ref.shape[0], select_ref.shape[1] // 2
    for g in range(groups):
        rows = pl.ds(g * side, side)
        pairs = jnp.concatenate([k_ref[rows], v_ref[rows]], axis=0)
        path = jnp.dot(select_ref[g], pairs, preferred_element_type=F32).astype(BF16)
        acc_ref[rows] = path.reshape(side, 2, path.shape[1])


def remote_kernel(dims, page_indices, *refs, between):
    page_len, draft, heads, long_count = dims
    count = len(page_indices)
    msgs, table_ref, pool_ref = refs[:count], refs[count], refs[count + 1]
    outs = refs[count + 2 : 2 * count + 2]
    page_ref, sems = refs[2 * count + 2 :]
    width = heads * HD
    tokens = long_count * draft
    copies, limits = [], []
    for n, page_index in enumerate(page_indices):
        facts = msgs[n][pl.ds(tokens, META), :].astype(F32)[:, :page_len]
        for i in range(long_count):
            member = jnp.max(facts[3 * i : 3 * i + 1]).astype(jnp.int32)
            copy = pltpu.make_async_copy(
                pool_ref.at[table_ref[page_index, member]], page_ref.at[n, i], sems.at[n, i]
            )
            copy.start()
            copies.append(copy)
            length = facts[3 * i + 1 : 3 * i + 2] * page_len + facts[3 * i + 2 : 3 * i + 3]
            limits.append(length - page_index * page_len)
    picker = unpick(page_len)
    lane = lax.broadcasted_iota(jnp.int32, (heads * draft, page_len), 1).astype(F32)
    table = Rows(heads * draft)
    near_stats = between()
    for copy in copies:
        copy.wait()
    for n in range(count):
        for i in range(long_count):
            stacked = head_rows(msgs[n][pl.ds(i * draft, draft), :], heads)
            keys, values = split_page(page_ref[n, i], picker, page_len)
            scores = jnp.where(lane < limits[n * long_count + i], dot_t(stacked, keys), NEG)
            mixed, top, total = attend([scores], [values])
            outs[n][pl.ds(i * draft, draft)] = head_lanes(mixed, heads, draft, width).astype(BF16)
            table.add(top)
            table.add(total)
    for column in near_stats:
        table.add(column)
    rows = table.rows()
    each = 2 * long_count
    for n in range(count):
        terms = [t.astype(F32) for k in range(each) for t in split3(rows[each * n + k : each * n + k + 1])]
        terms.append(jnp.zeros((META - len(terms), width), F32))
        outs[n][pl.ds(tokens, META)] = jnp.concatenate(terms, axis=0).astype(BF16)
    return rows[each * count :]


def near_pages(dims, msg_ref, key_ref, value_ref, out_ref):
    draft, heads = dims
    requests, page_len, width = key_ref.shape[1:]
    tokens = requests * draft
    limits = msg_ref[pl.ds(tokens, META), :].astype(F32)[:, :page_len]
    lane = lax.broadcasted_iota(jnp.int32, (heads * draft, page_len), 1).astype(F32)
    stats = []
    for r in range(requests):
        stacked = head_rows(msg_ref[pl.ds(r * draft, draft), :], heads)
        scores = jnp.where(lane < limits[r : r + 1], dot_t(stacked, key_ref[1, r]), NEG)
        mixed, top, total = attend([scores], [value_ref[1, r]])
        out_ref[pl.ds(r * draft, draft)] = head_lanes(mixed, heads, draft, width).astype(BF16)
        stats += [top, total]
    return stats


def visiting_kernel(dims, page_indices, msg_ref, key_ref, value_ref, *refs):
    page_len, draft, heads, long_count = dims
    count = len(page_indices)
    near = functools.partial(near_pages, (draft, heads), msg_ref, key_ref, value_ref, refs[count + 2])
    rows = remote_kernel(dims, page_indices, *refs[: count + 2], *refs[count + 3 :], between=near)
    requests = key_ref.shape[1]
    terms = [t.astype(F32) for k in range(2 * requests) for t in split3(rows[k : k + 1])]
    refs[count + 2][pl.ds(requests * draft, len(terms))] = jnp.concatenate(terms, axis=0).astype(BF16)


def local_kernel(dims, len_ref, q_ref, k_ref, v_ref, bias_ref, key_ref, value_ref, keep_ref, out_ref, stats_ref, kept_ref):
    kept_ref[...] = keep_ref[...]
    requests, draft, heads = dims
    page_len, width = key_ref.shape[2:]
    lane = lax.broadcasted_iota(jnp.int32, (heads * draft, page_len), 1)
    table = Rows(heads * draft)
    for r in range(requests):
        rows = pl.ds(r * draft, draft)
        stacked = head_rows(q_ref[rows, :], heads)
        bias = jnp.concatenate([bias_ref[rows, :]] * heads, axis=0)
        mixed, top, total = attend(
            [jnp.where(lane < len_ref[r], dot_t(stacked, key_ref[0, r]), NEG), dot_t(stacked, k_ref[rows, :]) + bias],
            [value_ref[0, r], v_ref[rows, :]],
        )
        out_ref[rows] = head_lanes(mixed, heads, draft, width)
        table.add(top)
        table.add(total)
    stats_ref[...] = table.rows()[: 2 * requests]


def merge_kernel(dims, len_ref, own_ref, stats_ref, near_ref, *refs):
    requests, draft, heads, page_len, long_count = dims
    width = heads * HD
    msgs, out_ref, order_ref, facts_ref = refs[:-3], refs[-3], refs[-2], refs[-1]
    write_order(len_ref, order_ref, requests, page_len)
    tokens = requests * draft
    facts_ref[...] = near_ref[pl.ds(tokens, 6 * requests), :].astype(F32)
    far = [ref[pl.ds(ref.shape[0] - META, META), :].astype(F32) for ref in msgs]
    factors, begins = [], []
    for p in range(requests):
        r = order_ref[p]
        near = [facts_ref[pl.ds(6 * r + k, 1), :] for k in range(6)]
        tops = [stats_ref[pl.ds(2 * r, 1), :], near[0] + near[1] + near[2]]
        totals = [stats_ref[pl.ds(2 * r + 1, 1), :], near[3] + near[4] + near[5]]
        for f in far if p < long_count else ():
            part = [f[6 * p + k : 6 * p + k + 1] for k in range(6)]
            tops.append(part[0] + part[1] + part[2])
            totals.append(part[3] + part[4] + part[5])
        best = functools.reduce(jnp.maximum, tops)
        scales = [jnp.exp(t - best) for t in tops]
        denom = sum(s * t for s, t in zip(scales, totals))
        begins.append(len(factors))
        factors += [s / denom for s in scales]
    factors.append(jnp.zeros((128 - len(factors), width), F32))
    columns = jnp.transpose(jnp.concatenate(factors, axis=0))
    for p in range(requests):
        rows = pl.ds(pl.multiple_of(order_ref[p] * draft, draft), draft)
        parts = [own_ref[rows, :], near_ref[rows, :].astype(F32)]
        parts += [ref[pl.ds(p * draft, draft), :].astype(F32) for ref in (msgs if p < long_count else ())]
        out = None
        for j, part in enumerate(parts):
            c = begins[p] + j
            term = part * head_lanes(columns[:, c : c + 1], heads, draft, width)
            out = term if out is None else out + term
        out_ref[pl.ds(p * draft, draft)] = out.astype(BF16)


def norm(values, sums, squares, gain, width_all):
    center = sums / width_all
    spread = squares / width_all - center * center
    return (values - center) * lax.rsqrt(spread + EPS) * gain


def forward_kernel(dims, len_ref, *refs):
    requests, draft, page_len, first, count = dims
    att, hid = refs[0:4], refs[4:8]
    wout, (gain_ref, up_ref, down_ref) = refs[8:12], refs[12:15]
    parts, normed_ref = refs[15:19], refs[19]
    order_ref, z_ref = refs[20:]
    me = lax.axis_index("tp")
    share = hid[0].shape[1]
    width_all = z_ref.shape[1]
    write_order(len_ref, order_ref, requests, page_len)
    for p in range(count):
        rows = pl.ds(pl.multiple_of(order_ref[first + p] * draft, draft), draft)
        for flip in range(4):
            at = pl.ds(pl.multiple_of((me ^ flip) * share, share), share)
            z_ref[pl.ds(p * draft, draft), at] = hid[flip][rows, :].astype(F32)
    branch = None
    for flip in range(4):
        term = jnp.dot(att[flip][pl.ds(first * draft, count * draft)], wout[flip][...], preferred_element_type=F32)
        branch = term if branch is None else branch + term
    z = z_ref[...] + branch
    sums = jnp.sum(z, axis=-1, keepdims=True)
    squares = jnp.sum(z * z, axis=-1, keepdims=True)
    normed_wide = norm(z, sums, squares, gain_ref[...], width_all)
    normed = normed_wide.astype(BF16)
    z_ref[...] = normed_wide
    normed_ref[...] = z_ref[:, pl.ds(pl.multiple_of(me * share, share), share)].astype(BF16)
    inner = jnp.dot(normed, up_ref[...], preferred_element_type=F32)
    inner = (0.5 * inner * (1.0 + lax.erf(inner * (0.5 ** 0.5)))).astype(BF16)
    for flip in range(4):
        at = pl.ds(pl.multiple_of((me ^ flip) * share, share), share)
        parts[flip][...] = jnp.dot(inner, down_ref[:, at], preferred_element_type=F32).astype(BF16)


def gather_sum_kernel(*refs):
    groups = (len(refs) - 1) // 6
    stats_ref = refs[-1]
    place = 0
    for g in range(groups):
        a_ref, b_ref, c_ref, d_ref, normed_ref = refs[5 * g : 5 * g + 5]
        x = normed_ref[...].astype(F32) + (
            (a_ref[...].astype(F32) + b_ref[...].astype(F32)) + (c_ref[...].astype(F32) + d_ref[...].astype(F32))
        )
        refs[5 * groups + g][...] = x
        rows = x.shape[0]
        row = lax.broadcasted_iota(jnp.int32, (stats_ref.shape[0], rows), 0)
        sums = to_row(jnp.sum(x, axis=-1, keepdims=True))
        squares = to_row(jnp.sum(x * x, axis=-1, keepdims=True))
        stats_ref[:, pl.ds(place, rows)] = jnp.where(row == 0, sums, jnp.where(row == 1, squares, 0.0))
        place += rows


def finish_kernel(dims, len_ref, gain_ref, *refs):
    requests, draft, page_len = dims
    order_ref = refs[-1]
    out_ref = refs[-2]
    stats_refs = refs[-6:-2]
    me = lax.axis_index("tp")
    write_order(len_ref, order_ref, requests, page_len)
    share = out_ref.shape[1]
    gain = gain_ref[:, pl.ds(pl.multiple_of(me * share, share), share)]
    width_all = gain_ref.shape[1]
    stats = sum(ref[...] for ref in stats_refs)
    stats = jnp.transpose(jnp.concatenate([stats] * (128 // stats.shape[0]), axis=0))
    place = 0
    for x_ref in refs[:-6]:
        count = x_ref.shape[0] // draft
        own = stats[place * draft : (place + count) * draft]
        y = norm(x_ref[...], own[:, 0:1], own[:, 1:2], gain, width_all).astype(BF16)
        for p in range(count):
            rows = pl.ds(pl.multiple_of(order_ref[place] * draft, draft), draft)
            out_ref[rows, :] = y[p * draft : (p + 1) * draft]
            place += 1


def shards(hidden_in, w_qkv, w_out, first_gain, w_up, w_down, second_gain, cache_pool,
           page_table, cache_len, tree_parent, accept_node):
    tokens, share = hidden_in.shape
    cache_pool = pltpu.with_memory_space_constraint(cache_pool, pltpu.HBM)
    requests, draft = tree_parent.shape
    width = w_qkv.shape[2]
    heads = width // HD
    pages = page_table.shape[0]
    page_len = cache_pool.shape[1]
    width_all = w_qkv.shape[0]
    long_count = (requests + 3) // 4
    long_rows = long_count * draft
    msg_rows = long_rows + META
    side = 4 * draft
    dma = pltpu.SemaphoreType.DMA
    order = pltpu.SMEM((requests,), jnp.int32)

    w_planes = jnp.transpose(w_qkv, (1, 0, 2))
    gain_1 = first_gain.reshape(1, -1)
    gain_2 = second_gain.reshape(1, -1)
    parents = tree_parent.reshape(requests * draft // side, side)

    hid_y = send_tp(hidden_in, 2)
    hid_core = send_tp(hidden_in, 1)
    bias, select = call(
        functools.partial(tree_kernel, (requests, draft)),
        [shape_of((tokens, draft), F32), shape_of((requests * draft // side, 2 * side, 2 * side), BF16)],
        [SMEM, VMEM], [VMEM] * 2, [pltpu.VMEM((side, side), F32)],
        (accept_node, parents), "tree", flops=14 * 256 ** 3 * 2,
    )
    split = shape_of((2, requests, page_len, width), BF16)
    page_keys, page_values = call(
        pages_kernel, [split, split], [SMEM, ANY], [VMEM] * 2,
        [pltpu.VMEM((2, requests) + cache_pool.shape[1:], BF16), dma((2, requests))],
        (page_table, cache_pool), "pages", flops=2 * requests * 2 * 256 ** 3,
    )

    hid_y, _, _ = lax.optimization_barrier((hid_y, bias, page_keys))
    hid_diag = send_tp(hid_y, 1)
    hid = (hidden_in, hid_core, hid_y, hid_diag)
    wout_core = send_tp(w_out, 1)
    block = shape_of((tokens, width), BF16)
    queries, message, near_message = call(
        functools.partial(query_kernel, (requests, draft, page_len, long_count)),
        [block, shape_of((msg_rows, width), BF16), shape_of((tokens + META, width), BF16)],
        [SMEM] + [VMEM] * 5, [VMEM] * 3, [order],
        (cache_len, *hid, w_planes), "queries",
        flops=2 * tokens * width_all * width, nbytes=2 * width_all * width, after=(bias, page_keys, wout_core),
    )
    near_asked = send_req(near_message, 1)
    queue = [j for j in (7, 6, 3, 2, 5, 4) if j < pages] + list(range(8, pages))
    early, late = queue, []
    asked = {j: send_req(message, j) for j in early}

    key_new, value_new, accepted = call(
        key_value_kernel,
        [block, block, shape_of((tokens, 2, width), BF16)],
        [VMEM] * 6, [VMEM] * 3, [],
        (*hid, w_planes, select), "keys_values",
        flops=2 * tokens * width_all * width * 2, nbytes=2 * width_all * width * 2, after=(message,),
    )
    own, own_stats, message = call(
        functools.partial(local_kernel, (requests, draft, heads)),
        [shape_of((tokens, width), F32), shape_of((2 * requests, width), F32), shape_of((msg_rows, width), BF16)],
        [SMEM] + [VMEM] * 7, [VMEM] * 3, [],
        (cache_len, queries, key_new, value_new, bias, page_keys, page_values, message), "local_attention",
    )
    asked |= {j: send_req(message, j) for j in late}

    answer = shape_of((msg_rows, width), BF16)
    buffers = lambda n: [pltpu.VMEM((n, long_count) + cache_pool.shape[1:], BF16), dma((n, long_count))]
    near_answer, *outs = call(
        functools.partial(visiting_kernel, (page_len, draft, heads, long_count), tuple(early)),
        [shape_of((tokens + 6 * requests, width), BF16)] + [answer] * len(early),
        [VMEM] * (3 + len(early)) + [SMEM, ANY], [VMEM] * (1 + len(early)), buffers(len(early)),
        (near_asked, page_keys, page_values, *[asked[j] for j in early], page_table, cache_pool), "visitors_early",
        after=(),
    )
    near_got = send_req(near_answer, -1)
    answers = [send_req(out, -j) for j, out in zip(early, outs)]
    last = (near_answer,)

    w_later, _ = lax.optimization_barrier((w_out, near_answer))
    wout_y = send_tp(w_later, 2)

    merged = call(
        functools.partial(merge_kernel, (requests, draft, heads, page_len, long_count)),
        block, [SMEM] + [VMEM] * (3 + len(answers)), VMEM,
        [order, pltpu.VMEM((6 * requests, width), F32)],
        (cache_len, own, own_stats, near_got, *answers), "merge",
    )
    att_y = send_tp(merged, 2)
    att_core = send_tp(merged, 1)
    wout_y, _ = lax.optimization_barrier((wout_y, near_got))
    wout = (w_out, wout_core, wout_y, send_tp(wout_y, 1))
    att = (merged, att_core, att_y, send_tp(att_y, 1))

    def forward(first, count, name, after):
        rows = count * draft
        part = shape_of((rows, share), BF16)
        outs = call(
            functools.partial(forward_kernel, (requests, draft, page_len, first, count)),
            [part] * 5, [SMEM] + [VMEM] * 15, [VMEM] * 5,
            [order, pltpu.VMEM((rows, width_all), F32)],
            (cache_len, *att, *hid, *wout, gain_1, w_up, w_down), name,
            flops=2 * rows * width_all * (width_all + 2 * w_up.shape[1]), nbytes=3 * 2 * 1024 * 1024, after=after,
        )
        got = [send_tp(outs[flip], flip) for flip in (2, 3, 1)]
        return outs, [outs[0], *got, outs[4]]

    outs_short, parts_short = forward(long_count, requests - long_count, "forward_short", ())
    outs_long, parts_long = forward(0, long_count, "forward_long", (outs_short[4],))

    x_long, x_short, stats = call(
        gather_sum_kernel,
        [shape_of((long_rows, share), F32), shape_of((tokens - long_rows, share), F32), shape_of((8, tokens), F32)],
        [VMEM] * 10, [VMEM] * 3, [], (*parts_long, *parts_short), "gather_sum",
    )
    all_stats = (stats,) + tuple(send_tp(stats, flip) for flip in (2, 3, 1))
    layer_out = call(
        functools.partial(finish_kernel, (requests, draft, page_len)),
        shape_of((tokens, share), BF16), [SMEM] + [VMEM] * 7, VMEM, [order],
        (cache_len, gain_2, x_long, x_short, *all_stats), "finish",
    )
    accepted_kv = accepted.reshape(requests, draft, 2, width)
    return (layer_out, accepted_kv)


def solution(mesh):
    placed = (
        P("req", "tp"),
        P(None, None, "tp"),
        P("tp", None),
        P(),
        P(None, "tp"),
        P("tp", None),
        P(),
        P("req", None, None, "tp"),
        P("req", None),
        P("req"),
        P("req", None),
        P("req"),
    )
    return jax.shard_map(
        shards,
        mesh=mesh,
        in_specs=placed,
        out_specs=(P("req", "tp"), P("req", None, None, "tp")),
        check_vma=False,
    )
```

```python
import functools

import jax
import jax.numpy as jnp
from jax import lax
from jax.experimental import pallas as pl
from jax.experimental.pallas import tpu as pltpu
from jax.sharding import PartitionSpec as P

HD = 64
NEG = -1e30
EPS = 1e-05
META = 16
F32 = jnp.float32
BF16 = jnp.bfloat16

VMEM = pl.BlockSpec(memory_space=pltpu.VMEM)
SMEM = pl.BlockSpec(memory_space=pltpu.SMEM)
ANY = pl.BlockSpec(memory_space=pl.ANY)


def shape_of(dims, dtype):
    return jax.ShapeDtypeStruct(dims, dtype)


def call(kernel, outs, ins, out_specs, scratch, operands, name, flops=0, nbytes=0, after=(), vmem=24):
    split = len(operands)

    def body(*refs):
        kernel(*refs[:split], *refs[split + len(after) :])

    return pl.pallas_call(
        body,
        out_shape=outs,
        in_specs=list(ins) + [ANY] * len(after),
        out_specs=out_specs,
        scratch_shapes=scratch,
        compiler_params=pltpu.CompilerParams(vmem_limit_bytes=vmem << 20),
        cost_estimate=pl.CostEstimate(flops=flops, bytes_accessed=nbytes, transcendentals=0),
        name=name,
    )(*operands, *after)


def send_req(value, by):
    size = lax.axis_size("req")
    return lax.ppermute(value, "req", [(i, (i + by) % size) for i in range(size)])


def send_tp(value, flip):
    size = lax.axis_size("tp")
    return lax.ppermute(value, "tp", [(i, i ^ flip) for i in range(size)])


def write_order(len_ref, order_ref, requests, page_len):
    flags = [(len_ref[r] > 2 * page_len).astype(jnp.int32) for r in range(requests)]
    total = sum(flags)
    before = jnp.int32(0)
    for r in range(requests):
        place = jnp.where(flags[r] > 0, before, total + r - before)
        order_ref[place] = jnp.int32(r)
        before = before + flags[r]


def split3(value):
    high = value.astype(BF16)
    rest = value - high.astype(F32)
    middle = rest.astype(BF16)
    low = (rest - middle.astype(F32)).astype(BF16)
    return high, middle, low


def dot_t(a, b):
    return lax.dot_general(a, b, (((1,), (1,)), ((), ())), preferred_element_type=F32)


def head_rows(value, heads):
    lane = lax.broadcasted_iota(jnp.int32, value.shape, 1) // HD
    zero = jnp.zeros_like(value)
    return jnp.concatenate([jnp.where(lane == h, value, zero) for h in range(heads)], axis=0)


def head_lanes(stacked, heads, rows, width):
    lane = lax.broadcasted_iota(jnp.int32, (rows, width), 1) // HD
    out = jnp.zeros((rows, width), stacked.dtype)
    for h in range(heads):
        piece = stacked[h * rows : (h + 1) * rows]
        if piece.shape[1] != width:
            piece = jnp.broadcast_to(piece[:, :1], (rows, width))
        out = jnp.where(lane == h, piece, out)
    return out


def unpick(page_len):
    row = lax.broadcasted_iota(jnp.int32, (2 * page_len, 2 * page_len), 0)
    col = lax.broadcasted_iota(jnp.int32, (2 * page_len, 2 * page_len), 1)
    source = jnp.where(row < page_len, 2 * row, 2 * (row - page_len) + 1)
    return jnp.where(source == col, 1.0, 0.0).astype(BF16)


def split_page(page, picker, page_len):
    flat = page.reshape(2 * page_len, page.shape[2])
    both = jnp.dot(picker, flat, preferred_element_type=F32).astype(BF16)
    return both[:page_len], both[page_len:]


class Rows:
    def __init__(self, rows):
        self.lane = lax.broadcasted_iota(jnp.int32, (rows, 128), 1)
        self.table = jnp.zeros((rows, 128), F32)
        self.count = 0

    def add(self, column):
        self.table = jnp.where(self.lane == self.count, column, self.table)
        self.count += 1

    def rows(self):
        return jnp.transpose(self.table)


def to_row(column):
    return jnp.transpose(jnp.broadcast_to(column, (column.shape[0], 128)))[:1]


def attend(scores, values):
    top = functools.reduce(jnp.maximum, [jnp.max(s, axis=-1, keepdims=True) for s in scores])
    weights = [jnp.exp(s - top).astype(BF16) for s in scores]
    total = sum(jnp.sum(w.astype(F32), axis=-1, keepdims=True) for w in weights)
    mixed = sum(jnp.dot(w, v, preferred_element_type=F32) for w, v in zip(weights, values))
    return mixed, top, total


def pages_kernel(table_ref, pool_ref, key_ref, value_ref, page_ref, sems):
    rows, requests, page_len = key_ref.shape[:3]
    copies = [
        pltpu.make_async_copy(pool_ref.at[table_ref[j, m]], page_ref.at[j, m], sems.at[j, m])
        for j in range(rows)
        for m in range(requests)
    ]
    for copy in copies:
        copy.start()
    picker = unpick(page_len)
    for copy in copies:
        copy.wait()
    for j in range(rows):
        for m in range(requests):
            key_ref[j, m], value_ref[j, m] = split_page(page_ref[j, m], picker, page_len)


def full_product(hid, w_ref, part):
    me = lax.axis_index("tp")
    share = hid[0].shape[1]
    total = None
    for flip, ref in enumerate(hid):
        at = pl.multiple_of((me ^ flip) * share, share)
        term = jnp.dot(ref[...], w_ref[part, pl.ds(at, share), :], preferred_element_type=F32)
        total = term if total is None else total + term
    return total


def tree_kernel(dims, accept_ref, parent_ref, bias_ref, select_ref, wide_ref):
    requests, draft = dims
    group = parent_ref.shape[1] // draft
    side = group * draft
    row = lax.broadcasted_iota(jnp.int32, (side, side), 0)
    col = lax.broadcasted_iota(jnp.int32, (side, side), 1)
    eye = jnp.where(row == col, 1.0, 0.0)
    up = []
    for g in range(requests // group):
        parent = parent_ref[pl.ds(g, 1), :]
        lane = lax.broadcasted_iota(jnp.int32, parent.shape, 1)
        target = jnp.where(parent < 0, -1, parent + (lane // draft) * draft)
        up.append((eye + jnp.where(row == target, 1.0, 0.0)).astype(BF16))
    for sweep in range(max(1, (draft - 1).bit_length())):
        up = [jnp.minimum(jnp.dot(u, u, preferred_element_type=F32), 1.0).astype(BF16) for u in up]
    row = lax.broadcasted_iota(jnp.int32, (2 * side, 2 * side), 0)
    col = lax.broadcasted_iota(jnp.int32, (2 * side, 2 * side), 1)
    fits = (row % 2 == col // side) & (row // (2 * draft) == (col % side) // draft)
    level = ((row // 2) % draft).astype(F32)
    for g in range(requests // group):
        wide = up[g].astype(F32)
        reach = jnp.transpose(wide)
        wide_ref[...] = reach
        depth = jnp.sum(wide, axis=0, keepdims=True) - 1.0
        chosen = jnp.zeros((1, side), F32)
        for i in range(group):
            r = g * group + i
            own = reach[i * draft : (i + 1) * draft, i * draft : (i + 1) * draft]
            bias_ref[pl.ds(r * draft, draft), :] = jnp.where(own > 0.5, 0.0, NEG)
            chosen += wide_ref[pl.ds(i * draft + accept_ref[r], 1), :]
        depth = jnp.concatenate([depth, depth], axis=1)
        chosen = jnp.concatenate([chosen, chosen], axis=1)
        select_ref[g] = jnp.where(fits & (depth == level), chosen, 0.0).astype(BF16)


def query_kernel(dims, len_ref, own_ref, core_ref, y_ref, diag_ref, w_ref, q_ref, out_ref, near_ref, order_ref):
    requests, draft, page_len, long_count = dims
    rows = long_count * draft
    width = q_ref.shape[1]
    write_order(len_ref, order_ref, requests, page_len)
    row = lax.broadcasted_iota(jnp.int32, (META, width), 0)
    facts = jnp.zeros((META, width), jnp.int32)
    for i in range(long_count):
        member = order_ref[i]
        length = len_ref[member]
        facts = jnp.where(row == 3 * i, member, facts)
        facts = jnp.where(row == 3 * i + 1, length // page_len, facts)
        facts = jnp.where(row == 3 * i + 2, length % page_len, facts)
    out_ref[pl.ds(rows, META)] = facts.astype(F32).astype(BF16)
    limits = jnp.zeros((META, width), jnp.int32)
    for r in range(requests):
        limits = jnp.where(row == r, jnp.clip(len_ref[r] - page_len, 0, page_len), limits)
    near_ref[pl.ds(requests * draft, META)] = limits.astype(F32).astype(BF16)
    queries = (full_product((own_ref, core_ref, y_ref, diag_ref), w_ref, 0) * 0.125).astype(BF16)
    q_ref[...] = queries
    near_ref[pl.ds(0, requests * draft)] = queries
    for i in range(long_count):
        at = pl.multiple_of(order_ref[i] * draft, draft)
        out_ref[pl.ds(i * draft, draft)] = q_ref[pl.ds(at, draft), :]


def key_value_kernel(own_ref, core_ref, y_ref, diag_ref, w_ref, select_ref, k_ref, v_ref, acc_ref):
    hid = (own_ref, core_ref, y_ref, diag_ref)
    k_ref[...] = full_product(hid, w_ref, 1).astype(BF16)
    v_ref[...] = full_product(hid, w_ref, 2).astype(BF16)
    groups, side = select_ref.shape[0], select_ref.shape[1] // 2
    for g in range(groups):
        rows = pl.ds(g * side, side)
        pairs = jnp.concatenate([k_ref[rows], v_ref[rows]], axis=0)
        path = jnp.dot(select_ref[g], pairs, preferred_element_type=F32).astype(BF16)
        acc_ref[rows] = path.reshape(side, 2, path.shape[1])


def remote_kernel(dims, page_indices, *refs, between):
    page_len, draft, heads, long_count = dims
    count = len(page_indices)
    msgs, table_ref, pool_ref = refs[:count], refs[count], refs[count + 1]
    outs = refs[count + 2 : 2 * count + 2]
    page_ref, sems = refs[2 * count + 2 :]
    width = heads * HD
    tokens = long_count * draft
    copies, limits = [], []
    for n, page_index in enumerate(page_indices):
        facts = msgs[n][pl.ds(tokens, META), :].astype(F32)[:, :page_len]
        for i in range(long_count):
            member = jnp.max(facts[3 * i : 3 * i + 1]).astype(jnp.int32)
            copy = pltpu.make_async_copy(
                pool_ref.at[table_ref[page_index, member]], page_ref.at[n, i], sems.at[n, i]
            )
            copy.start()
            copies.append(copy)
            length = facts[3 * i + 1 : 3 * i + 2] * page_len + facts[3 * i + 2 : 3 * i + 3]
            limits.append(length - page_index * page_len)
    picker = unpick(page_len)
    lane = lax.broadcasted_iota(jnp.int32, (heads * draft, page_len), 1).astype(F32)
    table = Rows(heads * draft)
    near_stats = between()
    for copy in copies:
        copy.wait()
    for n in range(count):
        for i in range(long_count):
            stacked = head_rows(msgs[n][pl.ds(i * draft, draft), :], heads)
            keys, values = split_page(page_ref[n, i], picker, page_len)
            scores = jnp.where(lane < limits[n * long_count + i], dot_t(stacked, keys), NEG)
            mixed, top, total = attend([scores], [values])
            outs[n][pl.ds(i * draft, draft)] = head_lanes(mixed, heads, draft, width).astype(BF16)
            table.add(top)
            table.add(total)
    for column in near_stats:
        table.add(column)
    rows = table.rows()
    each = 2 * long_count
    for n in range(count):
        terms = [t.astype(F32) for k in range(each) for t in split3(rows[each * n + k : each * n + k + 1])]
        terms.append(jnp.zeros((META - len(terms), width), F32))
        outs[n][pl.ds(tokens, META)] = jnp.concatenate(terms, axis=0).astype(BF16)
    return rows[each * count :]


def near_pages(dims, msg_ref, key_ref, value_ref, out_ref):
    draft, heads = dims
    requests, page_len, width = key_ref.shape[1:]
    tokens = requests * draft
    limits = msg_ref[pl.ds(tokens, META), :].astype(F32)[:, :page_len]
    lane = lax.broadcasted_iota(jnp.int32, (heads * draft, page_len), 1).astype(F32)
    stats = []
    for r in range(requests):
        stacked = head_rows(msg_ref[pl.ds(r * draft, draft), :], heads)
        scores = jnp.where(lane < limits[r : r + 1], dot_t(stacked, key_ref[1, r]), NEG)
        mixed, top, total = attend([scores], [value_ref[1, r]])
        out_ref[pl.ds(r * draft, draft)] = head_lanes(mixed, heads, draft, width).astype(BF16)
        stats += [top, total]
    return stats


def visiting_kernel(dims, page_indices, msg_ref, key_ref, value_ref, *refs):
    page_len, draft, heads, long_count = dims
    count = len(page_indices)
    near = functools.partial(near_pages, (draft, heads), msg_ref, key_ref, value_ref, refs[count + 2])
    rows = remote_kernel(dims, page_indices, *refs[: count + 2], *refs[count + 3 :], between=near)
    requests = key_ref.shape[1]
    terms = [t.astype(F32) for k in range(2 * requests) for t in split3(rows[k : k + 1])]
    refs[count + 2][pl.ds(requests * draft, len(terms))] = jnp.concatenate(terms, axis=0).astype(BF16)


def local_kernel(dims, len_ref, q_ref, k_ref, v_ref, bias_ref, key_ref, value_ref, keep_ref, out_ref, stats_ref, kept_ref):
    kept_ref[...] = keep_ref[...]
    requests, draft, heads = dims
    page_len, width = key_ref.shape[2:]
    lane = lax.broadcasted_iota(jnp.int32, (heads * draft, page_len), 1)
    table = Rows(heads * draft)
    for r in range(requests):
        rows = pl.ds(r * draft, draft)
        stacked = head_rows(q_ref[rows, :], heads)
        bias = jnp.concatenate([bias_ref[rows, :]] * heads, axis=0)
        mixed, top, total = attend(
            [jnp.where(lane < len_ref[r], dot_t(stacked, key_ref[0, r]), NEG), dot_t(stacked, k_ref[rows, :]) + bias],
            [value_ref[0, r], v_ref[rows, :]],
        )
        out_ref[rows] = head_lanes(mixed, heads, draft, width)
        table.add(top)
        table.add(total)
    stats_ref[...] = table.rows()[: 2 * requests]


def merge_kernel(dims, len_ref, own_ref, stats_ref, near_ref, *refs):
    requests, draft, heads, page_len, long_count = dims
    width = heads * HD
    msgs, out_ref, order_ref, facts_ref = refs[:-3], refs[-3], refs[-2], refs[-1]
    write_order(len_ref, order_ref, requests, page_len)
    tokens = requests * draft
    facts_ref[...] = near_ref[pl.ds(tokens, 6 * requests), :].astype(F32)
    far = [ref[pl.ds(ref.shape[0] - META, META), :].astype(F32) for ref in msgs]
    factors, begins = [], []
    for p in range(requests):
        r = order_ref[p]
        near = [facts_ref[pl.ds(6 * r + k, 1), :] for k in range(6)]
        tops = [stats_ref[pl.ds(2 * r, 1), :], near[0] + near[1] + near[2]]
        totals = [stats_ref[pl.ds(2 * r + 1, 1), :], near[3] + near[4] + near[5]]
        for f in far if p < long_count else ():
            part = [f[6 * p + k : 6 * p + k + 1] for k in range(6)]
            tops.append(part[0] + part[1] + part[2])
            totals.append(part[3] + part[4] + part[5])
        best = functools.reduce(jnp.maximum, tops)
        scales = [jnp.exp(t - best) for t in tops]
        denom = sum(s * t for s, t in zip(scales, totals))
        begins.append(len(factors))
        factors += [s / denom for s in scales]
    factors.append(jnp.zeros((128 - len(factors), width), F32))
    columns = jnp.transpose(jnp.concatenate(factors, axis=0))
    for p in range(requests):
        rows = pl.ds(pl.multiple_of(order_ref[p] * draft, draft), draft)
        parts = [own_ref[rows, :], near_ref[rows, :].astype(F32)]
        parts += [ref[pl.ds(p * draft, draft), :].astype(F32) for ref in (msgs if p < long_count else ())]
        out = None
        for j, part in enumerate(parts):
            c = begins[p] + j
            term = part * head_lanes(columns[:, c : c + 1], heads, draft, width)
            out = term if out is None else out + term
        out_ref[pl.ds(p * draft, draft)] = out.astype(BF16)


def norm(values, sums, squares, gain, width_all):
    center = sums / width_all
    spread = squares / width_all - center * center
    return (values - center) * lax.rsqrt(spread + EPS) * gain


def forward_kernel(dims, len_ref, *refs):
    requests, draft, page_len, first, count = dims
    att, hid = refs[0:4], refs[4:8]
    wout, (gain_ref, up_ref, down_ref) = refs[8:12], refs[12:15]
    parts, normed_ref = refs[15:19], refs[19]
    order_ref, z_ref = refs[20:]
    me = lax.axis_index("tp")
    share = hid[0].shape[1]
    width_all = z_ref.shape[1]
    write_order(len_ref, order_ref, requests, page_len)
    for p in range(count):
        rows = pl.ds(pl.multiple_of(order_ref[first + p] * draft, draft), draft)
        for flip in range(4):
            at = pl.ds(pl.multiple_of((me ^ flip) * share, share), share)
            z_ref[pl.ds(p * draft, draft), at] = hid[flip][rows, :].astype(F32)
    branch = None
    for flip in range(4):
        term = jnp.dot(att[flip][pl.ds(first * draft, count * draft)], wout[flip][...], preferred_element_type=F32)
        branch = term if branch is None else branch + term
    z = z_ref[...] + branch
    sums = jnp.sum(z, axis=-1, keepdims=True)
    squares = jnp.sum(z * z, axis=-1, keepdims=True)
    normed_wide = norm(z, sums, squares, gain_ref[...], width_all)
    normed = normed_wide.astype(BF16)
    z_ref[...] = normed_wide
    normed_ref[...] = z_ref[:, pl.ds(pl.multiple_of(me * share, share), share)].astype(BF16)
    inner = jnp.dot(normed, up_ref[...], preferred_element_type=F32)
    inner = (0.5 * inner * (1.0 + lax.erf(inner * (0.5 ** 0.5)))).astype(BF16)
    for flip in range(4):
        at = pl.ds(pl.multiple_of((me ^ flip) * share, share), share)
        parts[flip][...] = jnp.dot(inner, down_ref[:, at], preferred_element_type=F32).astype(BF16)


def gather_sum_kernel(*refs):
    groups = (len(refs) - 1) // 6
    stats_ref = refs[-1]
    place = 0
    for g in range(groups):
        a_ref, b_ref, c_ref, d_ref, normed_ref = refs[5 * g : 5 * g + 5]
        x = normed_ref[...].astype(F32) + (
            (a_ref[...].astype(F32) + b_ref[...].astype(F32)) + (c_ref[...].astype(F32) + d_ref[...].astype(F32))
        )
        refs[5 * groups + g][...] = x
        rows = x.shape[0]
        row = lax.broadcasted_iota(jnp.int32, (stats_ref.shape[0], rows), 0)
        sums = to_row(jnp.sum(x, axis=-1, keepdims=True))
        squares = to_row(jnp.sum(x * x, axis=-1, keepdims=True))
        stats_ref[:, pl.ds(place, rows)] = jnp.where(row == 0, sums, jnp.where(row == 1, squares, 0.0))
        place += rows


def finish_kernel(dims, len_ref, gain_ref, *refs):
    requests, draft, page_len = dims
    order_ref = refs[-1]
    out_ref = refs[-2]
    stats_refs = refs[-6:-2]
    me = lax.axis_index("tp")
    write_order(len_ref, order_ref, requests, page_len)
    share = out_ref.shape[1]
    gain = gain_ref[:, pl.ds(pl.multiple_of(me * share, share), share)]
    width_all = gain_ref.shape[1]
    stats = sum(ref[...] for ref in stats_refs)
    stats = jnp.transpose(jnp.concatenate([stats] * (128 // stats.shape[0]), axis=0))
    place = 0
    for x_ref in refs[:-6]:
        count = x_ref.shape[0] // draft
        own = stats[place * draft : (place + count) * draft]
        y = norm(x_ref[...], own[:, 0:1], own[:, 1:2], gain, width_all).astype(BF16)
        for p in range(count):
            rows = pl.ds(pl.multiple_of(order_ref[place] * draft, draft), draft)
            out_ref[rows, :] = y[p * draft : (p + 1) * draft]
            place += 1


def shards(hidden_in, w_qkv, w_out, first_gain, w_up, w_down, second_gain, cache_pool,
           page_table, cache_len, tree_parent, accept_node):
    tokens, share = hidden_in.shape
    cache_pool = pltpu.with_memory_space_constraint(cache_pool, pltpu.HBM)
    requests, draft = tree_parent.shape
    width = w_qkv.shape[2]
    heads = width // HD
    pages = page_table.shape[0]
    page_len = cache_pool.shape[1]
    width_all = w_qkv.shape[0]
    long_count = (requests + 3) // 4
    long_rows = long_count * draft
    msg_rows = long_rows + META
    side = 4 * draft
    dma = pltpu.SemaphoreType.DMA
    order = pltpu.SMEM((requests,), jnp.int32)

    w_planes = jnp.transpose(w_qkv, (1, 0, 2))
    gain_1 = first_gain.reshape(1, -1)
    gain_2 = second_gain.reshape(1, -1)
    parents = tree_parent.reshape(requests * draft // side, side)

    hid_y = send_tp(hidden_in, 2)
    hid_core = send_tp(hidden_in, 1)
    bias, select = call(
        functools.partial(tree_kernel, (requests, draft)),
        [shape_of((tokens, draft), F32), shape_of((requests * draft // side, 2 * side, 2 * side), BF16)],
        [SMEM, VMEM], [VMEM] * 2, [pltpu.VMEM((side, side), F32)],
        (accept_node, parents), "tree", flops=14 * 256 ** 3 * 2,
    )
    split = shape_of((2, requests, page_len, width), BF16)
    page_keys, page_values = call(
        pages_kernel, [split, split], [SMEM, ANY], [VMEM] * 2,
        [pltpu.VMEM((2, requests) + cache_pool.shape[1:], BF16), dma((2, requests))],
        (page_table, cache_pool), "pages", flops=2 * requests * 2 * 256 ** 3,
    )

    hid_y, _, _ = lax.optimization_barrier((hid_y, bias, page_keys))
    hid_diag = send_tp(hid_y, 1)
    hid = (hidden_in, hid_core, hid_y, hid_diag)
    wout_core = send_tp(w_out, 1)
    block = shape_of((tokens, width), BF16)
    queries, message, near_message = call(
        functools.partial(query_kernel, (requests, draft, page_len, long_count)),
        [block, shape_of((msg_rows, width), BF16), shape_of((tokens + META, width), BF16)],
        [SMEM] + [VMEM] * 5, [VMEM] * 3, [order],
        (cache_len, *hid, w_planes), "queries",
        flops=2 * tokens * width_all * width, nbytes=2 * width_all * width, after=(bias, page_keys, wout_core),
    )
    near_asked = send_req(near_message, 1)
    queue = [j for j in (4, 5, 3, 7, 6, 2) if j < pages] + list(range(8, pages))
    early, late = queue, []
    asked = {j: send_req(message, j) for j in early}

    key_new, value_new, accepted = call(
        key_value_kernel,
        [block, block, shape_of((tokens, 2, width), BF16)],
        [VMEM] * 6, [VMEM] * 3, [],
        (*hid, w_planes, select), "keys_values",
        flops=2 * tokens * width_all * width * 2, nbytes=2 * width_all * width * 2, after=(message,),
    )
    own, own_stats, message = call(
        functools.partial(local_kernel, (requests, draft, heads)),
        [shape_of((tokens, width), F32), shape_of((2 * requests, width), F32), shape_of((msg_rows, width), BF16)],
        [SMEM] + [VMEM] * 7, [VMEM] * 3, [],
        (cache_len, queries, key_new, value_new, bias, page_keys, page_values, message), "local_attention",
    )
    asked |= {j: send_req(message, j) for j in late}

    answer = shape_of((msg_rows, width), BF16)
    buffers = lambda n: [pltpu.VMEM((n, long_count) + cache_pool.shape[1:], BF16), dma((n, long_count))]
    near_answer, *outs = call(
        functools.partial(visiting_kernel, (page_len, draft, heads, long_count), tuple(early)),
        [shape_of((tokens + 6 * requests, width), BF16)] + [answer] * len(early),
        [VMEM] * (3 + len(early)) + [SMEM, ANY], [VMEM] * (1 + len(early)), buffers(len(early)),
        (near_asked, page_keys, page_values, *[asked[j] for j in early], page_table, cache_pool), "visitors_early",
        after=(key_new,),
    )
    near_got = send_req(near_answer, -1)
    outs = dict(zip(early, outs))
    back = [j for j in (7, 6, 3, 2, 5, 4) if j < pages] + list(range(8, pages))
    answers = [send_req(outs[j], -j) for j in back]
    last = (near_answer,)

    w_later, _ = lax.optimization_barrier((w_out, near_answer))
    wout_y = send_tp(w_later, 2)

    merged = call(
        functools.partial(merge_kernel, (requests, draft, heads, page_len, long_count)),
        block, [SMEM] + [VMEM] * (3 + len(answers)), VMEM,
        [order, pltpu.VMEM((6 * requests, width), F32)],
        (cache_len, own, own_stats, near_got, *answers), "merge",
    )
    att_y = send_tp(merged, 2)
    att_core = send_tp(merged, 1)
    wout_y, _ = lax.optimization_barrier((wout_y, near_got))
    wout = (w_out, wout_core, wout_y, send_tp(wout_y, 1))
    att = (merged, att_core, att_y, send_tp(att_y, 1))

    def forward(first, count, name, after):
        rows = count * draft
        part = shape_of((rows, share), BF16)
        outs = call(
            functools.partial(forward_kernel, (requests, draft, page_len, first, count)),
            [part] * 5, [SMEM] + [VMEM] * 15, [VMEM] * 5,
            [order, pltpu.VMEM((rows, width_all), F32)],
            (cache_len, *att, *hid, *wout, gain_1, w_up, w_down), name,
            flops=2 * rows * width_all * (width_all + 2 * w_up.shape[1]), nbytes=3 * 2 * 1024 * 1024, after=after,
        )
        got = [send_tp(outs[flip], flip) for flip in (2, 3, 1)]
        return outs, [outs[0], *got, outs[4]]

    outs_short, parts_short = forward(long_count, requests - long_count, "forward_short", ())
    outs_long, parts_long = forward(0, long_count, "forward_long", (outs_short[4],))

    x_long, x_short, stats = call(
        gather_sum_kernel,
        [shape_of((long_rows, share), F32), shape_of((tokens - long_rows, share), F32), shape_of((8, tokens), F32)],
        [VMEM] * 10, [VMEM] * 3, [], (*parts_long, *parts_short), "gather_sum",
    )
    all_stats = (stats,) + tuple(send_tp(stats, flip) for flip in (2, 3, 1))
    layer_out = call(
        functools.partial(finish_kernel, (requests, draft, page_len)),
        shape_of((tokens, share), BF16), [SMEM] + [VMEM] * 7, VMEM, [order],
        (cache_len, gain_2, x_long, x_short, *all_stats), "finish",
    )
    accepted_kv = accepted.reshape(requests, draft, 2, width)
    return (layer_out, accepted_kv)


def solution(mesh):
    placed = (
        P("req", "tp"),
        P(None, None, "tp"),
        P("tp", None),
        P(),
        P(None, "tp"),
        P("tp", None),
        P(),
        P("req", None, None, "tp"),
        P("req", None),
        P("req"),
        P("req", None),
        P("req"),
    )
    return jax.shard_map(
        shards,
        mesh=mesh,
        in_specs=placed,
        out_specs=(P("req", "tp"), P("req", None, None, "tp")),
        check_vma=False,
    )
```

```python
import functools

import jax
import jax.numpy as jnp
from jax import lax
from jax.experimental import pallas as pl
from jax.experimental.pallas import tpu as pltpu
from jax.sharding import PartitionSpec as P

HD = 64
NEG = -1e30
EPS = 1e-05
META = 16
F32 = jnp.float32
BF16 = jnp.bfloat16

VMEM = pl.BlockSpec(memory_space=pltpu.VMEM)
SMEM = pl.BlockSpec(memory_space=pltpu.SMEM)
ANY = pl.BlockSpec(memory_space=pl.ANY)


def shape_of(dims, dtype):
    return jax.ShapeDtypeStruct(dims, dtype)


def call(kernel, outs, ins, out_specs, scratch, operands, name, flops=0, nbytes=0, after=(), vmem=24):
    split = len(operands)

    def body(*refs):
        kernel(*refs[:split], *refs[split + len(after) :])

    return pl.pallas_call(
        body,
        out_shape=outs,
        in_specs=list(ins) + [ANY] * len(after),
        out_specs=out_specs,
        scratch_shapes=scratch,
        compiler_params=pltpu.CompilerParams(vmem_limit_bytes=vmem << 20),
        cost_estimate=pl.CostEstimate(flops=flops, bytes_accessed=nbytes, transcendentals=0),
        name=name,
    )(*operands, *after)


def send_req(value, by):
    size = lax.axis_size("req")
    return lax.ppermute(value, "req", [(i, (i + by) % size) for i in range(size)])


def send_tp(value, flip):
    size = lax.axis_size("tp")
    return lax.ppermute(value, "tp", [(i, i ^ flip) for i in range(size)])


def write_order(len_ref, order_ref, requests, page_len):
    flags = [(len_ref[r] > 2 * page_len).astype(jnp.int32) for r in range(requests)]
    total = sum(flags)
    before = jnp.int32(0)
    for r in range(requests):
        place = jnp.where(flags[r] > 0, before, total + r - before)
        order_ref[place] = jnp.int32(r)
        before = before + flags[r]


def split3(value):
    high = value.astype(BF16)
    rest = value - high.astype(F32)
    middle = rest.astype(BF16)
    low = (rest - middle.astype(F32)).astype(BF16)
    return high, middle, low


def dot_t(a, b):
    return lax.dot_general(a, b, (((1,), (1,)), ((), ())), preferred_element_type=F32)


def head_rows(value, heads):
    lane = lax.broadcasted_iota(jnp.int32, value.shape, 1) // HD
    zero = jnp.zeros_like(value)
    return jnp.concatenate([jnp.where(lane == h, value, zero) for h in range(heads)], axis=0)


def head_lanes(stacked, heads, rows, width):
    lane = lax.broadcasted_iota(jnp.int32, (rows, width), 1) // HD
    out = jnp.zeros((rows, width), stacked.dtype)
    for h in range(heads):
        piece = stacked[h * rows : (h + 1) * rows]
        if piece.shape[1] != width:
            piece = jnp.broadcast_to(piece[:, :1], (rows, width))
        out = jnp.where(lane == h, piece, out)
    return out


def unpick(page_len):
    row = lax.broadcasted_iota(jnp.int32, (2 * page_len, 2 * page_len), 0)
    col = lax.broadcasted_iota(jnp.int32, (2 * page_len, 2 * page_len), 1)
    source = jnp.where(row < page_len, 2 * row, 2 * (row - page_len) + 1)
    return jnp.where(source == col, 1.0, 0.0).astype(BF16)


def split_page(page, picker, page_len):
    flat = page.reshape(2 * page_len, page.shape[2])
    both = jnp.dot(picker, flat, preferred_element_type=F32).astype(BF16)
    return both[:page_len], both[page_len:]


class Rows:
    def __init__(self, rows):
        self.lane = lax.broadcasted_iota(jnp.int32, (rows, 128), 1)
        self.table = jnp.zeros((rows, 128), F32)
        self.count = 0

    def add(self, column):
        self.table = jnp.where(self.lane == self.count, column, self.table)
        self.count += 1

    def rows(self):
        return jnp.transpose(self.table)


def to_row(column):
    return jnp.transpose(jnp.broadcast_to(column, (column.shape[0], 128)))[:1]


def attend(scores, values):
    top = functools.reduce(jnp.maximum, [jnp.max(s, axis=-1, keepdims=True) for s in scores])
    weights = [jnp.exp(s - top).astype(BF16) for s in scores]
    total = sum(jnp.sum(w.astype(F32), axis=-1, keepdims=True) for w in weights)
    mixed = sum(jnp.dot(w, v, preferred_element_type=F32) for w, v in zip(weights, values))
    return mixed, top, total


def pages_kernel(table_ref, pool_ref, key_ref, value_ref, page_ref, sems):
    rows, requests, page_len = key_ref.shape[:3]
    copies = [
        pltpu.make_async_copy(pool_ref.at[table_ref[j, m]], page_ref.at[j, m], sems.at[j, m])
        for j in range(rows)
        for m in range(requests)
    ]
    for copy in copies:
        copy.start()
    picker = unpick(page_len)
    for copy in copies:
        copy.wait()
    for j in range(rows):
        for m in range(requests):
            key_ref[j, m], value_ref[j, m] = split_page(page_ref[j, m], picker, page_len)


def full_product(hid, w_ref, part):
    me = lax.axis_index("tp")
    share = hid[0].shape[1]
    total = None
    for flip, ref in enumerate(hid):
        at = pl.multiple_of((me ^ flip) * share, share)
        term = jnp.dot(ref[...], w_ref[part, pl.ds(at, share), :], preferred_element_type=F32)
        total = term if total is None else total + term
    return total


def tree_kernel(dims, accept_ref, parent_ref, bias_ref, select_ref, wide_ref):
    requests, draft = dims
    group = parent_ref.shape[1] // draft
    side = group * draft
    row = lax.broadcasted_iota(jnp.int32, (side, side), 0)
    col = lax.broadcasted_iota(jnp.int32, (side, side), 1)
    eye = jnp.where(row == col, 1.0, 0.0)
    up = []
    for g in range(requests // group):
        parent = parent_ref[pl.ds(g, 1), :]
        lane = lax.broadcasted_iota(jnp.int32, parent.shape, 1)
        target = jnp.where(parent < 0, -1, parent + (lane // draft) * draft)
        up.append((eye + jnp.where(row == target, 1.0, 0.0)).astype(BF16))
    for sweep in range(max(1, (draft - 1).bit_length())):
        up = [jnp.minimum(jnp.dot(u, u, preferred_element_type=F32), 1.0).astype(BF16) for u in up]
    row = lax.broadcasted_iota(jnp.int32, (2 * side, 2 * side), 0)
    col = lax.broadcasted_iota(jnp.int32, (2 * side, 2 * side), 1)
    fits = (row % 2 == col // side) & (row // (2 * draft) == (col % side) // draft)
    level = ((row // 2) % draft).astype(F32)
    for g in range(requests // group):
        wide = up[g].astype(F32)
        reach = jnp.transpose(wide)
        wide_ref[...] = reach
        depth = jnp.sum(wide, axis=0, keepdims=True) - 1.0
        chosen = jnp.zeros((1, side), F32)
        for i in range(group):
            r = g * group + i
            own = reach[i * draft : (i + 1) * draft, i * draft : (i + 1) * draft]
            bias_ref[pl.ds(r * draft, draft), :] = jnp.where(own > 0.5, 0.0, NEG)
            chosen += wide_ref[pl.ds(i * draft + accept_ref[r], 1), :]
        depth = jnp.concatenate([depth, depth], axis=1)
        chosen = jnp.concatenate([chosen, chosen], axis=1)
        select_ref[g] = jnp.where(fits & (depth == level), chosen, 0.0).astype(BF16)


def query_kernel(dims, len_ref, own_ref, core_ref, y_ref, diag_ref, w_ref, q_ref, out_ref, near_ref, order_ref):
    requests, draft, page_len, long_count = dims
    rows = long_count * draft
    width = q_ref.shape[1]
    write_order(len_ref, order_ref, requests, page_len)
    row = lax.broadcasted_iota(jnp.int32, (META, width), 0)
    facts = jnp.zeros((META, width), jnp.int32)
    for i in range(long_count):
        member = order_ref[i]
        length = len_ref[member]
        facts = jnp.where(row == 3 * i, member, facts)
        facts = jnp.where(row == 3 * i + 1, length // page_len, facts)
        facts = jnp.where(row == 3 * i + 2, length % page_len, facts)
    out_ref[pl.ds(rows, META)] = facts.astype(F32).astype(BF16)
    limits = jnp.zeros((META, width), jnp.int32)
    for r in range(requests):
        limits = jnp.where(row == r, jnp.clip(len_ref[r] - page_len, 0, page_len), limits)
    near_ref[pl.ds(requests * draft, META)] = limits.astype(F32).astype(BF16)
    queries = (full_product((own_ref, core_ref, y_ref, diag_ref), w_ref, 0) * 0.125).astype(BF16)
    q_ref[...] = queries
    near_ref[pl.ds(0, requests * draft)] = queries
    for i in range(long_count):
        at = pl.multiple_of(order_ref[i] * draft, draft)
        out_ref[pl.ds(i * draft, draft)] = q_ref[pl.ds(at, draft), :]


def key_value_kernel(own_ref, core_ref, y_ref, diag_ref, w_ref, select_ref, k_ref, v_ref, acc_ref):
    hid = (own_ref, core_ref, y_ref, diag_ref)
    k_ref[...] = full_product(hid, w_ref, 1).astype(BF16)
    v_ref[...] = full_product(hid, w_ref, 2).astype(BF16)
    groups, side = select_ref.shape[0], select_ref.shape[1] // 2
    for g in range(groups):
        rows = pl.ds(g * side, side)
        pairs = jnp.concatenate([k_ref[rows], v_ref[rows]], axis=0)
        path = jnp.dot(select_ref[g], pairs, preferred_element_type=F32).astype(BF16)
        acc_ref[rows] = path.reshape(side, 2, path.shape[1])


def remote_kernel(dims, page_indices, *refs, between):
    page_len, draft, heads, long_count = dims
    count = len(page_indices)
    msgs, table_ref, pool_ref = refs[:count], refs[count], refs[count + 1]
    outs = refs[count + 2 : 2 * count + 2]
    page_ref, sems = refs[2 * count + 2 :]
    width = heads * HD
    tokens = long_count * draft
    copies, limits = [], []
    for n, page_index in enumerate(page_indices):
        facts = msgs[n][pl.ds(tokens, META), :].astype(F32)[:, :page_len]
        for i in range(long_count):
            member = jnp.max(facts[3 * i : 3 * i + 1]).astype(jnp.int32)
            copy = pltpu.make_async_copy(
                pool_ref.at[table_ref[page_index, member]], page_ref.at[n, i], sems.at[n, i]
            )
            copy.start()
            copies.append(copy)
            length = facts[3 * i + 1 : 3 * i + 2] * page_len + facts[3 * i + 2 : 3 * i + 3]
            limits.append(length - page_index * page_len)
    picker = unpick(page_len)
    lane = lax.broadcasted_iota(jnp.int32, (heads * draft, page_len), 1).astype(F32)
    table = Rows(heads * draft)
    near_stats = between()
    for copy in copies:
        copy.wait()
    for n in range(count):
        for i in range(long_count):
            stacked = head_rows(msgs[n][pl.ds(i * draft, draft), :], heads)
            keys, values = split_page(page_ref[n, i], picker, page_len)
            scores = jnp.where(lane < limits[n * long_count + i], dot_t(stacked, keys), NEG)
            mixed, top, total = attend([scores], [values])
            outs[n][pl.ds(i * draft, draft)] = head_lanes(mixed, heads, draft, width).astype(BF16)
            table.add(top)
            table.add(total)
    for column in near_stats:
        table.add(column)
    rows = table.rows()
    each = 2 * long_count
    for n in range(count):
        terms = [t.astype(F32) for k in range(each) for t in split3(rows[each * n + k : each * n + k + 1])]
        terms.append(jnp.zeros((META - len(terms), width), F32))
        outs[n][pl.ds(tokens, META)] = jnp.concatenate(terms, axis=0).astype(BF16)
    return rows[each * count :]


def near_pages(dims, msg_ref, key_ref, value_ref, out_ref):
    draft, heads = dims
    requests, page_len, width = key_ref.shape[1:]
    tokens = requests * draft
    limits = msg_ref[pl.ds(tokens, META), :].astype(F32)[:, :page_len]
    lane = lax.broadcasted_iota(jnp.int32, (heads * draft, page_len), 1).astype(F32)
    stats = []
    for r in range(requests):
        stacked = head_rows(msg_ref[pl.ds(r * draft, draft), :], heads)
        scores = jnp.where(lane < limits[r : r + 1], dot_t(stacked, key_ref[1, r]), NEG)
        mixed, top, total = attend([scores], [value_ref[1, r]])
        out_ref[pl.ds(r * draft, draft)] = head_lanes(mixed, heads, draft, width).astype(BF16)
        stats += [top, total]
    return stats


def visiting_kernel(dims, page_indices, msg_ref, key_ref, value_ref, *refs):
    page_len, draft, heads, long_count = dims
    count = len(page_indices)
    near = functools.partial(near_pages, (draft, heads), msg_ref, key_ref, value_ref, refs[count + 2])
    rows = remote_kernel(dims, page_indices, *refs[: count + 2], *refs[count + 3 :], between=near)
    requests = key_ref.shape[1]
    terms = [t.astype(F32) for k in range(2 * requests) for t in split3(rows[k : k + 1])]
    refs[count + 2][pl.ds(requests * draft, len(terms))] = jnp.concatenate(terms, axis=0).astype(BF16)


def local_kernel(dims, len_ref, q_ref, k_ref, v_ref, bias_ref, key_ref, value_ref, keep_ref, out_ref, stats_ref, kept_ref):
    kept_ref[...] = keep_ref[...]
    requests, draft, heads = dims
    page_len, width = key_ref.shape[2:]
    lane = lax.broadcasted_iota(jnp.int32, (heads * draft, page_len), 1)
    table = Rows(heads * draft)
    for r in range(requests):
        rows = pl.ds(r * draft, draft)
        stacked = head_rows(q_ref[rows, :], heads)
        bias = jnp.concatenate([bias_ref[rows, :]] * heads, axis=0)
        mixed, top, total = attend(
            [jnp.where(lane < len_ref[r], dot_t(stacked, key_ref[0, r]), NEG), dot_t(stacked, k_ref[rows, :]) + bias],
            [value_ref[0, r], v_ref[rows, :]],
        )
        out_ref[rows] = head_lanes(mixed, heads, draft, width)
        table.add(top)
        table.add(total)
    stats_ref[...] = table.rows()[: 2 * requests]


def merge_kernel(dims, len_ref, own_ref, stats_ref, near_ref, *refs):
    requests, draft, heads, page_len, long_count = dims
    width = heads * HD
    msgs, out_ref, order_ref, facts_ref = refs[:-3], refs[-3], refs[-2], refs[-1]
    write_order(len_ref, order_ref, requests, page_len)
    tokens = requests * draft
    facts_ref[...] = near_ref[pl.ds(tokens, 6 * requests), :].astype(F32)
    far = [ref[pl.ds(ref.shape[0] - META, META), :].astype(F32) for ref in msgs]
    factors, begins = [], []
    for p in range(requests):
        r = order_ref[p]
        near = [facts_ref[pl.ds(6 * r + k, 1), :] for k in range(6)]
        tops = [stats_ref[pl.ds(2 * r, 1), :], near[0] + near[1] + near[2]]
        totals = [stats_ref[pl.ds(2 * r + 1, 1), :], near[3] + near[4] + near[5]]
        for f in far if p < long_count else ():
            part = [f[6 * p + k : 6 * p + k + 1] for k in range(6)]
            tops.append(part[0] + part[1] + part[2])
            totals.append(part[3] + part[4] + part[5])
        best = functools.reduce(jnp.maximum, tops)
        scales = [jnp.exp(t - best) for t in tops]
        denom = sum(s * t for s, t in zip(scales, totals))
        begins.append(len(factors))
        factors += [s / denom for s in scales]
    factors.append(jnp.zeros((128 - len(factors), width), F32))
    columns = jnp.transpose(jnp.concatenate(factors, axis=0))
    for p in range(requests):
        rows = pl.ds(pl.multiple_of(order_ref[p] * draft, draft), draft)
        parts = [own_ref[rows, :], near_ref[rows, :].astype(F32)]
        parts += [ref[pl.ds(p * draft, draft), :].astype(F32) for ref in (msgs if p < long_count else ())]
        out = None
        for j, part in enumerate(parts):
            c = begins[p] + j
            term = part * head_lanes(columns[:, c : c + 1], heads, draft, width)
            out = term if out is None else out + term
        out_ref[pl.ds(p * draft, draft)] = out.astype(BF16)


def norm(values, sums, squares, gain, width_all):
    center = sums / width_all
    spread = squares / width_all - center * center
    return (values - center) * lax.rsqrt(spread + EPS) * gain


def forward_kernel(dims, len_ref, *refs):
    requests, draft, page_len, first, count = dims
    att, hid = refs[0:4], refs[4:8]
    wout, (gain_ref, up_ref, down_ref) = refs[8:12], refs[12:15]
    parts, normed_ref = refs[15:19], refs[19]
    order_ref, z_ref = refs[20:]
    me = lax.axis_index("tp")
    share = hid[0].shape[1]
    width_all = z_ref.shape[1]
    write_order(len_ref, order_ref, requests, page_len)
    for p in range(count):
        rows = pl.ds(pl.multiple_of(order_ref[first + p] * draft, draft), draft)
        for flip in range(4):
            at = pl.ds(pl.multiple_of((me ^ flip) * share, share), share)
            z_ref[pl.ds(p * draft, draft), at] = hid[flip][rows, :].astype(F32)
    branch = None
    for flip in range(4):
        term = jnp.dot(att[flip][pl.ds(first * draft, count * draft)], wout[flip][...], preferred_element_type=F32)
        branch = term if branch is None else branch + term
    z = z_ref[...] + branch
    sums = jnp.sum(z, axis=-1, keepdims=True)
    squares = jnp.sum(z * z, axis=-1, keepdims=True)
    normed_wide = norm(z, sums, squares, gain_ref[...], width_all)
    normed = normed_wide.astype(BF16)
    z_ref[...] = normed_wide
    normed_ref[...] = z_ref[:, pl.ds(pl.multiple_of(me * share, share), share)].astype(BF16)
    inner = jnp.dot(normed, up_ref[...], preferred_element_type=F32)
    inner = (0.5 * inner * (1.0 + lax.erf(inner * (0.5 ** 0.5)))).astype(BF16)
    for flip in range(4):
        at = pl.ds(pl.multiple_of((me ^ flip) * share, share), share)
        parts[flip][...] = jnp.dot(inner, down_ref[:, at], preferred_element_type=F32).astype(BF16)


def gather_sum_kernel(*refs):
    groups = (len(refs) - 1) // 6
    stats_ref = refs[-1]
    place = 0
    for g in range(groups):
        a_ref, b_ref, c_ref, d_ref, normed_ref = refs[5 * g : 5 * g + 5]
        x = normed_ref[...].astype(F32) + (
            (a_ref[...].astype(F32) + b_ref[...].astype(F32)) + (c_ref[...].astype(F32) + d_ref[...].astype(F32))
        )
        refs[5 * groups + g][...] = x
        rows = x.shape[0]
        row = lax.broadcasted_iota(jnp.int32, (stats_ref.shape[0], rows), 0)
        sums = to_row(jnp.sum(x, axis=-1, keepdims=True))
        squares = to_row(jnp.sum(x * x, axis=-1, keepdims=True))
        stats_ref[:, pl.ds(place, rows)] = jnp.where(row == 0, sums, jnp.where(row == 1, squares, 0.0))
        place += rows


def finish_kernel(dims, len_ref, gain_ref, *refs):
    requests, draft, page_len = dims
    order_ref = refs[-1]
    out_ref = refs[-2]
    stats_refs = refs[-6:-2]
    me = lax.axis_index("tp")
    write_order(len_ref, order_ref, requests, page_len)
    share = out_ref.shape[1]
    gain = gain_ref[:, pl.ds(pl.multiple_of(me * share, share), share)]
    width_all = gain_ref.shape[1]
    stats = sum(ref[...] for ref in stats_refs)
    stats = jnp.transpose(jnp.concatenate([stats] * (128 // stats.shape[0]), axis=0))
    place = 0
    for x_ref in refs[:-6]:
        count = x_ref.shape[0] // draft
        own = stats[place * draft : (place + count) * draft]
        y = norm(x_ref[...], own[:, 0:1], own[:, 1:2], gain, width_all).astype(BF16)
        for p in range(count):
            rows = pl.ds(pl.multiple_of(order_ref[place] * draft, draft), draft)
            out_ref[rows, :] = y[p * draft : (p + 1) * draft]
            place += 1


def shards(hidden_in, w_qkv, w_out, first_gain, w_up, w_down, second_gain, cache_pool,
           page_table, cache_len, tree_parent, accept_node):
    tokens, share = hidden_in.shape
    cache_pool = pltpu.with_memory_space_constraint(cache_pool, pltpu.HBM)
    requests, draft = tree_parent.shape
    width = w_qkv.shape[2]
    heads = width // HD
    pages = page_table.shape[0]
    page_len = cache_pool.shape[1]
    width_all = w_qkv.shape[0]
    long_count = (requests + 3) // 4
    long_rows = long_count * draft
    msg_rows = long_rows + META
    side = 4 * draft
    dma = pltpu.SemaphoreType.DMA
    order = pltpu.SMEM((requests,), jnp.int32)

    w_planes = jnp.transpose(w_qkv, (1, 0, 2))
    gain_1 = first_gain.reshape(1, -1)
    gain_2 = second_gain.reshape(1, -1)
    parents = tree_parent.reshape(requests * draft // side, side)

    hid_y = send_tp(hidden_in, 2)
    hid_core = send_tp(hidden_in, 1)
    bias, select = call(
        functools.partial(tree_kernel, (requests, draft)),
        [shape_of((tokens, draft), F32), shape_of((requests * draft // side, 2 * side, 2 * side), BF16)],
        [SMEM, VMEM], [VMEM] * 2, [pltpu.VMEM((side, side), F32)],
        (accept_node, parents), "tree", flops=14 * 256 ** 3 * 2,
    )
    split = shape_of((2, requests, page_len, width), BF16)
    page_keys, page_values = call(
        pages_kernel, [split, split], [SMEM, ANY], [VMEM] * 2,
        [pltpu.VMEM((2, requests) + cache_pool.shape[1:], BF16), dma((2, requests))],
        (page_table, cache_pool), "pages", flops=2 * requests * 2 * 256 ** 3,
    )

    hid_y, _, _ = lax.optimization_barrier((hid_y, bias, page_keys))
    hid_diag = send_tp(hid_y, 1)
    hid = (hidden_in, hid_core, hid_y, hid_diag)
    wout_core = send_tp(w_out, 1)
    block = shape_of((tokens, width), BF16)
    queries, message, near_message = call(
        functools.partial(query_kernel, (requests, draft, page_len, long_count)),
        [block, shape_of((msg_rows, width), BF16), shape_of((tokens + META, width), BF16)],
        [SMEM] + [VMEM] * 5, [VMEM] * 3, [order],
        (cache_len, *hid, w_planes), "queries",
        flops=2 * tokens * width_all * width, nbytes=2 * width_all * width, after=(bias, page_keys, wout_core),
    )
    near_asked = send_req(near_message, 1)
    queue = [j for j in (4, 5, 3, 7, 6, 2) if j < pages] + list(range(8, pages))
    early, late = queue, []
    asked = {j: send_req(message, j) for j in early}

    key_new, value_new, accepted = call(
        key_value_kernel,
        [block, block, shape_of((tokens, 2, width), BF16)],
        [VMEM] * 6, [VMEM] * 3, [],
        (*hid, w_planes, select), "keys_values",
        flops=2 * tokens * width_all * width * 2, nbytes=2 * width_all * width * 2, after=(message,),
    )
    own, own_stats, message = call(
        functools.partial(local_kernel, (requests, draft, heads)),
        [shape_of((tokens, width), F32), shape_of((2 * requests, width), F32), shape_of((msg_rows, width), BF16)],
        [SMEM] + [VMEM] * 7, [VMEM] * 3, [],
        (cache_len, queries, key_new, value_new, bias, page_keys, page_values, message), "local_attention",
    )
    asked |= {j: send_req(message, j) for j in late}

    answer = shape_of((msg_rows, width), BF16)
    buffers = lambda n: [pltpu.VMEM((n, long_count) + cache_pool.shape[1:], BF16), dma((n, long_count))]
    near_answer, *outs = call(
        functools.partial(visiting_kernel, (page_len, draft, heads, long_count), tuple(early)),
        [shape_of((tokens + 6 * requests, width), BF16)] + [answer] * len(early),
        [VMEM] * (3 + len(early)) + [SMEM, ANY], [VMEM] * (1 + len(early)), buffers(len(early)),
        (near_asked, page_keys, page_values, *[asked[j] for j in early], page_table, cache_pool), "visitors_early",
        after=(key_new,),
    )
    near_got = send_req(near_answer, -1)
    outs = dict(zip(early, outs))
    back = [j for j in (7, 6, 3, 2, 5, 4) if j < pages] + list(range(8, pages))
    answers = [send_req(outs[j], -j) for j in back]
    last = (near_answer,)

    w_later, _ = lax.optimization_barrier((w_out, near_answer))
    wout_y = send_tp(w_later, 2)

    merged = call(
        functools.partial(merge_kernel, (requests, draft, heads, page_len, long_count)),
        block, [SMEM] + [VMEM] * (3 + len(answers)), VMEM,
        [order, pltpu.VMEM((6 * requests, width), F32)],
        (cache_len, own, own_stats, near_got, *answers), "merge",
    )
    att_y = send_tp(merged, 2)
    att_core = send_tp(merged, 1)
    wout_y, _ = lax.optimization_barrier((wout_y, near_got))
    wout = (w_out, wout_core, wout_y, send_tp(wout_y, 1))
    att = (merged, att_core, att_y, send_tp(att_y, 1))

    def forward(first, count, name, after):
        rows = count * draft
        part = shape_of((rows, share), BF16)
        outs = call(
            functools.partial(forward_kernel, (requests, draft, page_len, first, count)),
            [part] * 5, [SMEM] + [VMEM] * 15, [VMEM] * 5,
            [order, pltpu.VMEM((rows, width_all), F32)],
            (cache_len, *att, *hid, *wout, gain_1, w_up, w_down), name,
            flops=2 * rows * width_all * (width_all + 2 * w_up.shape[1]), nbytes=3 * 2 * 1024 * 1024, after=after,
        )
        got = [send_tp(outs[flip], flip) for flip in (2, 3, 1)]
        return outs, [outs[0], *got, outs[4]]

    outs_short, parts_short = forward(long_count, requests - long_count, "forward_short", ())
    outs_long, parts_long = forward(0, long_count, "forward_long", (parts_short[3],))

    x_long, x_short, stats = call(
        gather_sum_kernel,
        [shape_of((long_rows, share), F32), shape_of((tokens - long_rows, share), F32), shape_of((8, tokens), F32)],
        [VMEM] * 10, [VMEM] * 3, [], (*parts_long, *parts_short), "gather_sum",
    )
    all_stats = (stats,) + tuple(send_tp(stats, flip) for flip in (2, 3, 1))
    layer_out = call(
        functools.partial(finish_kernel, (requests, draft, page_len)),
        shape_of((tokens, share), BF16), [SMEM] + [VMEM] * 7, VMEM, [order],
        (cache_len, gain_2, x_long, x_short, *all_stats), "finish",
    )
    accepted_kv = accepted.reshape(requests, draft, 2, width)
    return (layer_out, accepted_kv)


def solution(mesh):
    placed = (
        P("req", "tp"),
        P(None, None, "tp"),
        P("tp", None),
        P(),
        P(None, "tp"),
        P("tp", None),
        P(),
        P("req", None, None, "tp"),
        P("req", None),
        P("req"),
        P("req", None),
        P("req"),
    )
    return jax.shard_map(
        shards,
        mesh=mesh,
        in_specs=placed,
        out_specs=(P("req", "tp"), P("req", None, None, "tp")),
        check_vma=False,
    )
```

```python
import functools

import jax
import jax.numpy as jnp
from jax import lax
from jax.experimental import pallas as pl
from jax.experimental.pallas import tpu as pltpu
from jax.sharding import PartitionSpec as P

HD = 64
NEG = -1e30
EPS = 1e-05
META = 16
F32 = jnp.float32
BF16 = jnp.bfloat16

VMEM = pl.BlockSpec(memory_space=pltpu.VMEM)
SMEM = pl.BlockSpec(memory_space=pltpu.SMEM)
ANY = pl.BlockSpec(memory_space=pl.ANY)


def shape_of(dims, dtype):
    return jax.ShapeDtypeStruct(dims, dtype)


def call(kernel, outs, ins, out_specs, scratch, operands, name, flops=0, nbytes=0, after=(), vmem=24):
    split = len(operands)

    def body(*refs):
        kernel(*refs[:split], *refs[split + len(after) :])

    return pl.pallas_call(
        body,
        out_shape=outs,
        in_specs=list(ins) + [ANY] * len(after),
        out_specs=out_specs,
        scratch_shapes=scratch,
        compiler_params=pltpu.CompilerParams(vmem_limit_bytes=vmem << 20),
        cost_estimate=pl.CostEstimate(flops=flops, bytes_accessed=nbytes, transcendentals=0),
        name=name,
    )(*operands, *after)


def send_req(value, by):
    size = lax.axis_size("req")
    return lax.ppermute(value, "req", [(i, (i + by) % size) for i in range(size)])


def send_tp(value, flip):
    size = lax.axis_size("tp")
    return lax.ppermute(value, "tp", [(i, i ^ flip) for i in range(size)])


def write_order(len_ref, order_ref, requests, page_len):
    flags = [(len_ref[r] > 2 * page_len).astype(jnp.int32) for r in range(requests)]
    total = sum(flags)
    before = jnp.int32(0)
    for r in range(requests):
        place = jnp.where(flags[r] > 0, before, total + r - before)
        order_ref[place] = jnp.int32(r)
        before = before + flags[r]


def split3(value):
    high = value.astype(BF16)
    rest = value - high.astype(F32)
    middle = rest.astype(BF16)
    low = (rest - middle.astype(F32)).astype(BF16)
    return high, middle, low


def dot_t(a, b):
    return lax.dot_general(a, b, (((1,), (1,)), ((), ())), preferred_element_type=F32)


def head_rows(value, heads):
    lane = lax.broadcasted_iota(jnp.int32, value.shape, 1) // HD
    zero = jnp.zeros_like(value)
    return jnp.concatenate([jnp.where(lane == h, value, zero) for h in range(heads)], axis=0)


def head_lanes(stacked, heads, rows, width):
    lane = lax.broadcasted_iota(jnp.int32, (rows, width), 1) // HD
    out = jnp.zeros((rows, width), stacked.dtype)
    for h in range(heads):
        piece = stacked[h * rows : (h + 1) * rows]
        if piece.shape[1] != width:
            piece = jnp.broadcast_to(piece[:, :1], (rows, width))
        out = jnp.where(lane == h, piece, out)
    return out


def unpick(page_len):
    row = lax.broadcasted_iota(jnp.int32, (2 * page_len, 2 * page_len), 0)
    col = lax.broadcasted_iota(jnp.int32, (2 * page_len, 2 * page_len), 1)
    source = jnp.where(row < page_len, 2 * row, 2 * (row - page_len) + 1)
    return jnp.where(source == col, 1.0, 0.0).astype(BF16)


def split_page(page, picker, page_len):
    flat = page.reshape(2 * page_len, page.shape[2])
    both = jnp.dot(picker, flat, preferred_element_type=F32).astype(BF16)
    return both[:page_len], both[page_len:]


class Rows:
    def __init__(self, rows):
        self.lane = lax.broadcasted_iota(jnp.int32, (rows, 128), 1)
        self.table = jnp.zeros((rows, 128), F32)
        self.count = 0

    def add(self, column):
        self.table = jnp.where(self.lane == self.count, column, self.table)
        self.count += 1

    def rows(self):
        return jnp.transpose(self.table)


def to_row(column):
    return jnp.transpose(jnp.broadcast_to(column, (column.shape[0], 128)))[:1]


def attend(scores, values):
    top = functools.reduce(jnp.maximum, [jnp.max(s, axis=-1, keepdims=True) for s in scores])
    weights = [jnp.exp(s - top).astype(BF16) for s in scores]
    total = sum(jnp.sum(w.astype(F32), axis=-1, keepdims=True) for w in weights)
    mixed = sum(jnp.dot(w, v, preferred_element_type=F32) for w, v in zip(weights, values))
    return mixed, top, total


def pages_kernel(table_ref, pool_ref, key_ref, value_ref, page_ref, sems):
    rows, requests, page_len = key_ref.shape[:3]
    copies = [
        pltpu.make_async_copy(pool_ref.at[table_ref[j, m]], page_ref.at[j, m], sems.at[j, m])
        for j in range(rows)
        for m in range(requests)
    ]
    for copy in copies:
        copy.start()
    picker = unpick(page_len)
    for copy in copies:
        copy.wait()
    for j in range(rows):
        for m in range(requests):
            key_ref[j, m], value_ref[j, m] = split_page(page_ref[j, m], picker, page_len)


def full_product(hid, w_ref, part):
    me = lax.axis_index("tp")
    share = hid[0].shape[1]
    total = None
    for flip, ref in enumerate(hid):
        at = pl.multiple_of((me ^ flip) * share, share)
        term = jnp.dot(ref[...], w_ref[part, pl.ds(at, share), :], preferred_element_type=F32)
        total = term if total is None else total + term
    return total


def tree_kernel(dims, accept_ref, parent_ref, bias_ref, select_ref, wide_ref):
    requests, draft = dims
    group = parent_ref.shape[1] // draft
    side = group * draft
    row = lax.broadcasted_iota(jnp.int32, (side, side), 0)
    col = lax.broadcasted_iota(jnp.int32, (side, side), 1)
    eye = jnp.where(row == col, 1.0, 0.0)
    up = []
    for g in range(requests // group):
        parent = parent_ref[pl.ds(g, 1), :]
        lane = lax.broadcasted_iota(jnp.int32, parent.shape, 1)
        target = jnp.where(parent < 0, -1, parent + (lane // draft) * draft)
        up.append((eye + jnp.where(row == target, 1.0, 0.0)).astype(BF16))
    for sweep in range(max(1, (draft - 1).bit_length())):
        up = [jnp.minimum(jnp.dot(u, u, preferred_element_type=F32), 1.0).astype(BF16) for u in up]
    row = lax.broadcasted_iota(jnp.int32, (2 * side, 2 * side), 0)
    col = lax.broadcasted_iota(jnp.int32, (2 * side, 2 * side), 1)
    fits = (row % 2 == col // side) & (row // (2 * draft) == (col % side) // draft)
    level = ((row // 2) % draft).astype(F32)
    for g in range(requests // group):
        wide = up[g].astype(F32)
        reach = jnp.transpose(wide)
        wide_ref[...] = reach
        depth = jnp.sum(wide, axis=0, keepdims=True) - 1.0
        chosen = jnp.zeros((1, side), F32)
        for i in range(group):
            r = g * group + i
            own = reach[i * draft : (i + 1) * draft, i * draft : (i + 1) * draft]
            bias_ref[pl.ds(r * draft, draft), :] = jnp.where(own > 0.5, 0.0, NEG)
            chosen += wide_ref[pl.ds(i * draft + accept_ref[r], 1), :]
        depth = jnp.concatenate([depth, depth], axis=1)
        chosen = jnp.concatenate([chosen, chosen], axis=1)
        select_ref[g] = jnp.where(fits & (depth == level), chosen, 0.0).astype(BF16)


def query_kernel(dims, len_ref, own_ref, core_ref, y_ref, diag_ref, w_ref, q_ref, out_ref, near_ref, order_ref):
    requests, draft, page_len, long_count = dims
    rows = long_count * draft
    width = q_ref.shape[1]
    write_order(len_ref, order_ref, requests, page_len)
    row = lax.broadcasted_iota(jnp.int32, (META, width), 0)
    facts = jnp.zeros((META, width), jnp.int32)
    for i in range(long_count):
        member = order_ref[i]
        length = len_ref[member]
        facts = jnp.where(row == 3 * i, member, facts)
        facts = jnp.where(row == 3 * i + 1, length // page_len, facts)
        facts = jnp.where(row == 3 * i + 2, length % page_len, facts)
    out_ref[pl.ds(rows, META)] = facts.astype(F32).astype(BF16)
    limits = jnp.zeros((META, width), jnp.int32)
    for r in range(requests):
        limits = jnp.where(row == r, jnp.clip(len_ref[r] - page_len, 0, page_len), limits)
    near_ref[pl.ds(requests * draft, META)] = limits.astype(F32).astype(BF16)
    queries = (full_product((own_ref, core_ref, y_ref, diag_ref), w_ref, 0) * 0.125).astype(BF16)
    q_ref[...] = queries
    near_ref[pl.ds(0, requests * draft)] = queries
    for i in range(long_count):
        at = pl.multiple_of(order_ref[i] * draft, draft)
        out_ref[pl.ds(i * draft, draft)] = q_ref[pl.ds(at, draft), :]


def key_value_kernel(own_ref, core_ref, y_ref, diag_ref, w_ref, select_ref, k_ref, v_ref, acc_ref):
    hid = (own_ref, core_ref, y_ref, diag_ref)
    k_ref[...] = full_product(hid, w_ref, 1).astype(BF16)
    v_ref[...] = full_product(hid, w_ref, 2).astype(BF16)
    groups, side = select_ref.shape[0], select_ref.shape[1] // 2
    for g in range(groups):
        rows = pl.ds(g * side, side)
        pairs = jnp.concatenate([k_ref[rows], v_ref[rows]], axis=0)
        path = jnp.dot(select_ref[g], pairs, preferred_element_type=F32).astype(BF16)
        acc_ref[rows] = path.reshape(side, 2, path.shape[1])


def remote_kernel(dims, page_indices, *refs, between):
    page_len, draft, heads, long_count = dims
    count = len(page_indices)
    msgs, table_ref, pool_ref = refs[:count], refs[count], refs[count + 1]
    outs = refs[count + 2 : 2 * count + 2]
    page_ref, sems = refs[2 * count + 2 :]
    width = heads * HD
    tokens = long_count * draft
    copies, limits = [], []
    for n, page_index in enumerate(page_indices):
        facts = msgs[n][pl.ds(tokens, META), :].astype(F32)[:, :page_len]
        for i in range(long_count):
            member = jnp.max(facts[3 * i : 3 * i + 1]).astype(jnp.int32)
            copy = pltpu.make_async_copy(
                pool_ref.at[table_ref[page_index, member]], page_ref.at[n, i], sems.at[n, i]
            )
            copy.start()
            copies.append(copy)
            length = facts[3 * i + 1 : 3 * i + 2] * page_len + facts[3 * i + 2 : 3 * i + 3]
            limits.append(length - page_index * page_len)
    picker = unpick(page_len)
    lane = lax.broadcasted_iota(jnp.int32, (heads * draft, page_len), 1).astype(F32)
    table = Rows(heads * draft)
    near_stats = between()
    for copy in copies:
        copy.wait()
    for n in range(count):
        for i in range(long_count):
            stacked = head_rows(msgs[n][pl.ds(i * draft, draft), :], heads)
            keys, values = split_page(page_ref[n, i], picker, page_len)
            scores = jnp.where(lane < limits[n * long_count + i], dot_t(stacked, keys), NEG)
            mixed, top, total = attend([scores], [values])
            outs[n][pl.ds(i * draft, draft)] = head_lanes(mixed, heads, draft, width).astype(BF16)
            table.add(top)
            table.add(total)
    for column in near_stats:
        table.add(column)
    rows = table.rows()
    each = 2 * long_count
    for n in range(count):
        terms = [t.astype(F32) for k in range(each) for t in split3(rows[each * n + k : each * n + k + 1])]
        terms.append(jnp.zeros((META - len(terms), width), F32))
        outs[n][pl.ds(tokens, META)] = jnp.concatenate(terms, axis=0).astype(BF16)
    return rows[each * count :]


def near_pages(dims, msg_ref, key_ref, value_ref, out_ref):
    draft, heads = dims
    requests, page_len, width = key_ref.shape[1:]
    tokens = requests * draft
    limits = msg_ref[pl.ds(tokens, META), :].astype(F32)[:, :page_len]
    lane = lax.broadcasted_iota(jnp.int32, (heads * draft, page_len), 1).astype(F32)
    stats = []
    for r in range(requests):
        stacked = head_rows(msg_ref[pl.ds(r * draft, draft), :], heads)
        scores = jnp.where(lane < limits[r : r + 1], dot_t(stacked, key_ref[1, r]), NEG)
        mixed, top, total = attend([scores], [value_ref[1, r]])
        out_ref[pl.ds(r * draft, draft)] = head_lanes(mixed, heads, draft, width).astype(BF16)
        stats += [top, total]
    return stats


def visiting_kernel(dims, page_indices, msg_ref, key_ref, value_ref, *refs):
    page_len, draft, heads, long_count = dims
    count = len(page_indices)
    near = functools.partial(near_pages, (draft, heads), msg_ref, key_ref, value_ref, refs[count + 2])
    rows = remote_kernel(dims, page_indices, *refs[: count + 2], *refs[count + 3 :], between=near)
    requests = key_ref.shape[1]
    terms = [t.astype(F32) for k in range(2 * requests) for t in split3(rows[k : k + 1])]
    refs[count + 2][pl.ds(requests * draft, len(terms))] = jnp.concatenate(terms, axis=0).astype(BF16)


def local_kernel(dims, len_ref, q_ref, k_ref, v_ref, bias_ref, key_ref, value_ref, keep_ref, out_ref, stats_ref, kept_ref):
    kept_ref[...] = keep_ref[...]
    requests, draft, heads = dims
    page_len, width = key_ref.shape[2:]
    lane = lax.broadcasted_iota(jnp.int32, (heads * draft, page_len), 1)
    table = Rows(heads * draft)
    for r in range(requests):
        rows = pl.ds(r * draft, draft)
        stacked = head_rows(q_ref[rows, :], heads)
        bias = jnp.concatenate([bias_ref[rows, :]] * heads, axis=0)
        mixed, top, total = attend(
            [jnp.where(lane < len_ref[r], dot_t(stacked, key_ref[0, r]), NEG), dot_t(stacked, k_ref[rows, :]) + bias],
            [value_ref[0, r], v_ref[rows, :]],
        )
        out_ref[rows] = head_lanes(mixed, heads, draft, width)
        table.add(top)
        table.add(total)
    stats_ref[...] = table.rows()[: 2 * requests]


def merge_kernel(dims, len_ref, own_ref, stats_ref, near_ref, *refs):
    requests, draft, heads, page_len, long_count = dims
    width = heads * HD
    msgs, out_ref, order_ref, facts_ref = refs[:-3], refs[-3], refs[-2], refs[-1]
    write_order(len_ref, order_ref, requests, page_len)
    tokens = requests * draft
    facts_ref[...] = near_ref[pl.ds(tokens, 6 * requests), :].astype(F32)
    far = [ref[pl.ds(ref.shape[0] - META, META), :].astype(F32) for ref in msgs]
    factors, begins = [], []
    for p in range(requests):
        r = order_ref[p]
        near = [facts_ref[pl.ds(6 * r + k, 1), :] for k in range(6)]
        tops = [stats_ref[pl.ds(2 * r, 1), :], near[0] + near[1] + near[2]]
        totals = [stats_ref[pl.ds(2 * r + 1, 1), :], near[3] + near[4] + near[5]]
        for f in far if p < long_count else ():
            part = [f[6 * p + k : 6 * p + k + 1] for k in range(6)]
            tops.append(part[0] + part[1] + part[2])
            totals.append(part[3] + part[4] + part[5])
        best = functools.reduce(jnp.maximum, tops)
        scales = [jnp.exp(t - best) for t in tops]
        denom = sum(s * t for s, t in zip(scales, totals))
        begins.append(len(factors))
        factors += [s / denom for s in scales]
    factors.append(jnp.zeros((128 - len(factors), width), F32))
    columns = jnp.transpose(jnp.concatenate(factors, axis=0))
    for p in range(requests):
        rows = pl.ds(pl.multiple_of(order_ref[p] * draft, draft), draft)
        parts = [own_ref[rows, :], near_ref[rows, :].astype(F32)]
        parts += [ref[pl.ds(p * draft, draft), :].astype(F32) for ref in (msgs if p < long_count else ())]
        out = None
        for j, part in enumerate(parts):
            c = begins[p] + j
            term = part * head_lanes(columns[:, c : c + 1], heads, draft, width)
            out = term if out is None else out + term
        out_ref[pl.ds(p * draft, draft)] = out.astype(BF16)


def norm(values, sums, squares, gain, width_all):
    center = sums / width_all
    spread = squares / width_all - center * center
    return (values - center) * lax.rsqrt(spread + EPS) * gain


def forward_kernel(dims, len_ref, *refs):
    requests, draft, page_len, first, count = dims
    att, hid = refs[0:4], refs[4:8]
    wout, (gain_ref, up_ref, down_ref) = refs[8:12], refs[12:15]
    parts, normed_ref = refs[15:19], refs[19]
    order_ref, z_ref = refs[20:]
    me = lax.axis_index("tp")
    share = hid[0].shape[1]
    width_all = z_ref.shape[1]
    write_order(len_ref, order_ref, requests, page_len)
    for p in range(count):
        rows = pl.ds(pl.multiple_of(order_ref[first + p] * draft, draft), draft)
        for flip in range(4):
            at = pl.ds(pl.multiple_of((me ^ flip) * share, share), share)
            z_ref[pl.ds(p * draft, draft), at] = hid[flip][rows, :].astype(F32)
    branch = None
    for flip in range(4):
        term = jnp.dot(att[flip][pl.ds(first * draft, count * draft)], wout[flip][...], preferred_element_type=F32)
        branch = term if branch is None else branch + term
    z = z_ref[...] + branch
    sums = jnp.sum(z, axis=-1, keepdims=True)
    squares = jnp.sum(z * z, axis=-1, keepdims=True)
    normed_wide = norm(z, sums, squares, gain_ref[...], width_all)
    normed = normed_wide.astype(BF16)
    z_ref[...] = normed_wide
    normed_ref[...] = z_ref[:, pl.ds(pl.multiple_of(me * share, share), share)].astype(BF16)
    inner = jnp.dot(normed, up_ref[...], preferred_element_type=F32)
    inner = (0.5 * inner * (1.0 + lax.erf(inner * (0.5 ** 0.5)))).astype(BF16)
    for flip in range(4):
        at = pl.ds(pl.multiple_of((me ^ flip) * share, share), share)
        parts[flip][...] = jnp.dot(inner, down_ref[:, at], preferred_element_type=F32).astype(BF16)


def gather_sum_kernel(*refs):
    groups = (len(refs) - 1) // 6
    stats_ref = refs[-1]
    place = 0
    for g in range(groups):
        a_ref, b_ref, c_ref, d_ref, normed_ref = refs[5 * g : 5 * g + 5]
        x = normed_ref[...].astype(F32) + (
            (a_ref[...].astype(F32) + b_ref[...].astype(F32)) + (c_ref[...].astype(F32) + d_ref[...].astype(F32))
        )
        refs[5 * groups + g][...] = x
        rows = x.shape[0]
        row = lax.broadcasted_iota(jnp.int32, (stats_ref.shape[0], rows), 0)
        sums = to_row(jnp.sum(x, axis=-1, keepdims=True))
        squares = to_row(jnp.sum(x * x, axis=-1, keepdims=True))
        stats_ref[:, pl.ds(place, rows)] = jnp.where(row == 0, sums, jnp.where(row == 1, squares, 0.0))
        place += rows


def finish_kernel(dims, len_ref, gain_ref, *refs):
    requests, draft, page_len = dims
    order_ref = refs[-1]
    out_ref = refs[-2]
    stats_refs = refs[-6:-2]
    me = lax.axis_index("tp")
    write_order(len_ref, order_ref, requests, page_len)
    share = out_ref.shape[1]
    gain = gain_ref[:, pl.ds(pl.multiple_of(me * share, share), share)]
    width_all = gain_ref.shape[1]
    stats = sum(ref[...] for ref in stats_refs)
    stats = jnp.transpose(jnp.concatenate([stats] * (128 // stats.shape[0]), axis=0))
    place = 0
    for x_ref in refs[:-6]:
        count = x_ref.shape[0] // draft
        own = stats[place * draft : (place + count) * draft]
        y = norm(x_ref[...], own[:, 0:1], own[:, 1:2], gain, width_all).astype(BF16)
        for p in range(count):
            rows = pl.ds(pl.multiple_of(order_ref[place] * draft, draft), draft)
            out_ref[rows, :] = y[p * draft : (p + 1) * draft]
            place += 1


def shards(hidden_in, w_qkv, w_out, first_gain, w_up, w_down, second_gain, cache_pool,
           page_table, cache_len, tree_parent, accept_node):
    tokens, share = hidden_in.shape
    cache_pool = pltpu.with_memory_space_constraint(cache_pool, pltpu.HBM)
    requests, draft = tree_parent.shape
    width = w_qkv.shape[2]
    heads = width // HD
    pages = page_table.shape[0]
    page_len = cache_pool.shape[1]
    width_all = w_qkv.shape[0]
    long_count = (requests + 3) // 4
    long_rows = long_count * draft
    msg_rows = long_rows + META
    side = 4 * draft
    dma = pltpu.SemaphoreType.DMA
    order = pltpu.SMEM((requests,), jnp.int32)

    w_planes = jnp.transpose(w_qkv, (1, 0, 2))
    gain_1 = first_gain.reshape(1, -1)
    gain_2 = second_gain.reshape(1, -1)
    parents = tree_parent.reshape(requests * draft // side, side)

    hid_y = send_tp(hidden_in, 2)
    hid_core = send_tp(hidden_in, 1)
    bias, select = call(
        functools.partial(tree_kernel, (requests, draft)),
        [shape_of((tokens, draft), F32), shape_of((requests * draft // side, 2 * side, 2 * side), BF16)],
        [SMEM, VMEM], [VMEM] * 2, [pltpu.VMEM((side, side), F32)],
        (accept_node, parents), "tree", flops=14 * 256 ** 3 * 2,
    )
    split = shape_of((2, requests, page_len, width), BF16)
    page_keys, page_values = call(
        pages_kernel, [split, split], [SMEM, ANY], [VMEM] * 2,
        [pltpu.VMEM((2, requests) + cache_pool.shape[1:], BF16), dma((2, requests))],
        (page_table, cache_pool), "pages", flops=2 * requests * 2 * 256 ** 3,
    )

    hid_y, _, _ = lax.optimization_barrier((hid_y, bias, page_keys))
    hid_diag = send_tp(hid_y, 1)
    hid = (hidden_in, hid_core, hid_y, hid_diag)
    wout_core = send_tp(w_out, 1)
    block = shape_of((tokens, width), BF16)
    queries, message, near_message = call(
        functools.partial(query_kernel, (requests, draft, page_len, long_count)),
        [block, shape_of((msg_rows, width), BF16), shape_of((tokens + META, width), BF16)],
        [SMEM] + [VMEM] * 5, [VMEM] * 3, [order],
        (cache_len, *hid, w_planes), "queries",
        flops=2 * tokens * width_all * width, nbytes=2 * width_all * width, after=(bias, page_keys, wout_core),
    )
    near_asked = send_req(near_message, 1)
    queue = [j for j in (4, 5, 3, 7, 6, 2) if j < pages] + list(range(8, pages))
    early, late = queue, []
    asked = {j: send_req(message, j) for j in early}

    key_new, value_new, accepted = call(
        key_value_kernel,
        [block, block, shape_of((tokens, 2, width), BF16)],
        [VMEM] * 6, [VMEM] * 3, [],
        (*hid, w_planes, select), "keys_values",
        flops=2 * tokens * width_all * width * 2, nbytes=2 * width_all * width * 2, after=(message,),
    )
    own, own_stats, message = call(
        functools.partial(local_kernel, (requests, draft, heads)),
        [shape_of((tokens, width), F32), shape_of((2 * requests, width), F32), shape_of((msg_rows, width), BF16)],
        [SMEM] + [VMEM] * 7, [VMEM] * 3, [],
        (cache_len, queries, key_new, value_new, bias, page_keys, page_values, message), "local_attention",
    )
    asked |= {j: send_req(message, j) for j in late}

    answer = shape_of((msg_rows, width), BF16)
    buffers = lambda n: [pltpu.VMEM((n, long_count) + cache_pool.shape[1:], BF16), dma((n, long_count))]
    near_answer, *outs = call(
        functools.partial(visiting_kernel, (page_len, draft, heads, long_count), tuple(early)),
        [shape_of((tokens + 6 * requests, width), BF16)] + [answer] * len(early),
        [VMEM] * (3 + len(early)) + [SMEM, ANY], [VMEM] * (1 + len(early)), buffers(len(early)),
        (near_asked, page_keys, page_values, *[asked[j] for j in early], page_table, cache_pool), "visitors_early",
        after=(key_new,),
    )
    near_got = send_req(near_answer, -1)
    outs = dict(zip(early, outs))
    back = [j for j in (6, 7, 3, 2, 5, 4) if j < pages] + list(range(8, pages))
    answers = [send_req(outs[j], -j) for j in back]
    last = (near_answer,)

    w_later, _ = lax.optimization_barrier((w_out, near_answer))
    wout_y = send_tp(w_later, 2)

    merged = call(
        functools.partial(merge_kernel, (requests, draft, heads, page_len, long_count)),
        block, [SMEM] + [VMEM] * (3 + len(answers)), VMEM,
        [order, pltpu.VMEM((6 * requests, width), F32)],
        (cache_len, own, own_stats, near_got, *answers), "merge",
    )
    att_y = send_tp(merged, 2)
    att_core = send_tp(merged, 1)
    wout_y, _ = lax.optimization_barrier((wout_y, near_got))
    wout = (w_out, wout_core, wout_y, send_tp(wout_y, 1))
    att = (merged, att_core, att_y, send_tp(att_y, 1))

    def forward(first, count, name, after):
        rows = count * draft
        part = shape_of((rows, share), BF16)
        outs = call(
            functools.partial(forward_kernel, (requests, draft, page_len, first, count)),
            [part] * 5, [SMEM] + [VMEM] * 15, [VMEM] * 5,
            [order, pltpu.VMEM((rows, width_all), F32)],
            (cache_len, *att, *hid, *wout, gain_1, w_up, w_down), name,
            flops=2 * rows * width_all * (width_all + 2 * w_up.shape[1]), nbytes=3 * 2 * 1024 * 1024, after=after,
        )
        got = [send_tp(outs[flip], flip) for flip in (2, 3, 1)]
        return outs, [outs[0], *got, outs[4]]

    outs_short, parts_short = forward(long_count, requests - long_count, "forward_short", ())
    outs_long, parts_long = forward(0, long_count, "forward_long", (parts_short[3],))

    x_long, x_short, stats = call(
        gather_sum_kernel,
        [shape_of((long_rows, share), F32), shape_of((tokens - long_rows, share), F32), shape_of((8, tokens), F32)],
        [VMEM] * 10, [VMEM] * 3, [], (*parts_long, *parts_short), "gather_sum",
    )
    all_stats = (stats,) + tuple(send_tp(stats, flip) for flip in (2, 3, 1))
    layer_out = call(
        functools.partial(finish_kernel, (requests, draft, page_len)),
        shape_of((tokens, share), BF16), [SMEM] + [VMEM] * 7, VMEM, [order],
        (cache_len, gain_2, x_long, x_short, *all_stats), "finish",
    )
    accepted_kv = accepted.reshape(requests, draft, 2, width)
    return (layer_out, accepted_kv)


def solution(mesh):
    placed = (
        P("req", "tp"),
        P(None, None, "tp"),
        P("tp", None),
        P(),
        P(None, "tp"),
        P("tp", None),
        P(),
        P("req", None, None, "tp"),
        P("req", None),
        P("req"),
        P("req", None),
        P("req"),
    )
    return jax.shard_map(
        shards,
        mesh=mesh,
        in_specs=placed,
        out_specs=(P("req", "tp"), P("req", None, None, "tp")),
        check_vma=False,
    )
```
